32 devices in a mesh: dp: 4 (over y, x), tensor: 8 (over z, core).
Axes of the slice: x: 2, y: 2, z: 4, core: 2. Of those that a mesh axis runs over, the one named last changes fastest.
Arguments:
- hidden: bfloat16 [512, 8192], P('dp', 'tensor')
- norm_gain: float32 [8192], P('tensor'), may hold values from 0.5 to 1.5
- head: bfloat16 [8192, 36864], P(None, ('dp', 'tensor'))
- targets: int32 [512], P('dp'), may hold values from 0 to 36863
- old_logprob: float32 [512], P('dp'), may hold values from -20 to -1
- lengths: int32 [4], P('dp'), may hold values from 1 to 128, as said below
Outputs:
- new_logprob: float32 [512], P('dp')
- log_ratio: float32 [512], P('dp')
The draws below stay inside these ranges and needn't reach their ends.
Inputs may be any that keep to these rules, and one draw needn't show every extreme that they name: `lengths`: every length is at least 1 and at most 128; some sequence has 128 live tokens and some has 1.
All inputs are finite; a program needn't handle non-finite values.
Results may differ from the reference program's by a relative error of at most 0.00094.
Values may be sent and summed in bfloat16 or wider, within the bound.
No kernel may reach another device: no remote copies, remote signals or barrier semaphores. Data moves between devices by JAX's collectives and lax.ppermute only.
A program may use at most 128 MiB of HBM per device.

```python
import jax
import jax.numpy as jnp
from jax import lax

D = 8192
V_DEV = 1152
LEN = 128
TOKENS = 512
SEQS = 4
VOCAB = 36864
DEVICES = 32


def draw_hidden(key, part):
    first, second = jax.random.split(key, 2)
    ramp = jnp.exp(jnp.log(3.0) * jnp.arange(D, dtype=jnp.float32) / D)
    base = jax.random.normal(first, (TOKENS, D), jnp.float32)
    scales = jnp.exp(jax.random.uniform(second, (TOKENS, 1), jnp.float32, 0.0, jnp.log(10.0)))
    return (base * scales * ramp[None, :]).astype(jnp.bfloat16)


def draw_head(key, part):
    first, second = jax.random.split(key, 2)
    base = jax.random.normal(first, (D, VOCAB), jnp.float32)
    columns = jnp.exp(jax.random.uniform(second, (1, VOCAB), jnp.float32, 0.0, jnp.log(4.0)))
    return (base * columns * (3.0 / jnp.sqrt(jnp.float32(D)))).astype(jnp.bfloat16)


def draw_lengths(key, part):
    first, second = jax.random.split(key, 2)
    values = jax.random.randint(first, (SEQS,), 1, LEN + 1, jnp.int32)
    order = jax.random.permutation(second, SEQS)
    values = values.at[order[0]].set(LEN)
    values = values.at[order[1]].set(1)
    return values


def plant(entries, key, smallest, top_value):
    dims = entries.shape
    spot = [jax.random.randint(jax.random.fold_in(key, axis), (), 0, dims[axis]) for axis in range(len(dims))]
    entries = entries.at[tuple(spot)].set(smallest)
    longest = dims.index(max(dims))
    spot[longest] = (spot[longest] + 1) % dims[longest]
    return entries.at[tuple(spot)].set(top_value)


def shard_levels(own_key, shape, shards, low, top_value):
    def one(dim, parts):
        steps = jax.random.uniform(jax.random.fold_in(jax.random.fold_in(own_key, 6), dim), (parts,), jnp.float32, low / len(shards), top_value / len(shards))
        return jnp.repeat(jnp.exp(steps), shape[dim] // parts).reshape((-1,) + (1,) * (len(shape) - dim - 1))

    factor_of = one(*shards[0])
    for cut in shards[1:]:
        factor_of = factor_of * one(*cut)
    return factor_of


def setup_inputs(seed: int = 0) -> dict:
    key_of = jax.random.split(jax.random.key(seed), 7)
    hidden = draw_hidden(jax.random.fold_in(key_of[6], 71), 0)
    norm_gain = jnp.clip(1.0 + 0.1 * jax.random.normal(key_of[1], (D,), jnp.float32), 0.5, 1.5)
    head = draw_head(jax.random.fold_in(key_of[6], 71), 0)
    targets = plant(jax.random.randint(key_of[3], (TOKENS,), 0, VOCAB), jax.random.fold_in(key_of[3], 1), 0, VOCAB - 1).astype(jnp.int32)
    old_logprob = jnp.clip(-20.0 + 19.0 * jax.random.uniform(key_of[4], (TOKENS,), jnp.float32) ** shard_levels(key_of[4], (TOKENS,), ((0, 4),), -0.2, 0.2), -20.0, -1.0)
    lengths = draw_lengths(jax.random.fold_in(key_of[6], 71), 0)
    return {"hidden": hidden, "norm_gain": norm_gain, "head": head, "targets": targets, "old_logprob": old_logprob, "lengths": lengths}


def reference(hidden, norm_gain, head, targets, old_logprob, lengths):
    values = hidden.astype(jnp.float32)
    mean_sq = lax.optimization_barrier(jnp.mean(values * values, axis=1, keepdims=True))
    normed = (values * lax.rsqrt(mean_sq + 1e-06) * norm_gain[None, :]).astype(jnp.bfloat16)
    count = normed.shape[0]

    def block_step(carry, block):
        top, total, picked = carry
        start = (block * V_DEV).astype(jnp.int32)
        weights = lax.dynamic_slice_in_dim(head, start, V_DEV, 1)
        logits = jnp.dot(normed, weights, preferred_element_type=jnp.float32)
        block_top = lax.optimization_barrier(jnp.max(logits, axis=1))
        new_top = jnp.maximum(top, block_top)
        total = total * jnp.exp(top - new_top) + lax.optimization_barrier(jnp.sum(jnp.exp(logits - new_top[:, None]), axis=1))
        column = start + jnp.arange(V_DEV, dtype=jnp.int32)
        hits = column[None, :] == targets[:, None]
        picked = picked + lax.optimization_barrier(jnp.sum(jnp.where(hits, logits, jnp.float32(0.0)), axis=1))
        return ((new_top, total, picked), None)
    init = (jnp.full((count,), -jnp.inf, jnp.float32), jnp.zeros((count,), jnp.float32), jnp.zeros((count,), jnp.float32))
    (top, total, picked), _ = lax.scan(block_step, init, jnp.arange(DEVICES, dtype=jnp.int32))
    position = jnp.arange(LEN, dtype=jnp.int32)
    live = (position[None, :] < lengths[:, None]).reshape(-1).astype(jnp.float32)
    logprob = picked - top - jnp.log(total)
    return (live * logprob, live * (logprob - old_logprob))
```

```python
import jax
import jax.numpy as jnp
from jax import lax
from jax.sharding import PartitionSpec as P

D = 8192
CORES = 2


def sender(n_dp, n_t):
    cols = 2
    rows = n_dp // cols
    depth = n_t // CORES

    def send(a, dy=0, dx=0, dz=0, dc=0):
        perm = []
        for y in range(rows):
            for x in range(cols):
                for z in range(depth):
                    for c in range(CORES):
                        src = (y * cols + x) * n_t + z * CORES + c
                        dst = ((y + dy) % rows * cols + (x + dx) % cols) * n_t
                        dst += (z + dz) % depth * CORES + (c + dc) % CORES
                        perm.append((src, dst))
        return lax.ppermute(a, ("dp", "tensor"), perm)

    return rows, cols, depth, send


def body(hidden, norm_gain, head, targets, old_logprob, lengths):
    n_dp, n_t = lax.axis_size("dp"), lax.axis_size("tensor")
    rows, cols, depth, send = sender(n_dp, n_t)
    tok, feat = hidden.shape
    half = tok // 2
    tensor = lax.axis_index("tensor")
    z_me, c_me = tensor // CORES, tensor % CORES
    plane = [(dy, dx) for dy in range(rows) for dx in range(cols)]
    others = [(dz, dc) for dz in range(depth) for dc in range(CORES)]

    values = hidden.astype(jnp.float32)
    own_sq = jnp.sum(values * values, axis=1)
    packed = jnp.concatenate([norm_gain, own_sq])
    fine = {o: send(packed, dz=o[0], dc=o[1]) if any(o) else packed for o in others}
    layers = [hidden] + [send(hidden, dz=dz) for dz in range(1, depth)]

    sum_sq = sum(fine[o][feat:] for o in others)
    scaled = lax.rsqrt(sum_sq / D + 1e-06)
    marks = jnp.concatenate([scaled, targets.astype(jnp.float32)])
    coarse = {p: send(marks, dy=p[0], dx=p[1]) if any(p) else marks for p in plane}
    scale_all = jnp.concatenate([coarse[p][:tok] for p in plane])
    target_all = jnp.concatenate([coarse[p][tok:] for p in plane]).astype(jnp.int32)

    vocab_cols = head.shape[1]
    logits = jnp.zeros((tok * n_dp, vocab_cols), jnp.float32)
    for dz, mine in enumerate(layers):
        got = {(0, 0): mine}
        for dx in range(1, cols):
            got[0, dx] = send(mine, dx=dx)
        for dy in range(1, rows):
            got[dy, 0] = send(mine, dy=dy)
        for dy in range(1, rows):
            for dx in range(1, cols):
                first = send(got[0, dx][:half], dy=dy)
                second = send(got[dy, 0][half:], dx=dx)
                got[dy, dx] = jnp.concatenate([first, second])
        block = jnp.concatenate([got[p] for p in plane])
        sibling = send(block, dc=1)
        for dc, part in ((0, block), (1, sibling)):
            gain = fine[dz, dc][:feat]
            normed = (part.astype(jnp.float32) * scale_all[:, None] * gain[None, :]).astype(jnp.bfloat16)
            source = (z_me - dz) % depth * CORES + (c_me - dc) % CORES
            weights = lax.dynamic_slice_in_dim(head, source * feat, feat, 0)
            logits = logits + jnp.dot(normed, weights, preferred_element_type=jnp.float32)

    vocab_start = lax.axis_index(("dp", "tensor")) * vocab_cols
    block_top = jnp.max(logits, axis=1)
    block_total = jnp.sum(jnp.exp(logits - block_top[:, None]), axis=1)
    column = vocab_start + jnp.arange(vocab_cols, dtype=jnp.int32)
    hits = column[None, :] == target_all[:, None]
    block_pick = jnp.sum(jnp.where(hits, logits, jnp.float32(0.0)), axis=1)
    stats = jnp.stack([block_top, block_total, block_pick])

    def merge(parts):
        top = parts[0][0]
        for p in parts[1:]:
            top = jnp.maximum(top, p[0])
        total = sum(p[1] * jnp.exp(p[0] - top) for p in parts)
        return jnp.stack([top, total, sum(p[2] for p in parts)])

    pieces = {p: stats[:, i * tok : (i + 1) * tok] for i, p in enumerate(plane)}
    stats = merge([send(pieces[p], dy=-p[0], dx=-p[1]) if any(p) else pieces[p] for p in plane])
    stats = merge([send(stats, dz=o[0], dc=o[1]) if any(o) else stats for o in others])
    top, total, picked = stats[0], stats[1], stats[2]

    seq_count = lengths.shape[0]
    position = jnp.arange(tok // seq_count, dtype=jnp.int32)
    live = (position[None, :] < lengths[:, None]).reshape(-1).astype(jnp.float32)
    logprob = picked - top - jnp.log(total)
    return (live * logprob, live * (logprob - old_logprob))


def solution(mesh):
    in_specs = (
        P("dp", "tensor"),
        P("tensor"),
        P(None, ("dp", "tensor")),
        P("dp"),
        P("dp"),
        P("dp"),
    )
    out_specs = (P("dp"), P("dp"))
    return jax.shard_map(body, mesh=mesh, in_specs=in_specs, out_specs=out_specs, check_vma=False)
```

```python
import jax
import jax.numpy as jnp
from jax import lax
from jax.sharding import PartitionSpec as P

D = 8192
CORES = 2
X_ONLY, Y_ONLY = (0, 1), (1, 0)


class Grid:
    def __init__(self, n_dp, n_t):
        self.n_t = n_t
        self.cols = 2
        self.rows = n_dp // self.cols
        self.depth = n_t // CORES
        self.square = self.rows == self.cols
        self.first = (X_ONLY, Y_ONLY) if self.square else (X_ONLY, X_ONLY)
        self.second = (Y_ONLY, X_ONLY) if self.square else (Y_ONLY, Y_ONLY)

    def permute(self, a, place):
        perm = []
        for y in range(self.rows):
            for x in range(self.cols):
                for z in range(self.depth):
                    for c in range(CORES):
                        src = (y * self.cols + x) * self.n_t + z * CORES + c
                        v, u, w, d = place(y, x, z, c)
                        dst = (v % self.rows * self.cols + u % self.cols) * self.n_t
                        perm.append((src, dst + w % self.depth * CORES + d % CORES))
        return lax.ppermute(a, ("dp", "tensor"), perm)

    def plane(self, a, ways, step):
        def place(y, x, z, c):
            return y + ways[c][0] * step, x + ways[c][1] * step, z, c

        return self.permute(a, place)

    def along(self, a, step):
        return self.permute(a, lambda y, x, z, c: (y, x, z + step, c))

    def flip(self, a, bit):
        return self.permute(a, lambda y, x, z, c: (y, x, z ^ bit, c))

    def sibling(self, a):
        return self.permute(a, lambda y, x, z, c: (y, x, z, c + 1))

    def spread(self, a):
        line = [a] + [self.plane(a, self.first, k) for k in range(1, self.cols)]
        line = jnp.stack(line)
        whole = [line] + [self.plane(line, self.second, k) for k in range(1, self.rows)]
        return jnp.stack(whole)

    def as_sibling(self, a):
        return jnp.swapaxes(a, 0, 1) if self.square else a


def merge(parts):
    top = parts[0][..., 0, :]
    for p in parts[1:]:
        top = jnp.maximum(top, p[..., 0, :])
    total = sum(p[..., 1, :] * jnp.exp(p[..., 0, :] - top) for p in parts)
    return jnp.stack([top, total, sum(p[..., 2, :] for p in parts)], axis=-2)


def body(hidden, norm_gain, head, targets, old_logprob, lengths):
    n_dp, n_t = lax.axis_size("dp"), lax.axis_size("tensor")
    grid = Grid(n_dp, n_t)
    depth = grid.depth
    tok, feat = hidden.shape
    tensor = lax.axis_index("tensor")
    z_me, c_me = tensor // CORES, tensor % CORES
    order = [0, 1, depth - 1] + list(range(2, depth - 1))

    layers = {dz: grid.along(hidden, dz) if dz else hidden for dz in order}
    spread0 = grid.spread(hidden)

    values = hidden.astype(jnp.float32)
    own_sq = jnp.sum(values * values, axis=1)
    packed = jnp.concatenate([norm_gain, own_sq])
    column = jnp.stack([grid.along(packed, dz) if dz else packed for dz in range(depth)])
    beside = grid.sibling(column)
    gains = (column[:, :feat], beside[:, :feat])
    sum_sq = jnp.sum(column[:, feat:], axis=0) + jnp.sum(beside[:, feat:], axis=0)
    scaled = lax.rsqrt(sum_sq / D + 1e-06)
    marks = grid.spread(jnp.stack([scaled, targets.astype(jnp.float32)]))
    scale_all = marks[:, :, 0].reshape(n_dp * tok)
    target_all = marks[:, :, 1].reshape(n_dp * tok).astype(jnp.int32)

    vocab_cols = head.shape[1]
    logits = jnp.zeros((n_dp * tok, vocab_cols), jnp.float32)
    for dz in order:
        block = grid.spread(layers[dz]) if dz else spread0
        other = grid.as_sibling(grid.sibling(block))
        for dc, part in ((0, block), (1, other)):
            gain = gains[dc][dz]
            part = part.reshape(n_dp * tok, feat)
            normed = (part.astype(jnp.float32) * scale_all[:, None] * gain[None, :]).astype(jnp.bfloat16)
            source = (z_me - dz) % depth * CORES + (c_me - dc) % CORES
            weights = lax.dynamic_slice_in_dim(head, source * feat, feat, 0)
            logits = logits + jnp.dot(normed, weights, preferred_element_type=jnp.float32)

    vocab_start = lax.axis_index(("dp", "tensor")) * vocab_cols
    block_top = jnp.max(logits, axis=1)
    block_total = jnp.sum(jnp.exp(logits - block_top[:, None]), axis=1)
    entry = vocab_start + jnp.arange(vocab_cols, dtype=jnp.int32)
    hits = entry[None, :] == target_all[:, None]
    block_pick = jnp.sum(jnp.where(hits, logits, jnp.float32(0.0)), axis=1)

    stats = jnp.stack([block_top, block_total, block_pick])
    stats = jnp.moveaxis(stats.reshape(3, grid.rows, grid.cols, tok), 0, 2)
    stats = merge([stats[0]] + [grid.plane(stats[k], grid.second, -k) for k in range(1, grid.rows)])
    stats = merge([stats[0]] + [grid.plane(stats[k], grid.first, -k) for k in range(1, grid.cols)])
    bit = 1
    while bit < depth:
        stats = merge([stats, grid.flip(stats, bit)])
        bit *= 2
    stats = merge([stats, grid.sibling(stats)])
    top, total, picked = stats[0], stats[1], stats[2]

    seq_count = lengths.shape[0]
    position = jnp.arange(tok // seq_count, dtype=jnp.int32)
    live = (position[None, :] < lengths[:, None]).reshape(-1).astype(jnp.float32)
    logprob = picked - top - jnp.log(total)
    return (live * logprob, live * (logprob - old_logprob))


def solution(mesh):
    in_specs = (
        P("dp", "tensor"),
        P("tensor"),
        P(None, ("dp", "tensor")),
        P("dp"),
        P("dp"),
        P("dp"),
    )
    out_specs = (P("dp"), P("dp"))
    return jax.shard_map(body, mesh=mesh, in_specs=in_specs, out_specs=out_specs, check_vma=False)
```

```python
import functools

import jax
import jax.numpy as jnp
from jax import lax
from jax.experimental import pallas as pl
from jax.experimental.pallas import tpu as pltpu
from jax.sharding import PartitionSpec as P

D = 8192
CORES = 2
X_ONLY, Y_ONLY = (0, 1), (1, 0)
CHUNK = 512
VMEM_LIMIT = 48 * 1024 * 1024


class Grid:
    def __init__(self, n_dp, n_t):
        self.n_t = n_t
        self.cols = 2
        self.rows = n_dp // self.cols
        self.depth = n_t // CORES
        self.square = self.rows == self.cols
        self.first = (X_ONLY, Y_ONLY) if self.square else (X_ONLY, X_ONLY)
        self.second = (Y_ONLY, X_ONLY) if self.square else (Y_ONLY, Y_ONLY)
        self.spots = [(j, i) for j in range(self.rows) for i in range(self.cols)]

    def permute(self, a, place):
        perm = []
        for y in range(self.rows):
            for x in range(self.cols):
                for z in range(self.depth):
                    for c in range(CORES):
                        src = (y * self.cols + x) * self.n_t + z * CORES + c
                        v, u, w, d = place(y, x, z, c)
                        dst = (v % self.rows * self.cols + u % self.cols) * self.n_t
                        perm.append((src, dst + w % self.depth * CORES + d % CORES))
        return lax.ppermute(a, ("dp", "tensor"), perm)

    def plane(self, a, ways, step):
        def place(y, x, z, c):
            return y + ways[c][0] * step, x + ways[c][1] * step, z, c

        return self.permute(a, place)

    def along(self, a, step):
        return self.permute(a, lambda y, x, z, c: (y, x, z + step, c))

    def flip(self, a, bit):
        return self.permute(a, lambda y, x, z, c: (y, x, z ^ bit, c))

    def sibling(self, a):
        return self.permute(a, lambda y, x, z, c: (y, x, z, c + 1))

    def spread(self, a, late=()):
        got = {(0, 0): a}
        for i in range(1, self.cols):
            got[0, i] = self.plane(a, self.first, i)
        for j in range(1, self.rows):
            got[j, 0] = self.plane(a, self.second, j)
        for j in range(1, self.rows):
            for i in range(1, self.cols):
                got[j, i] = self.plane(after(got[0, i], *late), self.second, j)
        return [got[s] for s in self.spots]

    def sibling_spot(self, k):
        j, i = self.spots[k]
        return self.spots.index((i, j)) if self.square else k


def after(a, *others):
    return lax.optimization_barrier((a, *others))[0] if others else a


def merge(parts):
    top = parts[0][..., 0, :]
    for p in parts[1:]:
        top = jnp.maximum(top, p[..., 0, :])
    total = sum(p[..., 1, :] * jnp.exp(p[..., 0, :] - top) for p in parts)
    return jnp.stack([top, total, sum(p[..., 2, :] for p in parts)], axis=-2)


def diagonal(size):
    row = lax.broadcasted_iota(jnp.int32, (size, size), 0)
    return row == lax.broadcasted_iota(jnp.int32, (size, size), 1)


def to_column(row):
    return jnp.sum(jnp.where(diagonal(row.shape[1]), row, 0.0), axis=1, keepdims=True)


def to_row(column):
    return jnp.sum(jnp.where(diagonal(column.shape[0]), column, 0.0), axis=0, keepdims=True)


def layer_kernel(n, place, first, last, *refs):
    refs = list(refs)
    start_ref = refs.pop(0)
    marks = [refs.pop(0) for _ in range(n)]
    fine = [refs.pop(0) for _ in range(CORES)]
    blocks = [refs.pop(0) for _ in range(CORES * n)]
    head_ref = refs.pop(0)
    acc_ref = None if first else refs.pop(0)
    out_ref, raw, weights, normed, scale, gain, acc, raw_sem, head_sem, acc_sem = refs
    tok, feat = raw.shape[2:]
    chunk = normed.shape[1]
    per = feat // chunk

    def head_copy(k):
        offset = pl.multiple_of(start_ref[k // per] + k % per * chunk, chunk)
        return pltpu.make_async_copy(head_ref.at[pl.ds(offset, chunk)], weights.at[k], head_sem.at[k])

    def block_copy(c, k):
        spot = place[k] if c else k
        return pltpu.make_async_copy(blocks[c * n + k], raw.at[c, spot], raw_sem.at[c * n + k])

    for c in range(CORES):
        for k in range(n):
            block_copy(c, k).start()
        for k in range(c * per, (c + 1) * per):
            head_copy(k).start()
    if first:
        acc[...] = jnp.zeros_like(acc)
    else:
        acc_copy = pltpu.make_async_copy(acc_ref, acc, acc_sem)
        acc_copy.start()
    for k in range(n):
        scale[k] = jnp.broadcast_to(to_column(marks[k][0:1, :]), scale.shape[1:])
    for c in range(CORES):
        gain[c] = fine[c][:, :feat]
    if not first:
        acc_copy.wait()

    for c in range(CORES):
        for k in range(n):
            block_copy(c, k).wait()

        @pl.loop(0, per)
        def _(s):
            k = c * per + s
            columns = pl.ds(pl.multiple_of(s * chunk, chunk), chunk)
            for b in range(n):
                part = raw[c, b, :, columns].astype(jnp.float32) * scale[b][:, :1] * gain[c, :, columns]
                normed[b * tok : (b + 1) * tok, :] = part.astype(jnp.bfloat16)
            head_copy(k).wait()
            acc[...] += jnp.dot(normed[...], weights[k], preferred_element_type=jnp.float32)

    if not last:
        out_copy = pltpu.make_async_copy(acc, out_ref, acc_sem)
        out_copy.start()
        out_copy.wait()
        return
    base = start_ref[CORES]
    for b in range(n):
        logits = acc[b * tok : (b + 1) * tok, :]
        top = jnp.max(logits, axis=1, keepdims=True)
        total = jnp.sum(jnp.exp(logits - top), axis=1, keepdims=True)
        entry = lax.broadcasted_iota(jnp.int32, logits.shape, 1) + base
        target = to_column(marks[b][1:2, :]).astype(jnp.int32)
        pick = jnp.sum(jnp.where(entry == target, logits, 0.0), axis=1, keepdims=True)
        out_ref[b, 0:1, :] = to_row(top)
        out_ref[b, 1:2, :] = to_row(total)
        out_ref[b, 2:3, :] = to_row(pick)


def layer(starts, marks, fine, blocks, place, head, acc, last):
    n = len(marks)
    tok, feat = blocks[0].shape
    vocab = head.shape[1]
    chunk = min(CHUNK, feat)
    steps = CORES * feat // chunk
    vmem = pl.BlockSpec(memory_space=pltpu.VMEM)
    whole = pl.BlockSpec(memory_space=pl.ANY)
    first = acc is None
    if last:
        out_shape = jax.ShapeDtypeStruct((n, 3, tok), jnp.float32)
    else:
        out_shape = jax.ShapeDtypeStruct((n * tok, vocab), jnp.float32)
    operands = [starts, *marks, *fine, *blocks, head] + ([] if first else [acc])
    specs = [pl.BlockSpec(memory_space=pltpu.SMEM)] + [vmem] * (n + CORES)
    specs += [whole] * (len(operands) - len(specs))
    work = 2 * n * tok * CORES * feat * vocab
    return pl.pallas_call(
        functools.partial(layer_kernel, n, place, first, last),
        out_shape=out_shape,
        in_specs=specs,
        out_specs=vmem if last else whole,
        scratch_shapes=[
            pltpu.VMEM((CORES, n, tok, feat), jnp.bfloat16),
            pltpu.VMEM((steps, chunk, vocab), jnp.bfloat16),
            pltpu.VMEM((n * tok, chunk), jnp.bfloat16),
            pltpu.VMEM((n, tok, 128), jnp.float32),
            pltpu.VMEM((CORES, 1, feat), jnp.float32),
            pltpu.VMEM((n * tok, vocab), jnp.float32),
            pltpu.SemaphoreType.DMA((CORES * n,)),
            pltpu.SemaphoreType.DMA((steps,)),
            pltpu.SemaphoreType.DMA,
        ],
        compiler_params=pltpu.CompilerParams(vmem_limit_bytes=VMEM_LIMIT),
        cost_estimate=pl.CostEstimate(
            flops=work, bytes_accessed=2 * CORES * feat * (vocab + n * tok), transcendentals=0
        ),
    )(*operands)


def body(hidden, norm_gain, head, targets, old_logprob, lengths):
    n_dp, n_t = lax.axis_size("dp"), lax.axis_size("tensor")
    grid = Grid(n_dp, n_t)
    depth = grid.depth
    tok, feat = hidden.shape
    tensor = lax.axis_index("tensor")
    z_me, c_me = tensor // CORES, tensor % CORES
    order = [0, 1, depth - 1] + list(range(2, depth - 1))
    place = [grid.sibling_spot(k) for k in range(n_dp)]

    layers = {0: hidden}
    for before, dz in zip(order[:-1], order[1:], strict=True):
        layers[dz] = grid.along(after(hidden, layers[before]) if before else hidden, dz)
    spread = {0: grid.spread(hidden)}

    values = hidden.astype(jnp.float32)
    own_sq = jnp.sum(values * values, axis=1)
    packed = jnp.concatenate([norm_gain[None, :], own_sq[None, :]], axis=1)
    column = [grid.along(packed, dz) if dz else packed for dz in range(depth)]
    beside = [grid.sibling(a) for a in column]
    sum_sq = sum(a[:, feat:] for a in column) + sum(a[:, feat:] for a in beside)
    scaled = lax.rsqrt(sum_sq / D + 1e-06)
    marks = grid.spread(jnp.concatenate([scaled, targets.astype(jnp.float32)[None, :]]))

    vocab_cols = head.shape[1]
    vocab_start = lax.axis_index(("dp", "tensor")) * vocab_cols
    done = []
    for at, dz in enumerate(order):
        final = at == len(order) - 1
        if dz:
            late = done[at - 2 : at - 1] if at >= 2 else []
            spread[dz] = grid.spread(layers[dz], done[-1:] if final else late)
        blocks = spread[dz] + [grid.sibling(a) for a in spread[dz]]
        starts = jnp.stack(
            [((z_me - dz) % depth * CORES + (c_me - dc) % CORES) * feat for dc in range(CORES)]
            + [vocab_start]
        )
        fine = [column[dz], beside[dz]]
        done.append(layer(starts, marks, fine, blocks, place, head, done[-1] if done else None, final))

    stats = done[-1].reshape(grid.rows, grid.cols, 3, tok)
    stats = merge([stats[0]] + [grid.plane(stats[k], grid.second, -k) for k in range(1, grid.rows)])
    stats = merge([stats[0]] + [grid.plane(stats[k], grid.first, -k) for k in range(1, grid.cols)])
    bit = 1
    while bit < depth:
        stats = merge([stats, grid.flip(stats, bit)])
        bit *= 2
    stats = merge([stats, grid.sibling(stats)])
    top, total, picked = stats[0], stats[1], stats[2]

    seq_count = lengths.shape[0]
    position = jnp.arange(tok // seq_count, dtype=jnp.int32)
    live = (position[None, :] < lengths[:, None]).reshape(-1).astype(jnp.float32)
    logprob = picked - top - jnp.log(total)
    return (live * logprob, live * (logprob - old_logprob))


def solution(mesh):
    in_specs = (
        P("dp", "tensor"),
        P("tensor"),
        P(None, ("dp", "tensor")),
        P("dp"),
        P("dp"),
        P("dp"),
    )
    out_specs = (P("dp"), P("dp"))
    return jax.shard_map(body, mesh=mesh, in_specs=in_specs, out_specs=out_specs, check_vma=False)
```

```python
import functools

import jax
import jax.numpy as jnp
from jax import lax
from jax.experimental import pallas as pl
from jax.experimental.pallas import tpu as pltpu
from jax.sharding import PartitionSpec as P

D = 8192
CORES = 2
X_ONLY, Y_ONLY = (0, 1), (1, 0)
VMEM_LIMIT = 16 * 1024 * 1024
LOAD_LIMIT = 36 * 1024 * 1024


class Grid:
    def __init__(self, n_dp, n_t):
        self.n_t = n_t
        self.cols = 2
        self.rows = n_dp // self.cols
        self.depth = n_t // CORES
        self.square = self.rows == self.cols
        self.first = (X_ONLY, Y_ONLY) if self.square else (X_ONLY, X_ONLY)
        self.second = (Y_ONLY, X_ONLY) if self.square else (Y_ONLY, Y_ONLY)
        self.spots = [(j, i) for j in range(self.rows) for i in range(self.cols)]

    def permute(self, a, place):
        perm = []
        for y in range(self.rows):
            for x in range(self.cols):
                for z in range(self.depth):
                    for c in range(CORES):
                        src = (y * self.cols + x) * self.n_t + z * CORES + c
                        v, u, w, d = place(y, x, z, c)
                        dst = (v % self.rows * self.cols + u % self.cols) * self.n_t
                        perm.append((src, dst + w % self.depth * CORES + d % CORES))
        return lax.ppermute(a, ("dp", "tensor"), perm)

    def plane(self, a, ways, step):
        def place(y, x, z, c):
            return y + ways[c][0] * step, x + ways[c][1] * step, z, c

        return self.permute(a, place)

    def along(self, a, step):
        return self.permute(a, lambda y, x, z, c: (y, x, z + step, c))

    def back(self, a, j, i):
        def place(y, x, z, c):
            (fy, fx), (sy, sx) = self.first[c], self.second[c]
            return y - fy * i - sy * j, x - fx * i - sx * j, z, c

        return self.permute(a, place) if i or j else a

    def sibling(self, a):
        return self.permute(a, lambda y, x, z, c: (y, x, z, c + 1))

    def spread(self, a, late=()):
        got = {(0, 0): a}
        for i in range(1, self.cols):
            got[0, i] = self.plane(a, self.first, i)
        for j in range(1, self.rows):
            got[j, 0] = self.plane(a, self.second, j)
        for j in range(1, self.rows):
            for i in range(1, self.cols):
                got[j, i] = self.plane(after(got[0, i], *late), self.second, j)
        return [got[s] for s in self.spots]

    def sibling_spot(self, k):
        j, i = self.spots[k]
        return self.spots.index((i, j)) if self.square else k


def after(a, *others):
    return lax.optimization_barrier((a, *others))[0] if others else a


def merge(parts):
    top = parts[0][..., 0, :]
    for p in parts[1:]:
        top = jnp.maximum(top, p[..., 0, :])
    total = sum(p[..., 1, :] * jnp.exp(p[..., 0, :] - top) for p in parts)
    return jnp.stack([top, total, sum(p[..., 2, :] for p in parts)], axis=-2)


def diagonal(size):
    row = lax.broadcasted_iota(jnp.int32, (size, size), 0)
    return row == lax.broadcasted_iota(jnp.int32, (size, size), 1)


def to_column(row):
    return jnp.sum(jnp.where(diagonal(row.shape[1]), row, 0.0), axis=1, keepdims=True)


def to_row(column):
    return jnp.sum(jnp.where(diagonal(column.shape[0]), column, 0.0), axis=0, keepdims=True)


def group_kernel(n, place, size, first, last, *refs):
    refs = list(refs)
    start_ref = refs.pop(0)
    blocks = [refs.pop(0) for _ in range(CORES * n)]
    head_ref = refs.pop(0)
    acc_ref = None if first else refs.pop(0)
    marks = [refs.pop(0) for _ in range(n)] if last else None
    out_ref, rows, acc = refs if last else (*refs, refs[0])
    tok = rows.shape[1] // n
    feat = blocks[0].shape[1]
    for c in range(CORES):
        columns = pl.ds(pl.multiple_of(start_ref[size + c], feat), feat)
        for j in range(size):
            for k in range(n):
                spot = place[k] if c else k
                part = blocks[c * n + k][j * tok : (j + 1) * tok, :]
                rows[j, spot * tok : (spot + 1) * tok, columns] = part
    total = None if first else acc_ref[...]
    for j in range(size):
        offset = pl.multiple_of(start_ref[j], CORES * feat)
        weights = head_ref[pl.ds(offset, CORES * feat), :]
        product = jnp.dot(rows[j], weights, preferred_element_type=jnp.float32)
        total = product if total is None else total + product
    acc[...] = total
    if not last:
        return
    base = start_ref[size + CORES]
    for b in range(n):
        logits = acc[b * tok : (b + 1) * tok, :]
        top = jnp.max(logits, axis=1, keepdims=True)
        total = jnp.sum(jnp.exp(logits - top), axis=1, keepdims=True)
        entry = lax.broadcasted_iota(jnp.int32, logits.shape, 1) + base
        target = to_column(marks[b][...]).astype(jnp.int32)
        pick = jnp.sum(jnp.where(entry == target, logits, 0.0), axis=1, keepdims=True)
        out_ref[b, 0:1, :] = to_row(top)
        out_ref[b, 1:2, :] = to_row(total)
        out_ref[b, 2:3, :] = to_row(pick)


def group_product(starts, blocks, place, head, acc, marks, last):
    n = len(place)
    feat = blocks[0].shape[1]
    size = starts.shape[0] - 1 - CORES
    tok = blocks[0].shape[0] // size
    vocab = head.shape[1]
    vmem = pl.BlockSpec(memory_space=pltpu.VMEM)
    first = acc is None
    logits = jax.ShapeDtypeStruct((n * tok, vocab), jnp.float32)
    operands = [starts, *blocks, head] + ([] if first else [acc]) + (marks if last else [])
    scratch = [pltpu.VMEM((size, n * tok, CORES * feat), jnp.bfloat16)]
    if last:
        scratch.append(pltpu.VMEM(logits.shape, jnp.float32))
    work = 2 * n * tok * CORES * size * feat * vocab
    return pl.pallas_call(
        functools.partial(group_kernel, n, place, size, first, last),
        out_shape=jax.ShapeDtypeStruct((n, 3, tok), jnp.float32) if last else logits,
        in_specs=[pl.BlockSpec(memory_space=pltpu.SMEM)] + [vmem] * (len(operands) - 1),
        out_specs=vmem,
        scratch_shapes=scratch,
        compiler_params=pltpu.CompilerParams(vmem_limit_bytes=VMEM_LIMIT),
        cost_estimate=pl.CostEstimate(
            flops=work, bytes_accessed=2 * CORES * size * feat * vocab, transcendentals=0
        ),
    )(*operands)


def norm_kernel(size, *refs):
    blocks, sums, gains, out_ref = refs[:size], refs[size : size + 2], refs[size + 2 : -1], refs[-1]
    tok, feat = blocks[0].shape
    scale = to_column(lax.rsqrt((sums[0][...] + sums[1][...]) / D + 1e-06))
    for j in range(size):
        part = blocks[j][...].astype(jnp.float32) * scale * gains[j][:, :feat]
        out_ref[j * tok : (j + 1) * tok, :] = part.astype(jnp.bfloat16)


def normalized(blocks, sums, gains):
    tok, feat = blocks[0].shape
    return pl.pallas_call(
        functools.partial(norm_kernel, len(blocks)),
        out_shape=jax.ShapeDtypeStruct((len(blocks) * tok, feat), jnp.bfloat16),
        in_specs=[pl.BlockSpec(memory_space=pltpu.VMEM)] * (2 * len(blocks) + 2),
        out_specs=pl.BlockSpec(memory_space=pltpu.VMEM),
    )(*blocks, *sums, *gains)


def squares_kernel(hidden_ref, gain_ref, out_ref):
    values = hidden_ref[...].astype(jnp.float32)
    feat = values.shape[1]
    out_ref[:, :feat] = gain_ref[...]
    out_ref[:, feat:] = to_row(jnp.sum(values * values, axis=1, keepdims=True))


def load_kernel(head_ref, out_ref, sem):
    copy = pltpu.make_async_copy(head_ref, out_ref, sem)
    copy.start()
    copy.wait()


def loaded(head):
    return pl.pallas_call(
        load_kernel,
        out_shape=pltpu.VMEM(head.shape, head.dtype),
        in_specs=[pl.BlockSpec(memory_space=pl.ANY)],
        out_specs=pl.BlockSpec(memory_space=pltpu.VMEM),
        scratch_shapes=[pltpu.SemaphoreType.DMA],
        compiler_params=pltpu.CompilerParams(vmem_limit_bytes=LOAD_LIMIT),
    )(head)


def body(hidden, norm_gain, head, targets, old_logprob, lengths):
    n_dp, n_t = lax.axis_size("dp"), lax.axis_size("tensor")
    grid = Grid(n_dp, n_t)
    depth = grid.depth
    tok, feat = hidden.shape
    tensor = lax.axis_index("tensor")
    z_me, c_me = tensor // CORES, tensor % CORES
    groups = [[0]] + [[d, depth - d] for d in range(1, (depth + 1) // 2)] + [[depth // 2]]
    place = [grid.sibling_spot(k) for k in range(n_dp)]

    packed = pl.pallas_call(
        squares_kernel,
        out_shape=jax.ShapeDtypeStruct((1, feat + tok), jnp.float32),
    )(hidden, norm_gain[None, :])
    fine = [grid.along(packed, dz) if dz else packed for dz in range(depth)]
    near = after(head, packed)
    near = loaded(near)
    layers = {0: hidden}
    before = []
    for group in groups[1:]:
        for dz in group:
            layers[dz] = grid.along(after(hidden, *before), dz)
        before = [layers[dz] for dz in group]

    own_sum = sum(a[:, feat:] for a in fine)
    own_sum = after(own_sum, near, layers[1])
    sums = (own_sum, grid.sibling(own_sum))
    marks = grid.spread(targets.astype(jnp.float32)[None, :])

    vocab_cols = head.shape[1]
    vocab_start = lax.axis_index(("dp", "tensor")) * vocab_cols
    acc = None
    normed = None
    for at, group in enumerate(groups):
        final = at == len(groups) - 1
        sources = [layers[dz] for dz in group]
        if normed is not None:
            sources[0] = after(sources[0], normed)
        normed = normalized(sources, sums, [fine[dz] for dz in group])
        spread = grid.spread(normed, [acc] if at == 1 else [])
        blocks = spread + [grid.sibling(a) for a in spread]
        if at == 0:
            blocks[0] = after(blocks[0], *marks)
        starts = [(z_me - dz) % depth * (CORES * feat) for dz in group]
        starts += [(c_me - dc) % CORES * feat for dc in range(CORES)]
        acc = group_product(jnp.stack(starts + [vocab_start]), blocks, place, near, acc, marks, final)

    stats = acc.reshape(grid.rows, grid.cols, 3, tok)
    stats = merge([grid.back(stats[j, i], j, i) for j, i in grid.spots])
    stats = merge([stats] + [grid.along(stats, dz) for dz in range(1, depth)])
    stats = merge([stats, grid.sibling(stats)])
    top, total, picked = stats[0], stats[1], stats[2]

    seq_count = lengths.shape[0]
    position = jnp.arange(tok // seq_count, dtype=jnp.int32)
    live = (position[None, :] < lengths[:, None]).reshape(-1).astype(jnp.float32)
    logprob = picked - top - jnp.log(total)
    return (live * logprob, live * (logprob - old_logprob))


def solution(mesh):
    in_specs = (
        P("dp", "tensor"),
        P("tensor"),
        P(None, ("dp", "tensor")),
        P("dp"),
        P("dp"),
        P("dp"),
    )
    out_specs = (P("dp"), P("dp"))
    return jax.shard_map(body, mesh=mesh, in_specs=in_specs, out_specs=out_specs, check_vma=False)
```

```python
import functools

import jax
import jax.numpy as jnp
from jax import lax
from jax.experimental import pallas as pl
from jax.experimental.pallas import tpu as pltpu
from jax.sharding import PartitionSpec as P

D = 8192
CORES = 2
X_ONLY, Y_ONLY = (0, 1), (1, 0)
VMEM_LIMIT = 16 * 1024 * 1024
LOAD_LIMIT = 36 * 1024 * 1024
SMALL_LIMIT = 6 * 1024 * 1024
EXTRA = 16
BASE = 128


class Grid:
    def __init__(self, n_dp, n_t):
        self.n_t = n_t
        self.cols = 2
        self.rows = n_dp // self.cols
        self.depth = n_t // CORES
        self.square = self.rows == self.cols
        self.first = (X_ONLY, Y_ONLY) if self.square else (X_ONLY, X_ONLY)
        self.second = (Y_ONLY, X_ONLY) if self.square else (Y_ONLY, Y_ONLY)
        self.spots = [(j, i) for j in range(self.rows) for i in range(self.cols)]

    def permute(self, a, place):
        perm = []
        for y in range(self.rows):
            for x in range(self.cols):
                for z in range(self.depth):
                    for c in range(CORES):
                        src = (y * self.cols + x) * self.n_t + z * CORES + c
                        v, u, w, d = place(y, x, z, c)
                        dst = (v % self.rows * self.cols + u % self.cols) * self.n_t
                        perm.append((src, dst + w % self.depth * CORES + d % CORES))
        return lax.ppermute(a, ("dp", "tensor"), perm)

    def plane(self, a, ways, step):
        def place(y, x, z, c):
            return y + ways[c][0] * step, x + ways[c][1] * step, z, c

        return self.permute(a, place)

    def along(self, a, step):
        return self.permute(a, lambda y, x, z, c: (y, x, z + step, c))

    def sibling(self, a):
        return self.permute(a, lambda y, x, z, c: (y, x, z, c + 1))

    def reach(self, a):
        got = {(0, 0): a}
        for i in range(1, self.cols):
            got[0, i] = self.plane(a, self.first, i)
        for j in range(1, self.rows):
            got[j, 0] = self.plane(a, self.second, j)
        return got

    def fill(self, got):
        for j in range(1, self.rows):
            for i in range(1, self.cols):
                got[j, i] = self.plane(got[0, i], self.second, j)
        return [got[s] for s in self.spots]

    def owners(self, y, x, c):
        ways = [(self.first[k], self.second[k]) for k in range(CORES)]
        out = []
        for j, i in self.spots:
            at = [
                (y - f[0] * i - s[0] * j) % self.rows * self.cols + (x - f[1] * i - s[1] * j) % self.cols
                for f, s in ways
            ]
            out.append(jnp.where(c == 0, at[0], at[1]))
        return out

    def sibling_spot(self, k):
        j, i = self.spots[k]
        return self.spots.index((i, j)) if self.square else k


def after(a, *others):
    return lax.optimization_barrier((a, *others))[0] if others else a


def diagonal(size):
    row = lax.broadcasted_iota(jnp.int32, (size, size), 0)
    return row == lax.broadcasted_iota(jnp.int32, (size, size), 1)


def to_column(row):
    return jnp.sum(jnp.where(diagonal(row.shape[1]), row, 0.0), axis=1, keepdims=True)


def to_row(column):
    return jnp.sum(jnp.where(diagonal(column.shape[0]), column, 0.0), axis=0, keepdims=True)


def layer_kernel(n, place, layer, first, last, *refs):
    refs = list(refs)
    start_ref = refs.pop(0)
    blocks = [refs.pop(0) for _ in range(CORES * n)]
    head_ref = refs.pop(0)
    acc_ref = None if first else refs.pop(0)
    marks = [refs.pop(0) for _ in range(n)] if last else None
    out_ref, rows, acc = refs if last else (*refs, refs[0])
    tok = rows.shape[0] // n
    feat = blocks[0].shape[1]
    for c in range(CORES):
        columns = pl.ds(pl.multiple_of(start_ref[1 + c], feat), feat)
        for k in range(n):
            spot = place[k] if c else k
            part = blocks[c * n + k][layer * tok : (layer + 1) * tok, :]
            rows[spot * tok : (spot + 1) * tok, columns] = part
    offset = pl.multiple_of(start_ref[0], CORES * feat)
    weights = head_ref[pl.ds(offset, CORES * feat), :]
    product = jnp.dot(rows[...], weights, preferred_element_type=jnp.float32)
    acc[...] = product if first else acc_ref[...] + product
    if not last:
        return
    base = start_ref[1 + CORES]
    for b in range(n):
        logits = acc[b * tok : (b + 1) * tok, :]
        top = jnp.max(logits, axis=1, keepdims=True)
        total = jnp.sum(jnp.exp(logits - top), axis=1, keepdims=True)
        entry = lax.broadcasted_iota(jnp.int32, logits.shape, 1) + base
        digits = marks[b][tok : tok + EXTRA, :tok].astype(jnp.float32)
        target = (digits[0:1, :] * BASE + digits[1:2, :]) * BASE + digits[2:3, :]
        target = to_column(target).astype(jnp.int32)
        pick = jnp.sum(jnp.where(entry == target, logits, 0.0), axis=1, keepdims=True)
        spot = start_ref[2 + CORES + b]
        out_ref[spot, 0:1, :] = to_row(top)
        out_ref[spot, 1:2, :] = to_row(total)
        out_ref[spot, 2:3, :] = to_row(pick)


def layer_product(tok, starts, blocks, layer, place, head, acc, marks, last):
    n = len(place)
    feat = blocks[0].shape[1]
    vocab = head.shape[1]
    vmem = pl.BlockSpec(memory_space=pltpu.VMEM)
    first = acc is None
    logits = jax.ShapeDtypeStruct((n * tok, vocab), jnp.float32)
    operands = [starts, *blocks, head] + ([] if first else [acc]) + (marks if last else [])
    scratch = [pltpu.VMEM((n * tok, CORES * feat), jnp.bfloat16)]
    if last:
        scratch.append(pltpu.VMEM(logits.shape, jnp.float32))
    work = 2 * n * tok * CORES * feat * vocab
    return pl.pallas_call(
        functools.partial(layer_kernel, n, place, layer, first, last),
        out_shape=jax.ShapeDtypeStruct((n, 3, tok), jnp.float32) if last else logits,
        in_specs=[pl.BlockSpec(memory_space=pltpu.SMEM)] + [vmem] * (len(operands) - 1),
        out_specs=vmem,
        scratch_shapes=scratch,
        compiler_params=pltpu.CompilerParams(vmem_limit_bytes=VMEM_LIMIT),
        cost_estimate=pl.CostEstimate(
            flops=work, bytes_accessed=2 * CORES * feat * vocab, transcendentals=0
        ),
    )(*operands)


def norm_kernel(size, *refs):
    blocks, sums, gains, rest = refs[:size], refs[size : size + 2], refs[size + 2 : 2 * size + 2], refs[2 * size + 2 :]
    out_ref = rest[-1]
    tok, feat = blocks[0].shape
    scale = to_column(lax.rsqrt((sums[0][...] + sums[1][...]) / D + 1e-06))
    for j in range(size):
        part = blocks[j][...].astype(jnp.float32) * scale * gains[j][:, :feat]
        out_ref[j * tok : (j + 1) * tok, :] = part.astype(jnp.bfloat16)
    if len(rest) > 1:
        target = rest[0][...]
        row = lax.broadcasted_iota(jnp.int32, (EXTRA, tok), 0)
        digits = jnp.where(row == 0, target >> 14, jnp.where(row == 1, (target >> 7) & 127, target & 127))
        out_ref[tok:, :] = jnp.zeros((EXTRA, feat), jnp.bfloat16)
        out_ref[tok:, :tok] = digits.astype(jnp.float32).astype(jnp.bfloat16)


def normalized(blocks, sums, gains, target=None):
    tok, feat = blocks[0].shape
    operands = [*blocks, *sums, *gains] + ([] if target is None else [target])
    rows = len(blocks) * tok + (0 if target is None else EXTRA)
    return pl.pallas_call(
        functools.partial(norm_kernel, len(blocks)),
        out_shape=jax.ShapeDtypeStruct((rows, feat), jnp.bfloat16),
        in_specs=[pl.BlockSpec(memory_space=pltpu.VMEM)] * len(operands),
        out_specs=pl.BlockSpec(memory_space=pltpu.VMEM),
        compiler_params=pltpu.CompilerParams(vmem_limit_bytes=SMALL_LIMIT),
    )(*operands)


def squares_kernel(hidden_ref, gain_ref, out_ref):
    values = hidden_ref[...].astype(jnp.float32)
    feat = values.shape[1]
    out_ref[:, :feat] = gain_ref[...]
    out_ref[:, feat:] = to_row(jnp.sum(values * values, axis=1, keepdims=True))


def load_kernel(head_ref, out_ref, sem):
    copy = pltpu.make_async_copy(head_ref, out_ref, sem)
    copy.start()
    copy.wait()


def loaded(head):
    return pl.pallas_call(
        load_kernel,
        out_shape=pltpu.VMEM(head.shape, head.dtype),
        in_specs=[pl.BlockSpec(memory_space=pl.ANY)],
        out_specs=pl.BlockSpec(memory_space=pltpu.VMEM),
        scratch_shapes=[pltpu.SemaphoreType.DMA],
        compiler_params=pltpu.CompilerParams(vmem_limit_bytes=LOAD_LIMIT),
    )(head)


def body(hidden, norm_gain, head, targets, old_logprob, lengths):
    n_dp, n_t = lax.axis_size("dp"), lax.axis_size("tensor")
    grid = Grid(n_dp, n_t)
    depth = grid.depth
    tok, feat = hidden.shape
    tensor = lax.axis_index("tensor")
    z_me, c_me = tensor // CORES, tensor % CORES
    groups = [[0]] + [[d, depth - d] for d in range(1, (depth + 1) // 2)] + [[depth // 2]]
    place = [grid.sibling_spot(k) for k in range(n_dp)]

    packed = pl.pallas_call(
        squares_kernel,
        out_shape=jax.ShapeDtypeStruct((1, feat + tok), jnp.float32),
        compiler_params=pltpu.CompilerParams(vmem_limit_bytes=SMALL_LIMIT),
    )(hidden, norm_gain[None, :])
    fine = [grid.along(packed, dz) if dz else packed for dz in range(depth)]
    layers = {0: hidden}
    before = []
    for group in groups[1:]:
        for dz in group:
            layers[dz] = grid.along(after(hidden, *before), dz)
        before = [layers[dz] for dz in group]

    own_sum = sum(a[:, feat:] for a in fine)
    own_sum = after(own_sum, layers[1])
    sums = (own_sum, grid.sibling(own_sum))

    vocab_cols = head.shape[1]
    vocab_start = lax.axis_index(("dp", "tensor")) * vocab_cols
    plane = lax.axis_index("dp")
    owners = grid.owners(plane // grid.cols, plane % grid.cols, c_me)
    normed, reached = [], []
    for at, group in enumerate(groups):
        sources = [layers[dz] for dz in group]
        if at:
            sources[0] = after(sources[0], *reached[-1].values())
        gains = [fine[dz] for dz in group]
        normed.append(normalized(sources, sums, gains, None if at else targets[None, :]))
        reached.append(grid.reach(normed[-1]))
    near = loaded(after(head, *reached[0].values(), normed[1]))
    acc, marks = None, None
    for at, group in enumerate(groups):
        final = at == len(groups) - 1
        spread = grid.fill(dict(reached[at]))
        if marks is None:
            marks = spread
        blocks = spread + [grid.sibling(a) for a in spread]
        following = [] if final else [*reached[at + 1].values(), *normed[at + 2 : at + 3]]
        for layer, dz in enumerate(group):
            start = (z_me - dz) % depth * (CORES * feat)
            starts = [start] + [(c_me - dc) % CORES * feat for dc in range(CORES)] + [vocab_start] + owners
            if layer == len(group) - 1:
                blocks[0] = after(blocks[0], *following)
            last = final and layer == len(group) - 1
            acc = layer_product(tok, jnp.stack(starts), blocks, layer, place, near, acc, marks, last)

    spread_stats = jnp.broadcast_to(acc[:, None], (n_dp, n_t, 3, tok)).reshape(n_dp * n_t, 3, tok)
    parts = lax.all_to_all(spread_stats, ("dp", "tensor"), 0, 0, tiled=True)
    top = jnp.max(parts[:, 0], axis=0)
    total = jnp.sum(parts[:, 1] * jnp.exp(parts[:, 0] - top[None, :]), axis=0)
    picked = jnp.sum(parts[:, 2], axis=0)

    seq_count = lengths.shape[0]
    position = jnp.arange(tok // seq_count, dtype=jnp.int32)
    live = (position[None, :] < lengths[:, None]).reshape(-1).astype(jnp.float32)
    logprob = picked - top - jnp.log(total)
    return (live * logprob, live * (logprob - old_logprob))


def solution(mesh):
    in_specs = (
        P("dp", "tensor"),
        P("tensor"),
        P(None, ("dp", "tensor")),
        P("dp"),
        P("dp"),
        P("dp"),
    )
    out_specs = (P("dp"), P("dp"))
    return jax.shard_map(body, mesh=mesh, in_specs=in_specs, out_specs=out_specs, check_vma=False)
```

```python
import functools

import jax
import jax.numpy as jnp
from jax import lax
from jax.experimental import pallas as pl
from jax.experimental.pallas import tpu as pltpu
from jax.sharding import PartitionSpec as P

D = 8192
CORES = 2
X_ONLY, Y_ONLY = (0, 1), (1, 0)
VMEM_LIMIT = 16 * 1024 * 1024
LOAD_LIMIT = 36 * 1024 * 1024
SMALL_LIMIT = 6 * 1024 * 1024
EXTRA = 16
BASE = 128


class Grid:
    def __init__(self, n_dp, n_t):
        self.n_t = n_t
        self.cols = 2
        self.rows = n_dp // self.cols
        self.depth = n_t // CORES
        self.square = self.rows == self.cols
        self.first = (X_ONLY, Y_ONLY) if self.square else (X_ONLY, X_ONLY)
        self.second = (Y_ONLY, X_ONLY) if self.square else (Y_ONLY, Y_ONLY)
        self.spots = [(j, i) for j in range(self.rows) for i in range(self.cols)]

    def permute(self, a, place):
        perm = []
        for y in range(self.rows):
            for x in range(self.cols):
                for z in range(self.depth):
                    for c in range(CORES):
                        src = (y * self.cols + x) * self.n_t + z * CORES + c
                        v, u, w, d = place(y, x, z, c)
                        dst = (v % self.rows * self.cols + u % self.cols) * self.n_t
                        perm.append((src, dst + w % self.depth * CORES + d % CORES))
        return lax.ppermute(a, ("dp", "tensor"), perm)

    def plane(self, a, ways, step):
        def place(y, x, z, c):
            return y + ways[c][0] * step, x + ways[c][1] * step, z, c

        return self.permute(a, place)

    def along(self, a, step):
        return self.permute(a, lambda y, x, z, c: (y, x, z + step, c))

    def sibling(self, a):
        return self.permute(a, lambda y, x, z, c: (y, x, z, c + 1))

    def reach(self, a):
        got = {(0, 0): a}
        for i in range(1, self.cols):
            got[0, i] = self.plane(a, self.first, i)
        for j in range(1, self.rows):
            got[j, 0] = self.plane(a, self.second, j)
        return got

    def fill(self, got, *late):
        late = (*late, *got.values())
        for j in range(1, self.rows):
            for i in range(1, self.cols):
                got[j, i] = self.plane(after(got[0, i], *late), self.second, j)
        return [got[s] for s in self.spots]

    def owners(self, y, x, c):
        ways = [(self.first[k], self.second[k]) for k in range(CORES)]
        out = []
        for j, i in self.spots:
            at = [
                (y - f[0] * i - s[0] * j) % self.rows * self.cols + (x - f[1] * i - s[1] * j) % self.cols
                for f, s in ways
            ]
            out.append(jnp.where(c == 0, at[0], at[1]))
        return out

    def sibling_spot(self, k):
        j, i = self.spots[k]
        return self.spots.index((i, j)) if self.square else k


def after(a, *others):
    return lax.optimization_barrier((a, *others))[0] if others else a


def diagonal(size):
    row = lax.broadcasted_iota(jnp.int32, (size, size), 0)
    return row == lax.broadcasted_iota(jnp.int32, (size, size), 1)


def to_column(row):
    return jnp.sum(jnp.where(diagonal(row.shape[1]), row, 0.0), axis=1, keepdims=True)


def to_row(column):
    return jnp.sum(jnp.where(diagonal(column.shape[0]), column, 0.0), axis=0, keepdims=True)


def layer_kernel(n, place, layer, first, last, *refs):
    refs = list(refs)
    start_ref = refs.pop(0)
    blocks = [refs.pop(0) for _ in range(CORES * n)]
    head_ref = refs.pop(0)
    acc_ref = None if first else refs.pop(0)
    marks = [refs.pop(0) for _ in range(n)] if last else None
    out_ref, rows, acc = refs if last else (*refs, refs[0])
    tok = rows.shape[0] // n
    feat = blocks[0].shape[1]
    for c in range(CORES):
        columns = pl.ds(pl.multiple_of(start_ref[1 + c], feat), feat)
        for k in range(n):
            spot = place[k] if c else k
            part = blocks[c * n + k][layer * tok : (layer + 1) * tok, :]
            rows[spot * tok : (spot + 1) * tok, columns] = part
    offset = pl.multiple_of(start_ref[0], CORES * feat)
    weights = head_ref[pl.ds(offset, CORES * feat), :]
    product = jnp.dot(rows[...], weights, preferred_element_type=jnp.float32)
    acc[...] = product if first else acc_ref[...] + product
    if not last:
        return
    base = start_ref[1 + CORES]
    for b in range(n):
        logits = acc[b * tok : (b + 1) * tok, :]
        top = jnp.max(logits, axis=1, keepdims=True)
        total = jnp.sum(jnp.exp(logits - top), axis=1, keepdims=True)
        entry = lax.broadcasted_iota(jnp.int32, logits.shape, 1) + base
        digits = marks[b][tok : tok + EXTRA, :tok].astype(jnp.float32)
        target = (digits[0:1, :] * BASE + digits[1:2, :]) * BASE + digits[2:3, :]
        target = to_column(target).astype(jnp.int32)
        pick = jnp.sum(jnp.where(entry == target, logits, 0.0), axis=1, keepdims=True)
        spot = start_ref[2 + CORES + b]
        for peer in range(out_ref.shape[1]):
            out_ref[spot, peer, 0:1, :] = to_row(top)
            out_ref[spot, peer, 1:2, :] = to_row(total)
            out_ref[spot, peer, 2:3, :] = to_row(pick)


def layer_product(tok, peers, starts, blocks, layer, place, head, acc, marks, last):
    n = len(place)
    feat = blocks[0].shape[1]
    vocab = head.shape[1]
    vmem = pl.BlockSpec(memory_space=pltpu.VMEM)
    first = acc is None
    logits = jax.ShapeDtypeStruct((n * tok, vocab), jnp.float32)
    operands = [starts, *blocks, head] + ([] if first else [acc]) + (marks if last else [])
    scratch = [pltpu.VMEM((n * tok, CORES * feat), jnp.bfloat16)]
    if last:
        scratch.append(pltpu.VMEM(logits.shape, jnp.float32))
    work = 2 * n * tok * CORES * feat * vocab
    return pl.pallas_call(
        functools.partial(layer_kernel, n, place, layer, first, last),
        out_shape=jax.ShapeDtypeStruct((n, peers, 3, tok), jnp.float32) if last else logits,
        in_specs=[pl.BlockSpec(memory_space=pltpu.SMEM)] + [vmem] * (len(operands) - 1),
        out_specs=vmem,
        scratch_shapes=scratch,
        compiler_params=pltpu.CompilerParams(vmem_limit_bytes=VMEM_LIMIT),
        cost_estimate=pl.CostEstimate(
            flops=work, bytes_accessed=2 * CORES * feat * vocab, transcendentals=0
        ),
    )(*operands)


def fetch(pairs, sems):
    copies = [pltpu.make_async_copy(a, b, sems.at[i]) for i, (a, b) in enumerate(pairs)]
    for copy in copies:
        copy.start()
    for copy in copies:
        copy.wait()


def norm_kernel(size, *refs):
    blocks, sums, gains, rest = refs[:size], refs[size : size + 2], refs[size + 2 : 2 * size + 2], refs[2 * size + 2 :]
    out_ref, raw, sems = rest[-3:]
    tok, feat = blocks[0].shape
    fetch([(blocks[j], raw.at[j]) for j in range(size)], sems)
    scale = to_column(lax.rsqrt((sums[0][...] + sums[1][...]) / D + 1e-06))
    for j in range(size):
        part = raw[j].astype(jnp.float32) * scale * gains[j][:, :feat]
        out_ref[j * tok : (j + 1) * tok, :] = part.astype(jnp.bfloat16)
    if len(rest) > 3:
        target = rest[0][...]
        row = lax.broadcasted_iota(jnp.int32, (EXTRA, tok), 0)
        digits = jnp.where(row == 0, target >> 14, jnp.where(row == 1, (target >> 7) & 127, target & 127))
        out_ref[tok:, :] = jnp.zeros((EXTRA, feat), jnp.bfloat16)
        out_ref[tok:, :tok] = digits.astype(jnp.float32).astype(jnp.bfloat16)


def normalized(blocks, sums, gains, target=None):
    tok, feat = blocks[0].shape
    size = len(blocks)
    operands = [*blocks, *sums, *gains] + ([] if target is None else [target])
    rows = size * tok + (0 if target is None else EXTRA)
    vmem = pl.BlockSpec(memory_space=pltpu.VMEM)
    return pl.pallas_call(
        functools.partial(norm_kernel, size),
        out_shape=jax.ShapeDtypeStruct((rows, feat), jnp.bfloat16),
        in_specs=[pl.BlockSpec(memory_space=pl.ANY)] * size + [vmem] * (len(operands) - size),
        out_specs=vmem,
        scratch_shapes=[pltpu.VMEM((size, tok, feat), jnp.bfloat16), pltpu.SemaphoreType.DMA((size,))],
        compiler_params=pltpu.CompilerParams(vmem_limit_bytes=SMALL_LIMIT),
    )(*operands)


def squares_kernel(hidden_ref, gain_ref, out_ref, raw, gain, sems):
    fetch([(hidden_ref, raw), (gain_ref, gain)], sems)
    values = raw[...].astype(jnp.float32)
    feat = values.shape[1]
    out_ref[:, :feat] = gain[...]
    out_ref[:, feat:] = to_row(jnp.sum(values * values, axis=1, keepdims=True))


def squares(hidden, gain):
    tok, feat = hidden.shape
    return pl.pallas_call(
        squares_kernel,
        out_shape=jax.ShapeDtypeStruct((1, feat + tok), jnp.float32),
        in_specs=[pl.BlockSpec(memory_space=pl.ANY)] * 2,
        out_specs=pl.BlockSpec(memory_space=pltpu.VMEM),
        scratch_shapes=[
            pltpu.VMEM((tok, feat), jnp.bfloat16),
            pltpu.VMEM((1, feat), jnp.float32),
            pltpu.SemaphoreType.DMA((2,)),
        ],
        compiler_params=pltpu.CompilerParams(vmem_limit_bytes=SMALL_LIMIT),
    )(hidden, gain)


def load_kernel(head_ref, out_ref, sem):
    copy = pltpu.make_async_copy(head_ref, out_ref, sem)
    copy.start()
    copy.wait()


def loaded(head):
    return pl.pallas_call(
        load_kernel,
        out_shape=pltpu.VMEM(head.shape, head.dtype),
        in_specs=[pl.BlockSpec(memory_space=pl.ANY)],
        out_specs=pl.BlockSpec(memory_space=pltpu.VMEM),
        scratch_shapes=[pltpu.SemaphoreType.DMA],
        compiler_params=pltpu.CompilerParams(vmem_limit_bytes=LOAD_LIMIT),
    )(head)


def body(hidden, norm_gain, head, targets, old_logprob, lengths):
    n_dp, n_t = lax.axis_size("dp"), lax.axis_size("tensor")
    grid = Grid(n_dp, n_t)
    depth = grid.depth
    tok, feat = hidden.shape
    tensor = lax.axis_index("tensor")
    z_me, c_me = tensor // CORES, tensor % CORES
    groups = [[0]] + [[d, depth - d] for d in range(1, (depth + 1) // 2)] + [[depth // 2]]
    place = [grid.sibling_spot(k) for k in range(n_dp)]

    packed = squares(hidden, norm_gain[None, :])
    fine = [grid.along(packed, dz) if dz else packed for dz in range(depth)]
    layers = {0: hidden}
    before = []
    for group in groups[1:]:
        for dz in group:
            layers[dz] = grid.along(after(hidden, *before), dz)
        before = [layers[dz] for dz in group]

    own_sum = sum(a[:, feat:] for a in fine)
    own_sum = after(own_sum, *(layers[dz] for dz in groups[1]))
    sums = (own_sum, grid.sibling(own_sum))

    vocab_cols = head.shape[1]
    vocab_start = lax.axis_index(("dp", "tensor")) * vocab_cols
    plane = lax.axis_index("dp")
    owners = grid.owners(plane // grid.cols, plane % grid.cols, c_me)
    normed, reached = [], []
    for at, group in enumerate(groups):
        sources = [layers[dz] for dz in group]
        if at:
            sources[0] = after(sources[0], *reached[-1].values())
        gains = [fine[dz] for dz in group]
        normed.append(normalized(sources, sums, gains, None if at else targets[None, :]))
        reached.append(grid.reach(normed[-1]))
    near = loaded(after(head, normed[1]))
    acc, marks = None, None
    for at, group in enumerate(groups):
        final = at == len(groups) - 1
        held = [] if final or not at else [layers[dz] for dz in groups[at + 1]]
        spread = grid.fill(dict(reached[at]), *([acc] if at == 1 else []), *held)
        if marks is None:
            marks = spread
        blocks = spread + [grid.sibling(a) for a in spread]
        following = [] if final or not at else [*reached[at + 1].values(), *normed[at + 2 : at + 3]]
        for layer, dz in enumerate(group):
            start = (z_me - dz) % depth * (CORES * feat)
            starts = [start] + [(c_me - dc) % CORES * feat for dc in range(CORES)] + [vocab_start] + owners
            if layer == len(group) - 1:
                blocks[0] = after(blocks[0], *following)
            last = final and layer == len(group) - 1
            acc = layer_product(tok, n_t, jnp.stack(starts), blocks, layer, place, near, acc, marks, last)

    parts = lax.all_to_all(acc.reshape(n_dp * n_t, 3, tok), ("dp", "tensor"), 0, 0, tiled=True)
    top = jnp.max(parts[:, 0], axis=0)
    total = jnp.sum(parts[:, 1] * jnp.exp(parts[:, 0] - top[None, :]), axis=0)
    picked = jnp.sum(parts[:, 2], axis=0)

    seq_count = lengths.shape[0]
    position = jnp.arange(tok // seq_count, dtype=jnp.int32)
    live = (position[None, :] < lengths[:, None]).reshape(-1).astype(jnp.float32)
    logprob = picked - top - jnp.log(total)
    return (live * logprob, live * (logprob - old_logprob))


def solution(mesh):
    in_specs = (
        P("dp", "tensor"),
        P("tensor"),
        P(None, ("dp", "tensor")),
        P("dp"),
        P("dp"),
        P("dp"),
    )
    out_specs = (P("dp"), P("dp"))
    return jax.shard_map(body, mesh=mesh, in_specs=in_specs, out_specs=out_specs, check_vma=False)
```

```python
import jax
import jax.numpy as jnp
from jax import lax
from jax.sharding import PartitionSpec as P

D = 8192
CORES = 2
X_ONLY, Y_ONLY = (0, 1), (1, 0)


class Grid:
    def __init__(self, n_dp, n_t):
        self.n_t = n_t
        self.cols = 2
        self.rows = n_dp // self.cols
        self.depth = n_t // CORES
        self.square = self.rows == self.cols
        self.first = (X_ONLY, Y_ONLY) if self.square else (X_ONLY, X_ONLY)
        self.second = (Y_ONLY, X_ONLY) if self.square else (Y_ONLY, Y_ONLY)
        self.spots = [(j, i) for j in range(self.rows) for i in range(self.cols)]

    def permute(self, a, place):
        perm = []
        for y in range(self.rows):
            for x in range(self.cols):
                for z in range(self.depth):
                    for c in range(CORES):
                        src = (y * self.cols + x) * self.n_t + z * CORES + c
                        v, u, w, d = place(y, x, z, c)
                        dst = (v % self.rows * self.cols + u % self.cols) * self.n_t
                        perm.append((src, dst + w % self.depth * CORES + d % CORES))
        return lax.ppermute(a, ("dp", "tensor"), perm)

    def plane(self, a, ways, step):
        def place(y, x, z, c):
            return y + ways[c][0] * step, x + ways[c][1] * step, z, c

        return self.permute(a, place)

    def along(self, a, step):
        return self.permute(a, lambda y, x, z, c: (y, x, z + step, c))

    def sibling(self, a):
        return self.permute(a, lambda y, x, z, c: (y, x, z, c + 1))

    def reach(self, a):
        got = {(0, 0): a}
        for i in range(1, self.cols):
            got[0, i] = self.plane(a, self.first, i)
        for j in range(1, self.rows):
            got[j, 0] = self.plane(a, self.second, j)
        return got

    def fill(self, got, *late):
        late = (*late, *got.values())
        for j in range(1, self.rows):
            for i in range(1, self.cols):
                got[j, i] = self.plane(after(got[0, i], *late), self.second, j)
        return [got[s] for s in self.spots]

    def owners(self, y, x, c):
        ways = [(self.first[k], self.second[k]) for k in range(CORES)]
        out = []
        for j, i in self.spots:
            at = [
                (y - f[0] * i - s[0] * j) % self.rows * self.cols + (x - f[1] * i - s[1] * j) % self.cols
                for f, s in ways
            ]
            out.append(jnp.where(c == 0, at[0], at[1]))
        return out


def after(a, *others):
    return lax.optimization_barrier((a, *others))[0] if others else a


def exchange(a, axis):
    copies = jnp.broadcast_to(a[None], (lax.axis_size(axis), *a.shape))
    return lax.all_to_all(copies, axis, 0, 0, tiled=True)


def merge(parts):
    top = jnp.max(parts[:, 0], axis=0)
    total = jnp.sum(parts[:, 1] * jnp.exp(parts[:, 0] - top[None]), axis=0)
    return top, total, jnp.sum(parts[:, 2], axis=0)


def body(hidden, norm_gain, head, targets, old_logprob, lengths):
    n_dp, n_t = lax.axis_size("dp"), lax.axis_size("tensor")
    grid = Grid(n_dp, n_t)
    depth = grid.depth
    tok, feat = hidden.shape
    plane, tensor = lax.axis_index("dp"), lax.axis_index("tensor")
    z_me, c_me = tensor // CORES, tensor % CORES
    owners = grid.owners(plane // grid.cols, plane % grid.cols, c_me)
    groups = [[0]] + [[d, depth - d] for d in range(1, (depth + 1) // 2)] + [[depth // 2]]

    layers = {0: hidden}
    before = []
    for group in groups[1:]:
        for dz in group:
            layers[dz] = grid.along(after(hidden, *before), dz)
        before = [layers[dz] for dz in group]
    reached = [grid.reach(hidden)]
    for at, group in enumerate(groups[1:]):
        sources = after(tuple(layers[dz] for dz in group), *reached[at].values())
        joined = jnp.concatenate(sources) if len(sources) > 1 else sources[0]
        reached.append(grid.reach(joined))

    values = hidden.astype(jnp.float32)
    packed = jnp.concatenate([norm_gain, jnp.sum(values * values, axis=1)])
    fine = exchange(packed, "tensor")
    gains = fine[:, :feat]
    scaled = lax.rsqrt(jnp.sum(fine[:, feat:], axis=0) / D + 1e-06)
    marks = exchange(jnp.stack([scaled, targets.astype(jnp.float32)]), "dp")
    scale_all = marks[:, 0].reshape(n_dp * tok)
    target_all = marks[:, 1].reshape(n_dp * tok).astype(jnp.int32)

    vocab_cols = head.shape[1]
    logits = None
    for at, group in enumerate(groups):
        final = at == len(groups) - 1
        held = [] if final or not at else [layers[dz] for dz in groups[at + 1]]
        if at == 1:
            held.append(logits)
        spread = grid.fill(dict(reached[at]), *held)
        size = len(group)
        block = jnp.zeros((size * n_dp * tok, feat), hidden.dtype)
        for owner, part in zip(owners, spread, strict=True):
            for j in range(size):
                piece = part[j * tok : (j + 1) * tok]
                block = lax.dynamic_update_slice_in_dim(block, piece, (j * n_dp + owner) * tok, 0)
        other = grid.sibling(block)
        for j, dz in enumerate(group):
            for dc, part in ((0, block), (1, other)):
                source = (z_me - dz) % depth * CORES + (c_me - dc) % CORES
                gain = lax.dynamic_index_in_dim(gains, source, 0, False)
                raw = part[j * n_dp * tok : (j + 1) * n_dp * tok].astype(jnp.float32)
                normed = (raw * scale_all[:, None] * gain[None, :]).astype(jnp.bfloat16)
                weights = lax.dynamic_slice_in_dim(head, source * feat, feat, 0)
                product = jnp.dot(normed, weights, preferred_element_type=jnp.float32)
                logits = product if logits is None else logits + product

    vocab_start = lax.axis_index(("dp", "tensor")) * vocab_cols
    block_top = jnp.max(logits, axis=1)
    block_total = jnp.sum(jnp.exp(logits - block_top[:, None]), axis=1)
    entry = vocab_start + jnp.arange(vocab_cols, dtype=jnp.int32)
    hits = entry[None, :] == target_all[:, None]
    block_pick = jnp.sum(jnp.where(hits, logits, jnp.float32(0.0)), axis=1)

    stats = jnp.stack([s.reshape(n_dp, tok) for s in (block_top, block_total, block_pick)], axis=1)
    stats = jnp.stack(merge(lax.all_to_all(stats, "dp", 0, 0, tiled=True)))
    top, total, picked = merge(exchange(stats, "tensor"))

    seq_count = lengths.shape[0]
    position = jnp.arange(tok // seq_count, dtype=jnp.int32)
    live = (position[None, :] < lengths[:, None]).reshape(-1).astype(jnp.float32)
    logprob = picked - top - jnp.log(total)
    return (live * logprob, live * (logprob - old_logprob))


def solution(mesh):
    in_specs = (
        P("dp", "tensor"),
        P("tensor"),
        P(None, ("dp", "tensor")),
        P("dp"),
        P("dp"),
        P("dp"),
    )
    out_specs = (P("dp"), P("dp"))
    return jax.shard_map(body, mesh=mesh, in_specs=in_specs, out_specs=out_specs, check_vma=False)
```

```python
import functools

import jax
import jax.numpy as jnp
from jax import lax
from jax.experimental import pallas as pl
from jax.experimental.pallas import tpu as pltpu
from jax.sharding import PartitionSpec as P

D = 8192
CORES = 2
X_ONLY, Y_ONLY = (0, 1), (1, 0)
VMEM_LIMIT = 20 * 1024 * 1024
SMALL_LIMIT = 6 * 1024 * 1024
EXTRA = 16
BASE = 128


class Grid:
    def __init__(self, n_dp, n_t):
        self.n_t = n_t
        self.cols = 2
        self.rows = n_dp // self.cols
        self.depth = n_t // CORES
        self.square = self.rows == self.cols
        self.first = (X_ONLY, Y_ONLY) if self.square else (X_ONLY, X_ONLY)
        self.second = (Y_ONLY, X_ONLY) if self.square else (Y_ONLY, Y_ONLY)
        self.spots = [(j, i) for j in range(self.rows) for i in range(self.cols)]

    def permute(self, a, place):
        perm = []
        for y in range(self.rows):
            for x in range(self.cols):
                for z in range(self.depth):
                    for c in range(CORES):
                        src = (y * self.cols + x) * self.n_t + z * CORES + c
                        v, u, w, d = place(y, x, z, c)
                        dst = (v % self.rows * self.cols + u % self.cols) * self.n_t
                        perm.append((src, dst + w % self.depth * CORES + d % CORES))
        return lax.ppermute(a, ("dp", "tensor"), perm)

    def plane(self, a, ways, step):
        def place(y, x, z, c):
            return y + ways[c][0] * step, x + ways[c][1] * step, z, c

        return self.permute(a, place)

    def along(self, a, step):
        return self.permute(a, lambda y, x, z, c: (y, x, z + step, c))

    def sibling(self, a):
        return self.permute(a, lambda y, x, z, c: (y, x, z, c + 1))

    def reach(self, a):
        got = {(0, 0): a}
        for i in range(1, self.cols):
            got[0, i] = self.plane(a, self.first, i)
        for j in range(1, self.rows):
            got[j, 0] = self.plane(a, self.second, j)
        return got

    def fill(self, got, *late):
        late = (*late, *got.values())
        for j in range(1, self.rows):
            for i in range(1, self.cols):
                got[j, i] = self.plane(after(got[0, i], *late), self.second, j)
        return [got[s] for s in self.spots]

    def owners(self, y, x, c):
        ways = [(self.first[k], self.second[k]) for k in range(CORES)]
        out = []
        for j, i in self.spots:
            at = [
                (y - f[0] * i - s[0] * j) % self.rows * self.cols + (x - f[1] * i - s[1] * j) % self.cols
                for f, s in ways
            ]
            out.append(jnp.where(c == 0, at[0], at[1]))
        return out

    def sibling_spot(self, k):
        j, i = self.spots[k]
        return self.spots.index((i, j)) if self.square else k


def far(a):
    return pltpu.with_memory_space_constraint(a, pltpu.HBM)


def after(a, *others):
    return lax.optimization_barrier((a, *others))[0] if others else a


def diagonal(size):
    row = lax.broadcasted_iota(jnp.int32, (size, size), 0)
    return row == lax.broadcasted_iota(jnp.int32, (size, size), 1)


def to_column(row):
    return jnp.sum(jnp.where(diagonal(row.shape[1]), row, 0.0), axis=1, keepdims=True)


def to_row(column):
    return jnp.sum(jnp.where(diagonal(column.shape[0]), column, 0.0), axis=0, keepdims=True)


def layer_kernel(n, place, layer, first, last, *refs):
    refs = list(refs)
    start_ref = refs.pop(0)
    blocks = [refs.pop(0) for _ in range(CORES * n)]
    head_ref = refs.pop(0)
    acc_ref = None if first else refs.pop(0)
    marks = [refs.pop(0) for _ in range(n)] if last else None
    out_ref, rows, weights, sems = refs[:4]
    acc = refs[4] if last else out_ref
    tok = rows.shape[0] // n
    feat = blocks[0].shape[1]
    copies = []
    for half in range(CORES):
        offset = pl.multiple_of(start_ref[0] + half * feat, feat)
        source = head_ref.at[pl.ds(offset, feat)]
        copies.append(pltpu.make_async_copy(source, weights.at[half], sems.at[half]))
        copies[-1].start()
    for c in range(CORES):
        columns = pl.ds(pl.multiple_of(start_ref[1 + c], feat), feat)
        for k in range(n):
            spot = place[k] if c else k
            part = blocks[c * n + k][layer * tok : (layer + 1) * tok, :]
            rows[spot * tok : (spot + 1) * tok, columns] = part
    for half in range(CORES):
        copies[half].wait()
        part = rows[:, half * feat : (half + 1) * feat]
        product = jnp.dot(part, weights[half], preferred_element_type=jnp.float32)
        if half:
            acc[...] += product
        else:
            acc[...] = product if first else acc_ref[...] + product
    if not last:
        return
    base = start_ref[1 + CORES]
    for b in range(n):
        logits = acc[b * tok : (b + 1) * tok, :]
        top = jnp.max(logits, axis=1, keepdims=True)
        total = jnp.sum(jnp.exp(logits - top), axis=1, keepdims=True)
        entry = lax.broadcasted_iota(jnp.int32, logits.shape, 1) + base
        digits = marks[b][tok : tok + EXTRA, :tok].astype(jnp.float32)
        target = (digits[0:1, :] * BASE + digits[1:2, :]) * BASE + digits[2:3, :]
        target = to_column(target).astype(jnp.int32)
        pick = jnp.sum(jnp.where(entry == target, logits, 0.0), axis=1, keepdims=True)
        spot = start_ref[2 + CORES + b]
        for peer in range(out_ref.shape[1]):
            out_ref[spot, peer, 0:1, :] = to_row(top)
            out_ref[spot, peer, 1:2, :] = to_row(total)
            out_ref[spot, peer, 2:3, :] = to_row(pick)


def layer_product(tok, peers, starts, blocks, layer, place, head, acc, marks, last):
    n = len(place)
    feat = blocks[0].shape[1]
    vocab = head.shape[1]
    vmem = pl.BlockSpec(memory_space=pltpu.VMEM)
    first = acc is None
    logits = jax.ShapeDtypeStruct((n * tok, vocab), jnp.float32)
    operands = [starts, *blocks, far(head)] + ([] if first else [acc]) + (marks if last else [])
    specs = [vmem] * len(operands)
    specs[0] = pl.BlockSpec(memory_space=pltpu.SMEM)
    specs[1 + len(blocks)] = pl.BlockSpec(memory_space=pltpu.HBM)
    scratch = [
        pltpu.VMEM((n * tok, CORES * feat), jnp.bfloat16),
        pltpu.VMEM((CORES, feat, vocab), jnp.bfloat16),
        pltpu.SemaphoreType.DMA((CORES,)),
    ]
    if last:
        scratch.append(pltpu.VMEM(logits.shape, jnp.float32))
    work = 2 * n * tok * CORES * feat * vocab
    return pl.pallas_call(
        functools.partial(layer_kernel, n, place, layer, first, last),
        out_shape=jax.ShapeDtypeStruct((n, peers, 3, tok), jnp.float32) if last else logits,
        in_specs=specs,
        out_specs=vmem,
        scratch_shapes=scratch,
        compiler_params=pltpu.CompilerParams(vmem_limit_bytes=VMEM_LIMIT),
        cost_estimate=pl.CostEstimate(
            flops=work, bytes_accessed=2 * CORES * feat * vocab, transcendentals=0
        ),
    )(*operands)


def fetch(pairs, sems):
    copies = [pltpu.make_async_copy(a, b, sems.at[i]) for i, (a, b) in enumerate(pairs)]
    for copy in copies:
        copy.start()
    for copy in copies:
        copy.wait()


def norm_kernel(size, *refs):
    blocks, sums, gains, rest = refs[:size], refs[size : size + 2], refs[size + 2 : 2 * size + 2], refs[2 * size + 2 :]
    out_ref, raw, sems = rest[1], rest[2], rest[-1]
    if len(rest) == 3:
        out_ref, raw = rest[0], rest[1]
    tok, feat = blocks[0].shape
    with_target = len(rest) > 3
    target = rest[3] if with_target else None
    pairs = [(blocks[j], raw.at[j]) for j in range(size)] + ([(rest[0], target)] if with_target else [])
    fetch(pairs, sems)
    scale = to_column(lax.rsqrt((sums[0][...] + sums[1][...]) / D + 1e-06))
    for j in range(size):
        part = raw[j].astype(jnp.float32) * scale * gains[j][:, :feat]
        out_ref[j * tok : (j + 1) * tok, :] = part.astype(jnp.bfloat16)
    if with_target:
        target = target[...]
        row = lax.broadcasted_iota(jnp.int32, (EXTRA, tok), 0)
        digits = jnp.where(row == 0, target >> 14, jnp.where(row == 1, (target >> 7) & 127, target & 127))
        out_ref[tok:, :] = jnp.zeros((EXTRA, feat), jnp.bfloat16)
        out_ref[tok:, :tok] = digits.astype(jnp.float32).astype(jnp.bfloat16)


def normalized(blocks, sums, gains, target=None):
    tok, feat = blocks[0].shape
    size = len(blocks)
    if target is not None:
        blocks = [far(a) for a in blocks]
    operands = [*blocks, *sums, *gains] + ([] if target is None else [far(target)])
    rows = size * tok + (0 if target is None else EXTRA)
    vmem, whole = pl.BlockSpec(memory_space=pltpu.VMEM), pl.BlockSpec(memory_space=pl.ANY)
    specs = [whole] * size + [vmem] * (len(sums) + size) + ([] if target is None else [whole])
    scratch = [pltpu.VMEM((size, tok, feat), jnp.bfloat16)]
    if target is not None:
        scratch.append(pltpu.VMEM(target.shape, target.dtype))
    scratch.append(pltpu.SemaphoreType.DMA((size + 1,)))
    return pl.pallas_call(
        functools.partial(norm_kernel, size),
        out_shape=jax.ShapeDtypeStruct((rows, feat), jnp.bfloat16),
        in_specs=specs,
        out_specs=vmem,
        scratch_shapes=scratch,
        compiler_params=pltpu.CompilerParams(vmem_limit_bytes=SMALL_LIMIT),
    )(*operands)


def squares_kernel(hidden_ref, gain_ref, out_ref, raw, gain, sems):
    fetch([(hidden_ref, raw), (gain_ref, gain)], sems)
    values = raw[...].astype(jnp.float32)
    feat = values.shape[1]
    out_ref[:, :feat] = gain[...]
    out_ref[:, feat:] = to_row(jnp.sum(values * values, axis=1, keepdims=True))


def squares(hidden, gain):
    tok, feat = hidden.shape
    return pl.pallas_call(
        squares_kernel,
        out_shape=jax.ShapeDtypeStruct((1, feat + tok), jnp.float32),
        in_specs=[pl.BlockSpec(memory_space=pl.ANY)] * 2,
        out_specs=pl.BlockSpec(memory_space=pltpu.VMEM),
        scratch_shapes=[
            pltpu.VMEM((tok, feat), jnp.bfloat16),
            pltpu.VMEM((1, feat), jnp.float32),
            pltpu.SemaphoreType.DMA((2,)),
        ],
        compiler_params=pltpu.CompilerParams(vmem_limit_bytes=SMALL_LIMIT),
    )(far(hidden), far(gain))


def body(hidden, norm_gain, head, targets, old_logprob, lengths):
    n_dp, n_t = lax.axis_size("dp"), lax.axis_size("tensor")
    grid = Grid(n_dp, n_t)
    depth = grid.depth
    tok, feat = hidden.shape
    tensor = lax.axis_index("tensor")
    z_me, c_me = tensor // CORES, tensor % CORES
    groups = [[0]] + [[d, depth - d] for d in range(1, (depth + 1) // 2)] + [[depth // 2]]
    place = [grid.sibling_spot(k) for k in range(n_dp)]

    packed = squares(hidden, norm_gain[None, :])
    fine = [grid.along(packed, dz) if dz else packed for dz in range(depth)]
    layers = {0: hidden}
    before = []
    for group in groups[1:]:
        for dz in group:
            layers[dz] = grid.along(after(hidden, *before), dz)
        before = [layers[dz] for dz in group]

    own_sum = sum(a[:, feat:] for a in fine)
    own_sum = after(own_sum, *(layers[dz] for dz in groups[1]))
    sums = (own_sum, grid.sibling(own_sum))

    vocab_cols = head.shape[1]
    vocab_start = lax.axis_index(("dp", "tensor")) * vocab_cols
    plane = lax.axis_index("dp")
    owners = grid.owners(plane // grid.cols, plane % grid.cols, c_me)
    normed, reached = [], []
    for at, group in enumerate(groups):
        sources = [layers[dz] for dz in group]
        if at:
            earlier = [normed[0]] if at == 1 else list(reached[-1].values())
            sources[0] = after(sources[0], *earlier)
        gains = [fine[dz] for dz in group]
        normed.append(normalized(sources, sums, gains, None if at else targets[None, :]))
        reached.append(grid.reach(normed[-1]))
    acc, marks = None, None
    for at, group in enumerate(groups):
        final = at == len(groups) - 1
        held = [] if final else [layers[dz] for dz in groups[at + 1]] if at else [normed[1]]
        spread = grid.fill(dict(reached[at]), *([acc] if at == 1 else []), *held)
        if marks is None:
            marks = spread
        blocks = spread + [grid.sibling(a) for a in spread]
        following = [] if final or not at else [*reached[at + 1].values(), *normed[at + 2 : at + 3]]
        for layer, dz in enumerate(group):
            start = (z_me - dz) % depth * (CORES * feat)
            starts = [start] + [(c_me - dc) % CORES * feat for dc in range(CORES)] + [vocab_start] + owners
            if layer == len(group) - 1:
                blocks[0] = after(blocks[0], *following)
            last = final and layer == len(group) - 1
            acc = layer_product(tok, n_t, jnp.stack(starts), blocks, layer, place, head, acc, marks, last)

    parts = lax.all_to_all(acc.reshape(n_dp * n_t, 3, tok), ("dp", "tensor"), 0, 0, tiled=True)
    top = jnp.max(parts[:, 0], axis=0)
    total = jnp.sum(parts[:, 1] * jnp.exp(parts[:, 0] - top[None, :]), axis=0)
    picked = jnp.sum(parts[:, 2], axis=0)

    seq_count = lengths.shape[0]
    position = jnp.arange(tok // seq_count, dtype=jnp.int32)
    live = (position[None, :] < lengths[:, None]).reshape(-1).astype(jnp.float32)
    logprob = picked - top - jnp.log(total)
    return (live * logprob, live * (logprob - old_logprob))


def solution(mesh):
    in_specs = (
        P("dp", "tensor"),
        P("tensor"),
        P(None, ("dp", "tensor")),
        P("dp"),
        P("dp"),
        P("dp"),
    )
    out_specs = (P("dp"), P("dp"))
    return jax.shard_map(body, mesh=mesh, in_specs=in_specs, out_specs=out_specs, check_vma=False)
```

```python
import functools

import jax
import jax.numpy as jnp
from jax import lax
from jax.experimental import pallas as pl
from jax.experimental.pallas import tpu as pltpu
from jax.sharding import PartitionSpec as P

D = 8192
CORES = 2
X_ONLY, Y_ONLY = (0, 1), (1, 0)
VMEM_LIMIT = 24 * 1024 * 1024
SMALL_LIMIT = 6 * 1024 * 1024
TILES = (256, 384)


class Grid:
    def __init__(self, n_dp, n_t):
        self.n_t = n_t
        self.cols = 2
        self.rows = n_dp // self.cols
        self.depth = n_t // CORES
        self.square = self.rows == self.cols
        self.first = (X_ONLY, Y_ONLY) if self.square else (X_ONLY, X_ONLY)
        self.second = (Y_ONLY, X_ONLY) if self.square else (Y_ONLY, Y_ONLY)
        self.spots = [(j, i) for j in range(self.rows) for i in range(self.cols)]

    def permute(self, a, place):
        perm = []
        for y in range(self.rows):
            for x in range(self.cols):
                for z in range(self.depth):
                    for c in range(CORES):
                        src = (y * self.cols + x) * self.n_t + z * CORES + c
                        v, u, w, d = place(y, x, z, c)
                        dst = (v % self.rows * self.cols + u % self.cols) * self.n_t
                        perm.append((src, dst + w % self.depth * CORES + d % CORES))
        return lax.ppermute(a, ("dp", "tensor"), perm)

    def plane(self, a, ways, step):
        def place(y, x, z, c):
            return y + ways[c][0] * step, x + ways[c][1] * step, z, c

        return self.permute(a, place)

    def along(self, a, step):
        return self.permute(a, lambda y, x, z, c: (y, x, z + step, c))

    def sibling(self, a):
        return self.permute(a, lambda y, x, z, c: (y, x, z, c + 1))

    def reach(self, a):
        got = {(0, 0): a}
        for i in range(1, self.cols):
            got[0, i] = self.plane(a, self.first, i)
        for j in range(1, self.rows):
            got[j, 0] = self.plane(a, self.second, j)
        return got

    def fill(self, got, *late):
        late = (*late, *got.values())
        for j in range(1, self.rows):
            for i in range(1, self.cols):
                got[j, i] = self.plane(after(got[0, i], *late), self.second, j)
        return [got[s] for s in self.spots]

    def owners(self, y, x, c):
        ways = [(self.first[k], self.second[k]) for k in range(CORES)]
        out = []
        for j, i in self.spots:
            at = [
                (y - f[0] * i - s[0] * j) % self.rows * self.cols + (x - f[1] * i - s[1] * j) % self.cols
                for f, s in ways
            ]
            out.append(jnp.where(c == 0, at[0], at[1]))
        return out

    def sibling_spot(self, k):
        j, i = self.spots[k]
        return self.spots.index((i, j)) if self.square else k


def far(a):
    return pltpu.with_memory_space_constraint(a, pltpu.HBM)


def after(a, *others):
    return lax.optimization_barrier((a, *others))[0] if others else a


def diagonal(size):
    row = lax.broadcasted_iota(jnp.int32, (size, size), 0)
    return row == lax.broadcasted_iota(jnp.int32, (size, size), 1)


def to_column(row):
    return jnp.sum(jnp.where(diagonal(row.shape[1]), row, 0.0), axis=1, keepdims=True)


def to_row(column):
    return jnp.sum(jnp.where(diagonal(column.shape[0]), column, 0.0), axis=0, keepdims=True)


def column_tiles(vocab):
    cuts = [0]
    for width in TILES:
        if cuts[-1] + width < vocab:
            cuts.append(cuts[-1] + width)
    return list(zip(cuts, [*cuts[1:], vocab], strict=True))


def layer_kernel(n, n_t, place, layer, first, last, *refs):
    refs = list(refs)
    start_ref, fine_ref = refs.pop(0), refs.pop(0)
    blocks = [refs.pop(0) for _ in range(CORES * n)]
    head_ref = refs.pop(0)
    acc_ref = None if first else refs.pop(0)
    out_ref, raw, rows, weights, raw_sem, head_sem = refs[:6]
    acc = refs[6] if last else out_ref
    feat = raw.shape[2]
    tok = raw.shape[1] // n
    vocab = weights.shape[1]
    z_from, c_me, base = start_ref[0], start_ref[1], start_ref[2]
    owners = [start_ref[3 + k] for k in range(n)]

    offset = pl.multiple_of(z_from * (CORES * feat), CORES * feat)
    tiles = column_tiles(vocab)
    head_copies = [
        pltpu.make_async_copy(
            head_ref.at[pl.ds(offset, CORES * feat), pl.ds(lo, hi - lo)],
            weights.at[:, pl.ds(lo, hi - lo)],
            head_sem.at[i],
        )
        for i, (lo, hi) in enumerate(tiles)
    ]
    block_copies = []
    for c in range(CORES):
        for k in range(n):
            spot = place[k] if c else k
            block_copies.append(
                pltpu.make_async_copy(
                    blocks[c * n + k].at[pl.ds(layer * tok, tok)],
                    raw.at[c, pl.ds(spot * tok, tok)],
                    raw_sem.at[c * n + k],
                )
            )
    head_copies[0].start()
    for copy in block_copies:
        copy.start()
    for copy in head_copies[1:]:
        copy.start()

    def peer_rows(k):
        return pl.ds(pl.multiple_of(owners[k] * n_t, n_t), n_t)

    scales = []
    for k in range(n):
        sums = jnp.sum(fine_ref[peer_rows(k), feat : feat + tok], axis=0, keepdims=True)
        scales.append(to_column(lax.rsqrt(sums / D + 1e-06)))
    for c in range(CORES):
        core = 1 - c_me if c else c_me
        gain = fine_ref[pl.ds(z_from * CORES + core, 1), :feat]
        columns = pl.ds(pl.multiple_of(core * feat, feat), feat)
        for k in range(n):
            block_copies[c * n + k].wait()
        for k in range(n):
            here = slice(k * tok, (k + 1) * tok)
            part = raw[c, here, :].astype(jnp.float32) * scales[k] * gain
            rows[here, columns] = part.astype(jnp.bfloat16)
    for copy, (lo, hi) in zip(head_copies, tiles, strict=True):
        copy.wait()
        product = jnp.dot(rows[...], weights[:, lo:hi], preferred_element_type=jnp.float32)
        acc[:, lo:hi] = product if first else acc_ref[:, lo:hi] + product
    if not last:
        return
    for b in range(n):
        logits = acc[b * tok : (b + 1) * tok, :]
        top = jnp.max(logits, axis=1, keepdims=True)
        total = jnp.sum(jnp.exp(logits - top), axis=1, keepdims=True)
        entry = lax.broadcasted_iota(jnp.int32, logits.shape, 1) + base
        target = fine_ref[peer_rows(b), feat + tok : feat + 2 * tok][0:1, :]
        target = to_column(target).astype(jnp.int32)
        pick = jnp.sum(jnp.where(entry == target, logits, 0.0), axis=1, keepdims=True)
        for peer in range(n_t):
            out_ref[owners[b], peer, 0:1, :] = to_row(top)
            out_ref[owners[b], peer, 1:2, :] = to_row(total)
            out_ref[owners[b], peer, 2:3, :] = to_row(pick)


def layer_product(tok, n_t, starts, fine, blocks, layer, place, head, acc, last):
    n = len(place)
    feat = blocks[0].shape[1]
    vocab = head.shape[1]
    vmem, whole = pl.BlockSpec(memory_space=pltpu.VMEM), pl.BlockSpec(memory_space=pl.ANY)
    first = acc is None
    logits = jax.ShapeDtypeStruct((n * tok, vocab), jnp.float32)
    operands = [starts, fine, *blocks, far(head)] + ([] if first else [acc])
    specs = [pl.BlockSpec(memory_space=pltpu.SMEM), vmem] + [whole] * (len(blocks) + 1) + [vmem] * (not first)
    scratch = [
        pltpu.VMEM((CORES, n * tok, feat), jnp.bfloat16),
        pltpu.VMEM((n * tok, CORES * feat), jnp.bfloat16),
        pltpu.VMEM((CORES * feat, vocab), jnp.bfloat16),
        pltpu.SemaphoreType.DMA((CORES * n,)),
        pltpu.SemaphoreType.DMA((len(column_tiles(vocab)),)),
    ]
    if last:
        scratch.append(pltpu.VMEM(logits.shape, jnp.float32))
    work = 2 * n * tok * CORES * feat * vocab
    return pl.pallas_call(
        functools.partial(layer_kernel, n, n_t, place, layer, first, last),
        out_shape=jax.ShapeDtypeStruct((n, n_t, 3, tok), jnp.float32) if last else logits,
        in_specs=specs,
        out_specs=vmem,
        scratch_shapes=scratch,
        compiler_params=pltpu.CompilerParams(vmem_limit_bytes=VMEM_LIMIT),
        cost_estimate=pl.CostEstimate(
            flops=work, bytes_accessed=2 * CORES * feat * vocab, transcendentals=0
        ),
    )(*operands)


def squares_kernel(hidden_ref, gain_ref, target_ref, out_ref, raw, gain, target, sems):
    pairs = ((hidden_ref, raw), (gain_ref, gain), (target_ref, target))
    copies = [pltpu.make_async_copy(a, b, sems.at[i]) for i, (a, b) in enumerate(pairs)]
    for copy in copies:
        copy.start()
    for copy in copies:
        copy.wait()
    tok, feat = raw.shape
    values = raw[...].astype(jnp.float32)
    sums = to_row(jnp.sum(values * values, axis=1, keepdims=True))
    peers = out_ref.shape[0]
    out_ref[:, :feat] = jnp.broadcast_to(gain[...], (peers, feat))
    out_ref[:, feat : feat + tok] = jnp.broadcast_to(sums, (peers, tok))
    out_ref[:, feat + tok :] = jnp.broadcast_to(target[...].astype(jnp.float32), (peers, tok))


def squares(hidden, gain, targets, peers):
    tok, feat = hidden.shape
    return pl.pallas_call(
        squares_kernel,
        out_shape=jax.ShapeDtypeStruct((peers, feat + 2 * tok), jnp.float32),
        in_specs=[pl.BlockSpec(memory_space=pltpu.HBM)] * 3,
        out_specs=pl.BlockSpec(memory_space=pltpu.VMEM),
        scratch_shapes=[
            pltpu.VMEM(hidden.shape, hidden.dtype),
            pltpu.VMEM(gain.shape, gain.dtype),
            pltpu.VMEM(targets.shape, targets.dtype),
            pltpu.SemaphoreType.DMA((3,)),
        ],
        compiler_params=pltpu.CompilerParams(vmem_limit_bytes=SMALL_LIMIT),
    )(far(hidden), far(gain), far(targets))


def body(hidden, norm_gain, head, targets, old_logprob, lengths):
    n_dp, n_t = lax.axis_size("dp"), lax.axis_size("tensor")
    grid = Grid(n_dp, n_t)
    depth = grid.depth
    tok, feat = hidden.shape
    plane, tensor = lax.axis_index("dp"), lax.axis_index("tensor")
    z_me, c_me = tensor // CORES, tensor % CORES
    owners = grid.owners(plane // grid.cols, plane % grid.cols, c_me)
    groups = [[0]] + [[d, depth - d] for d in range(1, (depth + 1) // 2)] + [[depth // 2]]
    place = [grid.sibling_spot(k) for k in range(n_dp)]

    layers = {0: hidden}
    before = []
    for group in groups[1:]:
        for dz in group:
            layers[dz] = grid.along(after(hidden, *before), dz)
        before = [layers[dz] for dz in group]
    reached = [grid.reach(hidden)]
    for group in groups[1:]:
        sources = [layers[dz] for dz in group]
        sources[0] = after(sources[0], *reached[-1].values())
        joined = jnp.concatenate(sources) if len(sources) > 1 else sources[0]
        reached.append(grid.reach(joined))

    packed = squares(hidden, norm_gain[None, :], targets[None, :], n_dp * n_t)
    fine = lax.all_to_all(packed, ("dp", "tensor"), 0, 0, tiled=True)

    vocab_cols = head.shape[1]
    vocab_start = lax.axis_index(("dp", "tensor")) * vocab_cols
    acc = None
    for at, group in enumerate(groups):
        final = at == len(groups) - 1
        held = [] if final or not at else [layers[dz] for dz in groups[at + 1]]
        spread = grid.fill(dict(reached[at]), *([acc] if at == 1 else []), *held)
        blocks = spread + [grid.sibling(a) for a in spread]
        following = [] if final or not at else list(reached[at + 1].values())
        for layer, dz in enumerate(group):
            starts = jnp.stack([(z_me - dz) % depth, c_me, vocab_start] + owners)
            if layer == len(group) - 1:
                starts = after(starts, *following)
            last = final and layer == len(group) - 1
            acc = layer_product(tok, n_t, starts, fine, blocks, layer, place, head, acc, last)

    parts = lax.all_to_all(acc.reshape(n_dp * n_t, 3, tok), ("dp", "tensor"), 0, 0, tiled=True)
    top = jnp.max(parts[:, 0], axis=0)
    total = jnp.sum(parts[:, 1] * jnp.exp(parts[:, 0] - top[None, :]), axis=0)
    picked = jnp.sum(parts[:, 2], axis=0)

    seq_count = lengths.shape[0]
    position = jnp.arange(tok // seq_count, dtype=jnp.int32)
    live = (position[None, :] < lengths[:, None]).reshape(-1).astype(jnp.float32)
    logprob = picked - top - jnp.log(total)
    return (live * logprob, live * (logprob - old_logprob))


def solution(mesh):
    in_specs = (
        P("dp", "tensor"),
        P("tensor"),
        P(None, ("dp", "tensor")),
        P("dp"),
        P("dp"),
        P("dp"),
    )
    out_specs = (P("dp"), P("dp"))
    return jax.shard_map(body, mesh=mesh, in_specs=in_specs, out_specs=out_specs, check_vma=False)
```

```python
import functools

import jax
import jax.numpy as jnp
from jax import lax
from jax.experimental import pallas as pl
from jax.experimental.pallas import tpu as pltpu
from jax.sharding import PartitionSpec as P

D = 8192
CORES = 2
X_ONLY, Y_ONLY = (0, 1), (1, 0)
VMEM_LIMIT = 30 * 1024 * 1024
SMALL_LIMIT = 6 * 1024 * 1024
TILES = (256, 384)


class Grid:
    def __init__(self, n_dp, n_t):
        self.n_t = n_t
        self.cols = 2
        self.rows = n_dp // self.cols
        self.depth = n_t // CORES
        self.square = self.rows == self.cols
        self.first = (X_ONLY, Y_ONLY) if self.square else (X_ONLY, X_ONLY)
        self.second = (Y_ONLY, X_ONLY) if self.square else (Y_ONLY, Y_ONLY)
        self.spots = [(j, i) for j in range(self.rows) for i in range(self.cols)]

    def permute(self, a, place):
        perm = []
        for y in range(self.rows):
            for x in range(self.cols):
                for z in range(self.depth):
                    for c in range(CORES):
                        src = (y * self.cols + x) * self.n_t + z * CORES + c
                        v, u, w, d = place(y, x, z, c)
                        dst = (v % self.rows * self.cols + u % self.cols) * self.n_t
                        perm.append((src, dst + w % self.depth * CORES + d % CORES))
        return lax.ppermute(a, ("dp", "tensor"), perm)

    def plane(self, a, ways, step):
        def place(y, x, z, c):
            return y + ways[c][0] * step, x + ways[c][1] * step, z, c

        return self.permute(a, place)

    def along(self, a, step):
        return self.permute(a, lambda y, x, z, c: (y, x, z + step, c))

    def sibling(self, a):
        return self.permute(a, lambda y, x, z, c: (y, x, z, c + 1))

    def reach(self, a):
        got = {(0, 0): a}
        for i in range(1, self.cols):
            got[0, i] = self.plane(a, self.first, i)
        for j in range(1, self.rows):
            got[j, 0] = self.plane(a, self.second, j)
        return got

    def fill(self, got, *late):
        late = (*late, *got.values())
        for j in range(1, self.rows):
            for i in range(1, self.cols):
                got[j, i] = self.plane(after(got[0, i], *late), self.second, j)
        return [got[s] for s in self.spots]

    def owners(self, y, x, c):
        ways = [(self.first[k], self.second[k]) for k in range(CORES)]
        out = []
        for j, i in self.spots:
            at = [
                (y - f[0] * i - s[0] * j) % self.rows * self.cols + (x - f[1] * i - s[1] * j) % self.cols
                for f, s in ways
            ]
            out.append(jnp.where(c == 0, at[0], at[1]))
        return out

    def sibling_spot(self, k):
        j, i = self.spots[k]
        return self.spots.index((i, j)) if self.square else k


def far(a):
    return pltpu.with_memory_space_constraint(a, pltpu.HBM)


def after(a, *others):
    return lax.optimization_barrier((a, *others))[0] if others else a


def diagonal(size):
    row = lax.broadcasted_iota(jnp.int32, (size, size), 0)
    return row == lax.broadcasted_iota(jnp.int32, (size, size), 1)


def to_column(row):
    return jnp.sum(jnp.where(diagonal(row.shape[1]), row, 0.0), axis=1, keepdims=True)


def to_row(column):
    return jnp.sum(jnp.where(diagonal(column.shape[0]), column, 0.0), axis=0, keepdims=True)


def column_tiles(vocab):
    cuts = [0]
    for width in TILES:
        if cuts[-1] + width < vocab:
            cuts.append(cuts[-1] + width)
    return list(zip(cuts, [*cuts[1:], vocab], strict=True))


def group_kernel(n, n_t, place, size, first, last, *refs):
    refs = list(refs)
    start_ref, fine_ref = refs.pop(0), refs.pop(0)
    blocks = [refs.pop(0) for _ in range(CORES * n)]
    head_ref = refs.pop(0)
    acc_ref = None if first else refs.pop(0)
    out_ref, raw, rows, weights, acc, fine, raw_sem, head_sem, acc_sem, fine_sem = refs
    feat = raw.shape[3]
    tok = raw.shape[2] // n
    vocab = weights.shape[2]
    tiles = column_tiles(vocab)
    c_me, base = start_ref[size], start_ref[size + 1]
    owners = [start_ref[size + 2 + k] for k in range(n)]

    fine_copy = pltpu.make_async_copy(fine_ref, fine, fine_sem)
    fine_copy.start()
    head_copies, block_copies = [], []
    for j in range(size):
        offset = pl.multiple_of(start_ref[j] * (CORES * feat), CORES * feat)
        head_copies.append(
            [
                pltpu.make_async_copy(
                    head_ref.at[pl.ds(offset, CORES * feat), pl.ds(lo, hi - lo)],
                    weights.at[j, :, pl.ds(lo, hi - lo)],
                    head_sem.at[j, i],
                )
                for i, (lo, hi) in enumerate(tiles)
            ]
        )
        block_copies.append(
            [
                pltpu.make_async_copy(
                    blocks[c * n + k].at[pl.ds(j * tok, tok)],
                    raw.at[j, c, pl.ds((place[k] if c else k) * tok, tok)],
                    raw_sem.at[j, c * n + k],
                )
                for c in range(CORES)
                for k in range(n)
            ]
        )
        head_copies[j][0].start()
        for copy in block_copies[j]:
            copy.start()
        for copy in head_copies[j][1:]:
            copy.start()
        if j == 0 and not first:
            acc_copy = pltpu.make_async_copy(acc_ref, acc, acc_sem.at[len(tiles)])
            acc_copy.start()

    def peers(k):
        return pl.ds(owners[k] * n_t, n_t)

    fine_copy.wait()
    scales = []
    for k in range(n):
        sums = jnp.sum(fine[peers(k), :, feat : feat + tok], axis=0)
        scales.append(to_column(lax.rsqrt(sums / D + 1e-06)))
    out_copies = []
    for j in range(size):
        for c in range(CORES):
            core = 1 - c_me if c else c_me
            gain = fine[start_ref[j] * CORES + core, :, :feat]
            columns = pl.ds(pl.multiple_of(core * feat, feat), feat)
            for k in range(n):
                block_copies[j][c * n + k].wait()
            for k in range(n):
                here = slice(k * tok, (k + 1) * tok)
                part = raw[j, c, here, :].astype(jnp.float32) * scales[k] * gain
                rows[here, columns] = part.astype(jnp.bfloat16)
        for i, (lo, hi) in enumerate(tiles):
            head_copies[j][i].wait()
            product = jnp.dot(rows[...], weights[j, :, lo:hi], preferred_element_type=jnp.float32)
            if j == 0 and i == 0 and not first:
                acc_copy.wait()
            acc[:, lo:hi] = product if first and j == 0 else acc[:, lo:hi] + product
            if j == size - 1 and not last:
                here = pl.ds(lo, hi - lo)
                copy = pltpu.make_async_copy(acc.at[:, here], out_ref.at[:, here], acc_sem.at[i])
                copy.start()
                out_copies.append(copy)
    for copy in out_copies:
        copy.wait()
    if not last:
        return
    for b in range(n):
        logits = acc[b * tok : (b + 1) * tok, :]
        top = jnp.max(logits, axis=1, keepdims=True)
        total = jnp.sum(jnp.exp(logits - top), axis=1, keepdims=True)
        entry = lax.broadcasted_iota(jnp.int32, logits.shape, 1) + base
        target = fine[owners[b] * n_t, :, feat + tok : feat + 2 * tok]
        target = to_column(target).astype(jnp.int32)
        pick = jnp.sum(jnp.where(entry == target, logits, 0.0), axis=1, keepdims=True)
        for peer in range(n_t):
            out_ref[owners[b], peer, 0:1, :] = to_row(top)
            out_ref[owners[b], peer, 1:2, :] = to_row(total)
            out_ref[owners[b], peer, 2:3, :] = to_row(pick)


def group_product(tok, n_t, starts, size, fine, blocks, place, head, acc, last):
    n = len(place)
    feat = blocks[0].shape[1]
    vocab = head.shape[1]
    vmem, whole = pl.BlockSpec(memory_space=pltpu.VMEM), pl.BlockSpec(memory_space=pl.ANY)
    first = acc is None
    logits = jax.ShapeDtypeStruct((n * tok, vocab), jnp.float32)
    operands = [starts, fine, *blocks, far(head)] + ([] if first else [acc])
    specs = [pl.BlockSpec(memory_space=pltpu.SMEM)] + [whole] * (len(operands) - 1)
    tiles = len(column_tiles(vocab))
    scratch = [
        pltpu.VMEM((size, CORES, n * tok, feat), jnp.bfloat16),
        pltpu.VMEM((n * tok, CORES * feat), jnp.bfloat16),
        pltpu.VMEM((size, CORES * feat, vocab), jnp.bfloat16),
        pltpu.VMEM(logits.shape, jnp.float32),
        pltpu.VMEM(fine.shape, fine.dtype),
        pltpu.SemaphoreType.DMA((size, CORES * n)),
        pltpu.SemaphoreType.DMA((size, tiles)),
        pltpu.SemaphoreType.DMA((tiles + 1,)),
        pltpu.SemaphoreType.DMA,
    ]
    work = 2 * n * tok * CORES * feat * vocab * size
    return pl.pallas_call(
        functools.partial(group_kernel, n, n_t, place, size, first, last),
        out_shape=jax.ShapeDtypeStruct((n, n_t, 3, tok), jnp.float32) if last else logits,
        in_specs=specs,
        out_specs=vmem if last else whole,
        scratch_shapes=scratch,
        compiler_params=pltpu.CompilerParams(vmem_limit_bytes=VMEM_LIMIT),
        cost_estimate=pl.CostEstimate(
            flops=work, bytes_accessed=2 * CORES * feat * vocab * size, transcendentals=0
        ),
    )(*operands)


def squares_kernel(hidden_ref, gain_ref, target_ref, out_ref, raw, gain, target, sems):
    pairs = ((hidden_ref, raw), (gain_ref, gain), (target_ref, target))
    copies = [pltpu.make_async_copy(a, b, sems.at[i]) for i, (a, b) in enumerate(pairs)]
    for copy in copies:
        copy.start()
    for copy in copies:
        copy.wait()
    tok, feat = raw.shape
    values = raw[...].astype(jnp.float32)
    sums = to_row(jnp.sum(values * values, axis=1, keepdims=True))
    peers = out_ref.shape[0]
    for peer in range(peers):
        out_ref[peer, :, :feat] = gain[...]
        out_ref[peer, :, feat : feat + tok] = sums
        out_ref[peer, :, feat + tok :] = target[...].astype(jnp.float32)


def squares(hidden, gain, targets, peers):
    tok, feat = hidden.shape
    return pl.pallas_call(
        squares_kernel,
        out_shape=jax.ShapeDtypeStruct((peers, 1, feat + 2 * tok), jnp.float32),
        in_specs=[pl.BlockSpec(memory_space=pltpu.HBM)] * 3,
        out_specs=pl.BlockSpec(memory_space=pltpu.VMEM),
        scratch_shapes=[
            pltpu.VMEM(hidden.shape, hidden.dtype),
            pltpu.VMEM(gain.shape, gain.dtype),
            pltpu.VMEM(targets.shape, targets.dtype),
            pltpu.SemaphoreType.DMA((3,)),
        ],
        compiler_params=pltpu.CompilerParams(vmem_limit_bytes=SMALL_LIMIT),
    )(far(hidden), far(gain), far(targets))


def body(hidden, norm_gain, head, targets, old_logprob, lengths):
    n_dp, n_t = lax.axis_size("dp"), lax.axis_size("tensor")
    grid = Grid(n_dp, n_t)
    depth = grid.depth
    tok, feat = hidden.shape
    plane, tensor = lax.axis_index("dp"), lax.axis_index("tensor")
    z_me, c_me = tensor // CORES, tensor % CORES
    owners = grid.owners(plane // grid.cols, plane % grid.cols, c_me)
    groups = [[0]] + [[d, depth - d] for d in range(1, (depth + 1) // 2)] + [[depth // 2]]
    place = [grid.sibling_spot(k) for k in range(n_dp)]

    layers = {0: hidden}
    before = []
    for group in groups[1:]:
        for dz in group:
            layers[dz] = grid.along(after(hidden, *before), dz)
        before = [layers[dz] for dz in group]
    reached = [grid.reach(hidden)]
    for group in groups[1:]:
        sources = [layers[dz] for dz in group]
        sources[0] = after(sources[0], *reached[-1].values())
        joined = jnp.concatenate(sources) if len(sources) > 1 else sources[0]
        reached.append(grid.reach(joined))

    packed = squares(hidden, norm_gain[None, :], targets[None, :], n_dp * n_t)
    fine = lax.all_to_all(packed, ("dp", "tensor"), 0, 0, tiled=True)

    vocab_cols = head.shape[1]
    vocab_start = lax.axis_index(("dp", "tensor")) * vocab_cols
    acc = None
    for at, group in enumerate(groups):
        final = at == len(groups) - 1
        middle = at and not final
        own = grid.sibling(reached[at][0, 0])
        held = [layers[dz] for dz in groups[at + 1]] + [own] if middle else []
        spread = grid.fill(dict(reached[at]), *([acc] if at == 1 else []), *held)
        others = [own] + [grid.sibling(after(a, spread[-1]) if middle else a) for a in spread[1:-1]]
        others.append(grid.sibling(after(spread[-1], acc) if final else spread[-1]))
        blocks = spread + others
        if not at:
            blocks = [far(a) for a in blocks]
        starts = jnp.stack([(z_me - dz) % depth for dz in group] + [c_me, vocab_start] + owners)
        if middle:
            starts = after(starts, *reached[at + 1].values())
        acc = group_product(tok, n_t, starts, len(group), fine, blocks, place, head, acc, final)

    parts = lax.all_to_all(acc.reshape(n_dp * n_t, 3, tok), ("dp", "tensor"), 0, 0, tiled=True)
    top = jnp.max(parts[:, 0], axis=0)
    total = jnp.sum(parts[:, 1] * jnp.exp(parts[:, 0] - top[None, :]), axis=0)
    picked = jnp.sum(parts[:, 2], axis=0)

    seq_count = lengths.shape[0]
    position = jnp.arange(tok // seq_count, dtype=jnp.int32)
    live = (position[None, :] < lengths[:, None]).reshape(-1).astype(jnp.float32)
    logprob = picked - top - jnp.log(total)
    return (live * logprob, live * (logprob - old_logprob))


def solution(mesh):
    in_specs = (
        P("dp", "tensor"),
        P("tensor"),
        P(None, ("dp", "tensor")),
        P("dp"),
        P("dp"),
        P("dp"),
    )
    out_specs = (P("dp"), P("dp"))
    return jax.shard_map(body, mesh=mesh, in_specs=in_specs, out_specs=out_specs, check_vma=False)
```

```python
import functools

import jax
import jax.numpy as jnp
from jax import lax
from jax.experimental import pallas as pl
from jax.experimental.pallas import tpu as pltpu
from jax.sharding import PartitionSpec as P

D = 8192
CORES = 2
X_ONLY, Y_ONLY = (0, 1), (1, 0)
VMEM_LIMIT = 30 * 1024 * 1024
SMALL_LIMIT = 6 * 1024 * 1024
TILES = (256, 384)


class Grid:
    def __init__(self, n_dp, n_t):
        self.n_t = n_t
        self.cols = 2
        self.rows = n_dp // self.cols
        self.depth = n_t // CORES
        self.square = self.rows == self.cols
        self.first = (X_ONLY, Y_ONLY) if self.square else (X_ONLY, X_ONLY)
        self.second = (Y_ONLY, X_ONLY) if self.square else (Y_ONLY, Y_ONLY)
        self.spots = [(j, i) for j in range(self.rows) for i in range(self.cols)]

    def permute(self, a, place):
        perm = []
        for y in range(self.rows):
            for x in range(self.cols):
                for z in range(self.depth):
                    for c in range(CORES):
                        src = (y * self.cols + x) * self.n_t + z * CORES + c
                        v, u, w, d = place(y, x, z, c)
                        dst = (v % self.rows * self.cols + u % self.cols) * self.n_t
                        perm.append((src, dst + w % self.depth * CORES + d % CORES))
        return lax.ppermute(a, ("dp", "tensor"), perm)

    def plane(self, a, ways, step):
        def place(y, x, z, c):
            return y + ways[c][0] * step, x + ways[c][1] * step, z, c

        return self.permute(a, place)

    def along(self, a, step):
        return self.permute(a, lambda y, x, z, c: (y, x, z + step, c))

    def sibling(self, a):
        return self.permute(a, lambda y, x, z, c: (y, x, z, c + 1))

    def reach(self, a):
        got = {(0, 0): a}
        for i in range(1, self.cols):
            got[0, i] = self.plane(a, self.first, i)
        for j in range(1, self.rows):
            got[j, 0] = self.plane(a, self.second, j)
        return got

    def fill(self, got, *late):
        late = (*late, *got.values())
        for j in range(1, self.rows):
            for i in range(1, self.cols):
                got[j, i] = self.plane(after(got[0, i], *late), self.second, j)
        return [got[s] for s in self.spots]

    def owners(self, y, x, c):
        ways = [(self.first[k], self.second[k]) for k in range(CORES)]
        out = []
        for j, i in self.spots:
            at = [
                (y - f[0] * i - s[0] * j) % self.rows * self.cols + (x - f[1] * i - s[1] * j) % self.cols
                for f, s in ways
            ]
            out.append(jnp.where(c == 0, at[0], at[1]))
        return out

    def sibling_spot(self, k):
        j, i = self.spots[k]
        return self.spots.index((i, j)) if self.square else k


def far(a):
    return pltpu.with_memory_space_constraint(a, pltpu.HBM)


def after(a, *others):
    return lax.optimization_barrier((a, *others))[0] if others else a


def diagonal(size):
    row = lax.broadcasted_iota(jnp.int32, (size, size), 0)
    return row == lax.broadcasted_iota(jnp.int32, (size, size), 1)


def to_column(row):
    return jnp.sum(jnp.where(diagonal(row.shape[1]), row, 0.0), axis=1, keepdims=True)


def to_row(column):
    return jnp.sum(jnp.where(diagonal(column.shape[0]), column, 0.0), axis=0, keepdims=True)


def column_tiles(vocab):
    cuts = [0]
    for width in TILES:
        if cuts[-1] + width < vocab:
            cuts.append(cuts[-1] + width)
    return list(zip(cuts, [*cuts[1:], vocab], strict=True))


def group_kernel(n, n_t, place, size, first, last, *refs):
    refs = list(refs)
    start_ref, fine_ref = refs.pop(0), refs.pop(0)
    blocks = [refs.pop(0) for _ in range(CORES * n)]
    head_ref = refs.pop(0)
    acc_ref = None if first else refs.pop(0)
    out_ref, raw, rows, weights, acc, fine, raw_sem, head_sem, acc_sem, fine_sem = refs
    feat = raw.shape[3]
    tok = raw.shape[2] // n
    vocab = weights.shape[2]
    tiles = column_tiles(vocab)
    c_me, base = start_ref[size], start_ref[size + 1]
    owners = [start_ref[size + 2 + k] for k in range(n)]

    fine_copy = pltpu.make_async_copy(fine_ref, fine, fine_sem)
    head_copies, block_copies = [], []
    for j in range(size):
        offset = pl.multiple_of(start_ref[j] * (CORES * feat), CORES * feat)
        head_copies.append(
            [
                pltpu.make_async_copy(
                    head_ref.at[pl.ds(offset, CORES * feat), pl.ds(lo, hi - lo)],
                    weights.at[j, :, pl.ds(lo, hi - lo)],
                    head_sem.at[j, i],
                )
                for i, (lo, hi) in enumerate(tiles)
            ]
        )
        block_copies.append(
            [
                pltpu.make_async_copy(
                    blocks[c * n + k].at[pl.ds(j * tok, tok)],
                    raw.at[j, c, pl.ds((place[k] if c else k) * tok, tok)],
                    raw_sem.at[j, c * n + k],
                )
                for c in range(CORES)
                for k in range(n)
            ]
        )
    stages = []
    for j in range(size):
        stages.append([*block_copies[j], head_copies[j][0]])
        stages += [[copy] for copy in head_copies[j][1:]]
    stages[0].insert(0, fine_copy)
    if not first:
        acc_copy = pltpu.make_async_copy(acc_ref, acc, acc_sem.at[len(tiles)])
        stages[1].append(acc_copy)

    def advance():
        for copy in stages.pop(0) if stages else ():
            copy.start()

    advance()

    def peers(k):
        return pl.ds(owners[k] * n_t, n_t)

    fine_copy.wait()
    scales = []
    for k in range(n):
        sums = jnp.sum(fine[peers(k), :, feat : feat + tok], axis=0)
        scales.append(to_column(lax.rsqrt(sums / D + 1e-06)))
    out_copies = []
    for j in range(size):
        for c in range(CORES):
            core = 1 - c_me if c else c_me
            gain = fine[start_ref[j] * CORES + core, :, :feat]
            columns = pl.ds(pl.multiple_of(core * feat, feat), feat)
            for k in range(n):
                block_copies[j][c * n + k].wait()
            if j == 0 and c == CORES - 1:
                advance()
            for k in range(n):
                here = slice(k * tok, (k + 1) * tok)
                part = raw[j, c, here, :].astype(jnp.float32) * scales[k] * gain
                rows[here, columns] = part.astype(jnp.bfloat16)
        for i, (lo, hi) in enumerate(tiles):
            head_copies[j][i].wait()
            if i or j:
                advance()
            product = jnp.dot(rows[...], weights[j, :, lo:hi], preferred_element_type=jnp.float32)
            if j == 0 and i == 0 and not first:
                acc_copy.wait()
            acc[:, lo:hi] = product if first and j == 0 else acc[:, lo:hi] + product
            if j == size - 1 and not last:
                here = pl.ds(lo, hi - lo)
                copy = pltpu.make_async_copy(acc.at[:, here], out_ref.at[:, here], acc_sem.at[i])
                copy.start()
                out_copies.append(copy)
    for copy in out_copies:
        copy.wait()
    if not last:
        return
    for b in range(n):
        logits = acc[b * tok : (b + 1) * tok, :]
        top = jnp.max(logits, axis=1, keepdims=True)
        total = jnp.sum(jnp.exp(logits - top), axis=1, keepdims=True)
        entry = lax.broadcasted_iota(jnp.int32, logits.shape, 1) + base
        target = fine[owners[b] * n_t, :, feat + tok : feat + 2 * tok]
        target = to_column(target).astype(jnp.int32)
        pick = jnp.sum(jnp.where(entry == target, logits, 0.0), axis=1, keepdims=True)
        for peer in range(n_t):
            out_ref[owners[b], peer, 0:1, :] = to_row(top)
            out_ref[owners[b], peer, 1:2, :] = to_row(total)
            out_ref[owners[b], peer, 2:3, :] = to_row(pick)


def group_product(tok, n_t, starts, size, fine, blocks, place, head, acc, last):
    n = len(place)
    feat = blocks[0].shape[1]
    vocab = head.shape[1]
    vmem, whole = pl.BlockSpec(memory_space=pltpu.VMEM), pl.BlockSpec(memory_space=pl.ANY)
    first = acc is None
    logits = jax.ShapeDtypeStruct((n * tok, vocab), jnp.float32)
    operands = [starts, fine, *blocks, far(head)] + ([] if first else [far(acc)])
    specs = [pl.BlockSpec(memory_space=pltpu.SMEM)] + [whole] * (len(operands) - 1)
    tiles = len(column_tiles(vocab))
    scratch = [
        pltpu.VMEM((size, CORES, n * tok, feat), jnp.bfloat16),
        pltpu.VMEM((n * tok, CORES * feat), jnp.bfloat16),
        pltpu.VMEM((size, CORES * feat, vocab), jnp.bfloat16),
        pltpu.VMEM(logits.shape, jnp.float32),
        pltpu.VMEM(fine.shape, fine.dtype),
        pltpu.SemaphoreType.DMA((size, CORES * n)),
        pltpu.SemaphoreType.DMA((size, tiles)),
        pltpu.SemaphoreType.DMA((tiles + 1,)),
        pltpu.SemaphoreType.DMA,
    ]
    work = 2 * n * tok * CORES * feat * vocab * size
    return pl.pallas_call(
        functools.partial(group_kernel, n, n_t, place, size, first, last),
        out_shape=jax.ShapeDtypeStruct((n, n_t, 3, tok), jnp.float32) if last else pltpu.HBM(logits.shape, logits.dtype),
        in_specs=specs,
        out_specs=vmem if last else whole,
        scratch_shapes=scratch,
        compiler_params=pltpu.CompilerParams(vmem_limit_bytes=VMEM_LIMIT),
        cost_estimate=pl.CostEstimate(
            flops=work, bytes_accessed=2 * CORES * feat * vocab * size, transcendentals=0
        ),
    )(*operands)


def squares_kernel(hidden_ref, gain_ref, target_ref, out_ref, raw, gain, target, sems):
    pairs = ((hidden_ref, raw), (gain_ref, gain), (target_ref, target))
    copies = [pltpu.make_async_copy(a, b, sems.at[i]) for i, (a, b) in enumerate(pairs)]
    for copy in copies:
        copy.start()
    for copy in copies:
        copy.wait()
    tok, feat = raw.shape
    values = raw[...].astype(jnp.float32)
    sums = to_row(jnp.sum(values * values, axis=1, keepdims=True))
    peers = out_ref.shape[0]
    for peer in range(peers):
        out_ref[peer, :, :feat] = gain[...]
        out_ref[peer, :, feat : feat + tok] = sums
        out_ref[peer, :, feat + tok :] = target[...].astype(jnp.float32)


def squares(hidden, gain, targets, peers):
    tok, feat = hidden.shape
    return pl.pallas_call(
        squares_kernel,
        out_shape=jax.ShapeDtypeStruct((peers, 1, feat + 2 * tok), jnp.float32),
        in_specs=[pl.BlockSpec(memory_space=pltpu.HBM)] * 3,
        out_specs=pl.BlockSpec(memory_space=pltpu.VMEM),
        scratch_shapes=[
            pltpu.VMEM(hidden.shape, hidden.dtype),
            pltpu.VMEM(gain.shape, gain.dtype),
            pltpu.VMEM(targets.shape, targets.dtype),
            pltpu.SemaphoreType.DMA((3,)),
        ],
        compiler_params=pltpu.CompilerParams(vmem_limit_bytes=SMALL_LIMIT),
    )(far(hidden), far(gain), far(targets))


def body(hidden, norm_gain, head, targets, old_logprob, lengths):
    n_dp, n_t = lax.axis_size("dp"), lax.axis_size("tensor")
    grid = Grid(n_dp, n_t)
    depth = grid.depth
    tok, feat = hidden.shape
    plane, tensor = lax.axis_index("dp"), lax.axis_index("tensor")
    z_me, c_me = tensor // CORES, tensor % CORES
    owners = grid.owners(plane // grid.cols, plane % grid.cols, c_me)
    groups = [[0]] + [[d, depth - d] for d in range(1, (depth + 1) // 2)] + [[depth // 2]]
    place = [grid.sibling_spot(k) for k in range(n_dp)]

    layers = {0: hidden}
    reached = [grid.reach(hidden)]
    before = []
    for group in groups[1:]:
        for dz in group:
            layers[dz] = grid.along(after(hidden, *before), dz)
        before = list(reached[0].values()) if len(before) == 0 else [layers[dz] for dz in group]
    for group in groups[1:]:
        sources = [layers[dz] for dz in group]
        sources[0] = after(sources[0], *reached[-1].values())
        joined = jnp.concatenate(sources) if len(sources) > 1 else sources[0]
        reached.append(grid.reach(joined))

    packed = squares(hidden, norm_gain[None, :], targets[None, :], n_dp * n_t)
    fine = lax.all_to_all(packed, ("dp", "tensor"), 0, 0, tiled=True)

    vocab_cols = head.shape[1]
    vocab_start = lax.axis_index(("dp", "tensor")) * vocab_cols
    acc = None
    for at, group in enumerate(groups):
        final = at == len(groups) - 1
        middle = at and not final
        own = grid.sibling(reached[at][0, 0])
        held = [layers[dz] for dz in groups[at + 1]] + [own] if middle else []
        spread = grid.fill(dict(reached[at]), *([acc] if at == 1 else []), *held)
        following = list(reached[at + 1].values()) if middle else []
        others = [own] + [grid.sibling(after(a, *following)) for a in spread[1:-1]]
        others.append(grid.sibling(after(spread[-1], *([acc] if final else following))))
        blocks = spread + others
        if not at:
            blocks = [far(a) for a in blocks]
        starts = jnp.stack([(z_me - dz) % depth for dz in group] + [c_me, vocab_start] + owners)
        if middle:
            starts = after(starts, *following)
        acc = group_product(tok, n_t, starts, len(group), fine, blocks, place, head, acc, final)

    parts = lax.all_to_all(acc.reshape(n_dp * n_t, 3, tok), ("dp", "tensor"), 0, 0, tiled=True)
    top = jnp.max(parts[:, 0], axis=0)
    total = jnp.sum(parts[:, 1] * jnp.exp(parts[:, 0] - top[None, :]), axis=0)
    picked = jnp.sum(parts[:, 2], axis=0)

    seq_count = lengths.shape[0]
    position = jnp.arange(tok // seq_count, dtype=jnp.int32)
    live = (position[None, :] < lengths[:, None]).reshape(-1).astype(jnp.float32)
    logprob = picked - top - jnp.log(total)
    return (live * logprob, live * (logprob - old_logprob))


def solution(mesh):
    in_specs = (
        P("dp", "tensor"),
        P("tensor"),
        P(None, ("dp", "tensor")),
        P("dp"),
        P("dp"),
        P("dp"),
    )
    out_specs = (P("dp"), P("dp"))
    return jax.shard_map(body, mesh=mesh, in_specs=in_specs, out_specs=out_specs, check_vma=False)
```

```python
import functools

import jax
import jax.numpy as jnp
from jax import lax
from jax.experimental import pallas as pl
from jax.experimental.pallas import tpu as pltpu
from jax.sharding import PartitionSpec as P

D = 8192
CORES = 2
X_ONLY, Y_ONLY = (0, 1), (1, 0)
VMEM_LIMIT = 16 * 1024 * 1024
SMALL_LIMIT = 6 * 1024 * 1024


class Grid:
    def __init__(self, n_dp, n_t):
        self.n_t = n_t
        self.cols = 2
        self.rows = n_dp // self.cols
        self.depth = n_t // CORES
        self.square = self.rows == self.cols
        self.first = (X_ONLY, Y_ONLY) if self.square else (X_ONLY, X_ONLY)
        self.second = (Y_ONLY, X_ONLY) if self.square else (Y_ONLY, Y_ONLY)
        self.spots = [(j, i) for j in range(self.rows) for i in range(self.cols)]

    def permute(self, a, place):
        perm = []
        for y in range(self.rows):
            for x in range(self.cols):
                for z in range(self.depth):
                    for c in range(CORES):
                        src = (y * self.cols + x) * self.n_t + z * CORES + c
                        v, u, w, d = place(y, x, z, c)
                        dst = (v % self.rows * self.cols + u % self.cols) * self.n_t
                        perm.append((src, dst + w % self.depth * CORES + d % CORES))
        return lax.ppermute(a, ("dp", "tensor"), perm)

    def plane(self, a, ways, step):
        def place(y, x, z, c):
            return y + ways[c][0] * step, x + ways[c][1] * step, z, c

        return self.permute(a, place)

    def along(self, a, step):
        return self.permute(a, lambda y, x, z, c: (y, x, z + step, c))

    def sibling(self, a):
        return self.permute(a, lambda y, x, z, c: (y, x, z, c + 1))

    def reach(self, a):
        got = {(0, 0): a}
        for i in range(1, self.cols):
            got[0, i] = self.plane(a, self.first, i)
        for j in range(1, self.rows):
            got[j, 0] = self.plane(a, self.second, j)
        return got

    def fill(self, got, *late):
        late = (*late, *got.values())
        for j in range(1, self.rows):
            for i in range(1, self.cols):
                got[j, i] = self.plane(after(got[0, i], *late), self.second, j)
        return [got[s] for s in self.spots]

    def owners(self, y, x, c):
        ways = [(self.first[k], self.second[k]) for k in range(CORES)]
        out = []
        for j, i in self.spots:
            at = [
                (y - f[0] * i - s[0] * j) % self.rows * self.cols + (x - f[1] * i - s[1] * j) % self.cols
                for f, s in ways
            ]
            out.append(jnp.where(c == 0, at[0], at[1]))
        return out

    def sibling_spot(self, k):
        j, i = self.spots[k]
        return self.spots.index((i, j)) if self.square else k


def far(a):
    return pltpu.with_memory_space_constraint(a, pltpu.HBM)


def after(a, *others):
    return lax.optimization_barrier((a, *others))[0] if others else a


def diagonal(size):
    row = lax.broadcasted_iota(jnp.int32, (size, size), 0)
    return row == lax.broadcasted_iota(jnp.int32, (size, size), 1)


def to_column(row):
    return jnp.sum(jnp.where(diagonal(row.shape[1]), row, 0.0), axis=1, keepdims=True)


def to_row(column):
    return jnp.sum(jnp.where(diagonal(column.shape[0]), column, 0.0), axis=0, keepdims=True)


def load_kernel(offsets, start_ref, head_ref, out_ref, sems):
    size, deep = out_ref.shape[:2]
    copies = []
    for j in range(size):
        rows = pl.ds(pl.multiple_of(start_ref[offsets[j]] * deep, deep), deep)
        copies.append(pltpu.make_async_copy(head_ref.at[rows], out_ref.at[j], sems.at[j]))
        copies[-1].start()
    for copy in copies:
        copy.wait()


def loaded(starts, offsets, head, deep):
    return pl.pallas_call(
        functools.partial(load_kernel, offsets),
        out_shape=pltpu.VMEM((len(offsets), deep, head.shape[1]), head.dtype),
        in_specs=[pl.BlockSpec(memory_space=pltpu.SMEM), pl.BlockSpec(memory_space=pl.ANY)],
        out_specs=pl.BlockSpec(memory_space=pltpu.VMEM),
        scratch_shapes=[pltpu.SemaphoreType.DMA((len(offsets),))],
        compiler_params=pltpu.CompilerParams(vmem_limit_bytes=SMALL_LIMIT),
    )(starts, far(head))


def join_kernel(*refs):
    tok = refs[0].shape[0]
    for j, ref in enumerate(refs[:-1]):
        refs[-1][j * tok : (j + 1) * tok, :] = ref[...]


def joined(blocks):
    tok, feat = blocks[0].shape
    vmem = pl.BlockSpec(memory_space=pltpu.VMEM)
    return pl.pallas_call(
        join_kernel,
        out_shape=jax.ShapeDtypeStruct((len(blocks) * tok, feat), blocks[0].dtype),
        in_specs=[vmem] * len(blocks),
        out_specs=vmem,
        compiler_params=pltpu.CompilerParams(vmem_limit_bytes=SMALL_LIMIT),
    )(*blocks)


def group_kernel(n, n_t, place, offsets, first, last, *refs):
    refs = list(refs)
    start_ref, fine = refs.pop(0), refs.pop(0)
    blocks = [refs.pop(0) for _ in range(CORES * n)]
    weights = refs.pop(0)
    acc_ref = None if first else refs.pop(0)
    out_ref, rows = refs[:2]
    acc = refs[2] if last else out_ref
    feat = blocks[0].shape[1]
    tok = rows.shape[0] // n
    c_me, base = start_ref[0], start_ref[1]
    owners = [start_ref[2 + k] for k in range(n)]
    scales = []
    for k in range(n):
        sums = jnp.sum(fine[pl.ds(owners[k] * n_t, n_t), :, feat : feat + tok], axis=0)
        scales.append(to_column(lax.rsqrt(sums / D + 1e-06)))
    for j, offset in enumerate(offsets):
        for c in range(CORES):
            core = 1 - c_me if c else c_me
            gain = fine[start_ref[offset] * CORES + core, :, :feat]
            columns = pl.ds(pl.multiple_of(core * feat, feat), feat)
            for k in range(n):
                spot = place[k] if c else k
                part = blocks[c * n + k][j * tok : (j + 1) * tok, :].astype(jnp.float32)
                part = part * scales[spot] * gain
                rows[spot * tok : (spot + 1) * tok, columns] = part.astype(jnp.bfloat16)
        product = jnp.dot(rows[...], weights[j], preferred_element_type=jnp.float32)
        if j:
            acc[...] += product
        else:
            acc[...] = product if first else acc_ref[...] + product
    if not last:
        return
    for b in range(n):
        logits = acc[b * tok : (b + 1) * tok, :]
        top = jnp.max(logits, axis=1, keepdims=True)
        total = jnp.sum(jnp.exp(logits - top), axis=1, keepdims=True)
        entry = lax.broadcasted_iota(jnp.int32, logits.shape, 1) + base
        target = fine[owners[b] * n_t, :, feat + tok : feat + 2 * tok]
        target = to_column(target).astype(jnp.int32)
        pick = jnp.sum(jnp.where(entry == target, logits, 0.0), axis=1, keepdims=True)
        for peer in range(n_t):
            out_ref[owners[b], peer, 0:1, :] = to_row(top)
            out_ref[owners[b], peer, 1:2, :] = to_row(total)
            out_ref[owners[b], peer, 2:3, :] = to_row(pick)


def group_product(tok, n_t, starts, offsets, fine, blocks, place, weights, acc, last):
    n = len(place)
    feat = blocks[0].shape[1]
    size, deep, vocab = weights.shape
    vmem = pl.BlockSpec(memory_space=pltpu.VMEM)
    first = acc is None
    logits = jax.ShapeDtypeStruct((n * tok, vocab), jnp.float32)
    operands = [starts, fine, *blocks, weights] + ([] if first else [acc])
    scratch = [pltpu.VMEM((n * tok, deep), jnp.bfloat16)]
    if last:
        scratch.append(pltpu.VMEM(logits.shape, jnp.float32))
    return pl.pallas_call(
        functools.partial(group_kernel, n, n_t, place, offsets, first, last),
        out_shape=jax.ShapeDtypeStruct((n, n_t, 3, tok), jnp.float32) if last else logits,
        in_specs=[pl.BlockSpec(memory_space=pltpu.SMEM)] + [vmem] * (len(operands) - 1),
        out_specs=vmem,
        scratch_shapes=scratch,
        compiler_params=pltpu.CompilerParams(vmem_limit_bytes=VMEM_LIMIT),
        cost_estimate=pl.CostEstimate(
            flops=2 * n * tok * deep * vocab * size, bytes_accessed=2 * deep * vocab * size, transcendentals=0
        ),
    )(*operands)


def squares_kernel(hidden_ref, gain_ref, target_ref, out_ref, raw, gain, target, sems):
    pairs = ((hidden_ref, raw), (gain_ref, gain), (target_ref, target))
    copies = [pltpu.make_async_copy(a, b, sems.at[i]) for i, (a, b) in enumerate(pairs)]
    for copy in copies:
        copy.start()
    for copy in copies:
        copy.wait()
    tok, feat = raw.shape
    values = raw[...].astype(jnp.float32)
    sums = to_row(jnp.sum(values * values, axis=1, keepdims=True))
    peers = out_ref.shape[0]
    for peer in range(peers):
        out_ref[peer, :, :feat] = gain[...]
        out_ref[peer, :, feat : feat + tok] = sums
        out_ref[peer, :, feat + tok :] = target[...].astype(jnp.float32)


def squares(hidden, gain, targets, peers):
    tok, feat = hidden.shape
    return pl.pallas_call(
        squares_kernel,
        out_shape=jax.ShapeDtypeStruct((peers, 1, feat + 2 * tok), jnp.float32),
        in_specs=[pl.BlockSpec(memory_space=pltpu.HBM)] * 3,
        out_specs=pl.BlockSpec(memory_space=pltpu.VMEM),
        scratch_shapes=[
            pltpu.VMEM(hidden.shape, hidden.dtype),
            pltpu.VMEM(gain.shape, gain.dtype),
            pltpu.VMEM(targets.shape, targets.dtype),
            pltpu.SemaphoreType.DMA((3,)),
        ],
        compiler_params=pltpu.CompilerParams(vmem_limit_bytes=SMALL_LIMIT),
    )(far(hidden), far(gain), far(targets))


def body(hidden, norm_gain, head, targets, old_logprob, lengths):
    n_dp, n_t = lax.axis_size("dp"), lax.axis_size("tensor")
    grid = Grid(n_dp, n_t)
    depth = grid.depth
    tok, feat = hidden.shape
    plane, tensor = lax.axis_index("dp"), lax.axis_index("tensor")
    z_me, c_me = tensor // CORES, tensor % CORES
    owners = grid.owners(plane // grid.cols, plane % grid.cols, c_me)
    groups = [[0]] + [[d, depth - d] for d in range(1, (depth + 1) // 2)] + [[depth // 2]]
    place = [grid.sibling_spot(k) for k in range(n_dp)]

    layers = {0: hidden}
    reached = [grid.reach(hidden)]
    before = []
    for group in groups[1:]:
        for dz in group:
            layers[dz] = grid.along(after(hidden, *before), dz)
        before = list(reached[0].values()) if len(before) == 0 else [layers[dz] for dz in group]
    for group in groups[1:]:
        sources = [layers[dz] for dz in group]
        sources[0] = after(sources[0], *reached[-1].values())
        reached.append(grid.reach(joined(sources) if len(sources) > 1 else sources[0]))

    vocab_cols = head.shape[1]
    vocab_start = lax.axis_index(("dp", "tensor")) * vocab_cols
    starts = jnp.stack([c_me, vocab_start] + owners + [(z_me - dz) % depth for dz in range(depth)])
    packed = squares(after(hidden, starts), norm_gain[None, :], targets[None, :], n_dp * n_t)
    fine = lax.all_to_all(packed, ("dp", "tensor"), 0, 0, tiled=True)

    acc, deep = None, CORES * feat
    for at, group in enumerate(groups):
        final = at == len(groups) - 1
        middle = at and not final
        offsets = [2 + n_dp + dz for dz in group]
        own = grid.sibling(reached[at][0, 0])
        held = [layers[dz] for dz in groups[at + 1]] + [own] if middle else []
        spread = grid.fill(dict(reached[at]), *([acc] if at == 1 else []), *held)
        if at == 0:
            weights = [loaded(starts, offsets, after(head, packed), deep)]
        elif at == 1:
            for later in groups[1:]:
                ready = after(head, acc, *(layers[dz] for dz in groups[2]))
                weights.append(loaded(starts, [2 + n_dp + dz for dz in later], ready, deep))
        following = [*reached[at + 1].values(), *weights[1:3]] if middle else []
        others = [own] + [grid.sibling(after(a, *following)) for a in spread[1:-1]]
        others.append(grid.sibling(after(spread[-1], *([acc] if final else following))))
        blocks = spread + others
        acc = group_product(tok, n_t, starts, offsets, fine, blocks, place, weights[at], acc, final)

    parts = lax.all_to_all(acc.reshape(n_dp * n_t, 3, tok), ("dp", "tensor"), 0, 0, tiled=True)
    top = jnp.max(parts[:, 0], axis=0)
    total = jnp.sum(parts[:, 1] * jnp.exp(parts[:, 0] - top[None, :]), axis=0)
    picked = jnp.sum(parts[:, 2], axis=0)

    seq_count = lengths.shape[0]
    position = jnp.arange(tok // seq_count, dtype=jnp.int32)
    live = (position[None, :] < lengths[:, None]).reshape(-1).astype(jnp.float32)
    logprob = picked - top - jnp.log(total)
    return (live * logprob, live * (logprob - old_logprob))


def solution(mesh):
    in_specs = (
        P("dp", "tensor"),
        P("tensor"),
        P(None, ("dp", "tensor")),
        P("dp"),
        P("dp"),
        P("dp"),
    )
    out_specs = (P("dp"), P("dp"))
    return jax.shard_map(body, mesh=mesh, in_specs=in_specs, out_specs=out_specs, check_vma=False)
```

```python
import functools

import jax
import jax.numpy as jnp
from jax import lax
from jax.experimental import pallas as pl
from jax.experimental.pallas import tpu as pltpu
from jax.sharding import PartitionSpec as P

D = 8192
CORES = 2
X_ONLY, Y_ONLY = (0, 1), (1, 0)
VMEM_LIMIT = 16 * 1024 * 1024
SMALL_LIMIT = 6 * 1024 * 1024


class Grid:
    def __init__(self, n_dp, n_t):
        self.n_t = n_t
        self.cols = 2
        self.rows = n_dp // self.cols
        self.depth = n_t // CORES
        self.square = self.rows == self.cols
        self.first = (X_ONLY, Y_ONLY) if self.square else (X_ONLY, X_ONLY)
        self.second = (Y_ONLY, X_ONLY) if self.square else (Y_ONLY, Y_ONLY)
        self.spots = [(j, i) for j in range(self.rows) for i in range(self.cols)]

    def permute(self, a, place):
        perm = []
        for y in range(self.rows):
            for x in range(self.cols):
                for z in range(self.depth):
                    for c in range(CORES):
                        src = (y * self.cols + x) * self.n_t + z * CORES + c
                        v, u, w, d = place(y, x, z, c)
                        dst = (v % self.rows * self.cols + u % self.cols) * self.n_t
                        perm.append((src, dst + w % self.depth * CORES + d % CORES))
        return lax.ppermute(a, ("dp", "tensor"), perm)

    def plane(self, a, ways, step):
        def place(y, x, z, c):
            return y + ways[c][0] * step, x + ways[c][1] * step, z, c

        return self.permute(a, place)

    def along(self, a, step):
        return self.permute(a, lambda y, x, z, c: (y, x, z + step, c))

    def sibling(self, a):
        return self.permute(a, lambda y, x, z, c: (y, x, z, c + 1))

    def reach(self, a):
        got = {(0, 0): a}
        for i in range(1, self.cols):
            got[0, i] = self.plane(a, self.first, i)
        for j in range(1, self.rows):
            got[j, 0] = self.plane(a, self.second, j)
        return got

    def fill(self, got, *late):
        late = (*late, *got.values())
        for j in range(1, self.rows):
            for i in range(1, self.cols):
                got[j, i] = self.plane(after(got[0, i], *late), self.second, j)
        return [got[s] for s in self.spots]

    def owners(self, y, x, c):
        ways = [(self.first[k], self.second[k]) for k in range(CORES)]
        out = []
        for j, i in self.spots:
            at = [
                (y - f[0] * i - s[0] * j) % self.rows * self.cols + (x - f[1] * i - s[1] * j) % self.cols
                for f, s in ways
            ]
            out.append(jnp.where(c == 0, at[0], at[1]))
        return out

    def sibling_spot(self, k):
        j, i = self.spots[k]
        return self.spots.index((i, j)) if self.square else k


def far(a):
    return pltpu.with_memory_space_constraint(a, pltpu.HBM)


def after(a, *others):
    return lax.optimization_barrier((a, *others))[0] if others else a


def diagonal(size):
    row = lax.broadcasted_iota(jnp.int32, (size, size), 0)
    return row == lax.broadcasted_iota(jnp.int32, (size, size), 1)


def to_column(row):
    return jnp.sum(jnp.where(diagonal(row.shape[1]), row, 0.0), axis=1, keepdims=True)


def to_row(column):
    return jnp.sum(jnp.where(diagonal(column.shape[0]), column, 0.0), axis=0, keepdims=True)


def load_kernel(offsets, start_ref, head_ref, out_ref, sems):
    size, deep = out_ref.shape[:2]
    copies = []
    for j in range(size):
        rows = pl.ds(pl.multiple_of(start_ref[offsets[j]] * deep, deep), deep)
        copies.append(pltpu.make_async_copy(head_ref.at[rows], out_ref.at[j], sems.at[j]))
        copies[-1].start()
    for copy in copies:
        copy.wait()


def loaded(starts, offsets, head, deep):
    return pl.pallas_call(
        functools.partial(load_kernel, offsets),
        out_shape=pltpu.VMEM((len(offsets), deep, head.shape[1]), head.dtype),
        in_specs=[pl.BlockSpec(memory_space=pltpu.SMEM), pl.BlockSpec(memory_space=pl.ANY)],
        out_specs=pl.BlockSpec(memory_space=pltpu.VMEM),
        scratch_shapes=[pltpu.SemaphoreType.DMA((len(offsets),))],
        compiler_params=pltpu.CompilerParams(vmem_limit_bytes=SMALL_LIMIT),
        cost_estimate=pl.CostEstimate(flops=0, bytes_accessed=0, transcendentals=0),
    )(starts, far(head))


def join_kernel(*refs):
    tok = refs[0].shape[0]
    for j, ref in enumerate(refs[:-1]):
        refs[-1][j * tok : (j + 1) * tok, :] = ref[...]


def joined(blocks):
    tok, feat = blocks[0].shape
    vmem = pl.BlockSpec(memory_space=pltpu.VMEM)
    return pl.pallas_call(
        join_kernel,
        out_shape=jax.ShapeDtypeStruct((len(blocks) * tok, feat), blocks[0].dtype),
        in_specs=[vmem] * len(blocks),
        out_specs=vmem,
        compiler_params=pltpu.CompilerParams(vmem_limit_bytes=SMALL_LIMIT),
    )(*blocks)


def layer_kernel(n, n_t, place, layer, offset, first, last, *refs):
    refs = list(refs)
    start_ref, fine = refs.pop(0), refs.pop(0)
    blocks = [refs.pop(0) for _ in range(CORES * n)]
    weights = refs.pop(0)
    acc_ref = None if first else refs.pop(0)
    out_ref, rows = refs[:2]
    acc = refs[2] if last else out_ref
    feat = blocks[0].shape[1]
    tok = rows.shape[0] // n
    c_me, base = start_ref[0], start_ref[1]
    owners = [start_ref[2 + k] for k in range(n)]
    scales = []
    for k in range(n):
        sums = jnp.sum(fine[pl.ds(owners[k] * n_t, n_t), :, feat : feat + tok], axis=0)
        scales.append(to_column(lax.rsqrt(sums / D + 1e-06)))
    for c in range(CORES):
        core = 1 - c_me if c else c_me
        gain = fine[start_ref[offset] * CORES + core, :, :feat]
        columns = pl.ds(pl.multiple_of(core * feat, feat), feat)
        for k in range(n):
            spot = place[k] if c else k
            part = blocks[c * n + k][layer * tok : (layer + 1) * tok, :].astype(jnp.float32)
            part = part * scales[spot] * gain
            rows[spot * tok : (spot + 1) * tok, columns] = part.astype(jnp.bfloat16)
    product = jnp.dot(rows[...], weights[layer], preferred_element_type=jnp.float32)
    acc[...] = product if first else acc_ref[...] + product
    if not last:
        return
    for b in range(n):
        logits = acc[b * tok : (b + 1) * tok, :]
        top = jnp.max(logits, axis=1, keepdims=True)
        total = jnp.sum(jnp.exp(logits - top), axis=1, keepdims=True)
        entry = lax.broadcasted_iota(jnp.int32, logits.shape, 1) + base
        target = fine[owners[b] * n_t, :, feat + tok : feat + 2 * tok]
        target = to_column(target).astype(jnp.int32)
        pick = jnp.sum(jnp.where(entry == target, logits, 0.0), axis=1, keepdims=True)
        for peer in range(n_t):
            out_ref[owners[b], peer, 0:1, :] = to_row(top)
            out_ref[owners[b], peer, 1:2, :] = to_row(total)
            out_ref[owners[b], peer, 2:3, :] = to_row(pick)


def layer_product(tok, n_t, starts, layer, offset, fine, blocks, place, weights, acc, last):
    n = len(place)
    feat = blocks[0].shape[1]
    deep, vocab = weights.shape[1:]
    vmem = pl.BlockSpec(memory_space=pltpu.VMEM)
    first = acc is None
    logits = jax.ShapeDtypeStruct((n * tok, vocab), jnp.float32)
    operands = [starts, fine, *blocks, weights] + ([] if first else [acc])
    scratch = [pltpu.VMEM((n * tok, deep), jnp.bfloat16)]
    if last:
        scratch.append(pltpu.VMEM(logits.shape, jnp.float32))
    return pl.pallas_call(
        functools.partial(layer_kernel, n, n_t, place, layer, offset, first, last),
        out_shape=jax.ShapeDtypeStruct((n, n_t, 3, tok), jnp.float32) if last else logits,
        in_specs=[pl.BlockSpec(memory_space=pltpu.SMEM)] + [vmem] * (len(operands) - 1),
        out_specs=vmem,
        scratch_shapes=scratch,
        compiler_params=pltpu.CompilerParams(vmem_limit_bytes=VMEM_LIMIT),
        cost_estimate=pl.CostEstimate(
            flops=0, bytes_accessed=0, transcendentals=0
        ),
    )(*operands)


def squares_kernel(hidden_ref, gain_ref, target_ref, out_ref, raw, gain, target, sems):
    pairs = ((hidden_ref, raw), (gain_ref, gain), (target_ref, target))
    copies = [pltpu.make_async_copy(a, b, sems.at[i]) for i, (a, b) in enumerate(pairs)]
    for copy in copies:
        copy.start()
    for copy in copies:
        copy.wait()
    tok, feat = raw.shape
    values = raw[...].astype(jnp.float32)
    sums = to_row(jnp.sum(values * values, axis=1, keepdims=True))
    peers = out_ref.shape[0]
    for peer in range(peers):
        out_ref[peer, :, :feat] = gain[...]
        out_ref[peer, :, feat : feat + tok] = sums
        out_ref[peer, :, feat + tok :] = target[...].astype(jnp.float32)


def squares(hidden, gain, targets, peers):
    tok, feat = hidden.shape
    return pl.pallas_call(
        squares_kernel,
        out_shape=jax.ShapeDtypeStruct((peers, 1, feat + 2 * tok), jnp.float32),
        in_specs=[pl.BlockSpec(memory_space=pltpu.HBM)] * 3,
        out_specs=pl.BlockSpec(memory_space=pltpu.VMEM),
        scratch_shapes=[
            pltpu.VMEM(hidden.shape, hidden.dtype),
            pltpu.VMEM(gain.shape, gain.dtype),
            pltpu.VMEM(targets.shape, targets.dtype),
            pltpu.SemaphoreType.DMA((3,)),
        ],
        compiler_params=pltpu.CompilerParams(vmem_limit_bytes=SMALL_LIMIT),
    )(far(hidden), far(gain), far(targets))


def body(hidden, norm_gain, head, targets, old_logprob, lengths):
    n_dp, n_t = lax.axis_size("dp"), lax.axis_size("tensor")
    grid = Grid(n_dp, n_t)
    depth = grid.depth
    tok, feat = hidden.shape
    plane, tensor = lax.axis_index("dp"), lax.axis_index("tensor")
    z_me, c_me = tensor // CORES, tensor % CORES
    owners = grid.owners(plane // grid.cols, plane % grid.cols, c_me)
    groups = [[0]] + [[d, depth - d] for d in range(1, (depth + 1) // 2)] + [[depth // 2]]
    place = [grid.sibling_spot(k) for k in range(n_dp)]

    layers = {0: hidden}
    reached = [grid.reach(hidden)]
    before = []
    for group in groups[1:]:
        for dz in group:
            layers[dz] = grid.along(after(hidden, *before), dz)
        before = list(reached[0].values()) if len(before) == 0 else [layers[dz] for dz in group]
    vocab_cols = head.shape[1]
    vocab_start = lax.axis_index(("dp", "tensor")) * vocab_cols
    starts = jnp.stack([c_me, vocab_start] + owners + [(z_me - dz) % depth for dz in range(depth)])
    packed = squares(after(hidden, starts), norm_gain[None, :], targets[None, :], n_dp * n_t)
    fine = lax.all_to_all(packed, ("dp", "tensor"), 0, 0, tiled=True)
    for group in groups[1:]:
        sources = [layers[dz] for dz in group]
        sources[0] = after(sources[0], packed, *reached[-1].values())
        reached.append(grid.reach(joined(sources) if len(sources) > 1 else sources[0]))

    acc, deep = None, CORES * feat
    for at, group in enumerate(groups):
        final = at == len(groups) - 1
        middle = at and not final
        offsets = [2 + n_dp + dz for dz in group]
        own = grid.sibling(reached[at][0, 0])
        held = [layers[dz] for dz in groups[at + 1]] + [own] if middle else []
        spread = grid.fill(dict(reached[at]), *([acc] if at == 1 else []), *held)
        if at == 0:
            weights = [loaded(starts, offsets, after(head, fine), deep)]
        elif at == 1:
            for later in groups[1:]:
                ready = after(head, acc, *(layers[dz] for dz in groups[2]))
                weights.append(loaded(starts, [2 + n_dp + dz for dz in later], ready, deep))
        ready = weights[1:3] if middle else []
        others = [own] + [grid.sibling(after(a, *ready)) for a in spread[1:-1]]
        others.append(grid.sibling(after(spread[-1], *([acc] if final else ready))))
        blocks = spread + others
        for layer, offset in enumerate(offsets):
            done = layer == len(offsets) - 1
            if middle and done:
                blocks[0] = after(blocks[0], *reached[at + 1].values())
            last = final and done
            acc = layer_product(tok, n_t, starts, layer, offset, fine, blocks, place, weights[at], acc, last)

    parts = lax.all_to_all(acc.reshape(n_dp * n_t, 3, tok), ("dp", "tensor"), 0, 0, tiled=True)
    top = jnp.max(parts[:, 0], axis=0)
    total = jnp.sum(parts[:, 1] * jnp.exp(parts[:, 0] - top[None, :]), axis=0)
    picked = jnp.sum(parts[:, 2], axis=0)

    seq_count = lengths.shape[0]
    position = jnp.arange(tok // seq_count, dtype=jnp.int32)
    live = (position[None, :] < lengths[:, None]).reshape(-1).astype(jnp.float32)
    logprob = picked - top - jnp.log(total)
    return (live * logprob, live * (logprob - old_logprob))


def solution(mesh):
    in_specs = (
        P("dp", "tensor"),
        P("tensor"),
        P(None, ("dp", "tensor")),
        P("dp"),
        P("dp"),
        P("dp"),
    )
    out_specs = (P("dp"), P("dp"))
    return jax.shard_map(body, mesh=mesh, in_specs=in_specs, out_specs=out_specs, check_vma=False)
```

```python
import functools

import jax
import jax.numpy as jnp
from jax import lax
from jax.experimental import pallas as pl
from jax.experimental.pallas import tpu as pltpu
from jax.sharding import PartitionSpec as P

D = 8192
CORES = 2
X_ONLY, Y_ONLY = (0, 1), (1, 0)
VMEM_LIMIT = 16 * 1024 * 1024
SMALL_LIMIT = 6 * 1024 * 1024


class Grid:
    def __init__(self, n_dp, n_t):
        self.n_t = n_t
        self.cols = 2
        self.rows = n_dp // self.cols
        self.depth = n_t // CORES
        self.square = self.rows == self.cols
        self.first = (X_ONLY, Y_ONLY) if self.square else (X_ONLY, X_ONLY)
        self.second = (Y_ONLY, X_ONLY) if self.square else (Y_ONLY, Y_ONLY)
        self.spots = [(j, i) for j in range(self.rows) for i in range(self.cols)]

    def permute(self, a, place):
        perm = []
        for y in range(self.rows):
            for x in range(self.cols):
                for z in range(self.depth):
                    for c in range(CORES):
                        src = (y * self.cols + x) * self.n_t + z * CORES + c
                        v, u, w, d = place(y, x, z, c)
                        dst = (v % self.rows * self.cols + u % self.cols) * self.n_t
                        perm.append((src, dst + w % self.depth * CORES + d % CORES))
        return lax.ppermute(a, ("dp", "tensor"), perm)

    def plane(self, a, ways, step):
        def place(y, x, z, c):
            return y + ways[c][0] * step, x + ways[c][1] * step, z, c

        return self.permute(a, place)

    def along(self, a, step):
        return self.permute(a, lambda y, x, z, c: (y, x, z + step, c))

    def sibling(self, a):
        return self.permute(a, lambda y, x, z, c: (y, x, z, c + 1))

    def reach(self, a):
        got = {(0, 0): a}
        for i in range(1, self.cols):
            got[0, i] = self.plane(a, self.first, i)
        for j in range(1, self.rows):
            got[j, 0] = self.plane(a, self.second, j)
        return got

    def fill(self, got, *late):
        late = (*late, *got.values())
        for j in range(1, self.rows):
            for i in range(1, self.cols):
                got[j, i] = self.plane(after(got[0, i], *late), self.second, j)
        return [got[s] for s in self.spots]

    def owners(self, y, x, c):
        ways = [(self.first[k], self.second[k]) for k in range(CORES)]
        out = []
        for j, i in self.spots:
            at = [
                (y - f[0] * i - s[0] * j) % self.rows * self.cols + (x - f[1] * i - s[1] * j) % self.cols
                for f, s in ways
            ]
            out.append(jnp.where(c == 0, at[0], at[1]))
        return out

    def sibling_spot(self, k):
        j, i = self.spots[k]
        return self.spots.index((i, j)) if self.square else k


def far(a):
    return pltpu.with_memory_space_constraint(a, pltpu.HBM)


def after(a, *others):
    return lax.optimization_barrier((a, *others))[0] if others else a


def diagonal(size):
    row = lax.broadcasted_iota(jnp.int32, (size, size), 0)
    return row == lax.broadcasted_iota(jnp.int32, (size, size), 1)


def to_column(row):
    return jnp.sum(jnp.where(diagonal(row.shape[1]), row, 0.0), axis=1, keepdims=True)


def to_row(column):
    return jnp.sum(jnp.where(diagonal(column.shape[0]), column, 0.0), axis=0, keepdims=True)


def load_kernel(offsets, start_ref, head_ref, out_ref, sems):
    size, deep = out_ref.shape[:2]
    copies = []
    for j in range(size):
        rows = pl.ds(pl.multiple_of(start_ref[offsets[j]] * deep, deep), deep)
        copies.append(pltpu.make_async_copy(head_ref.at[rows], out_ref.at[j], sems.at[j]))
        copies[-1].start()
    for copy in copies:
        copy.wait()


def loaded(starts, offsets, head, deep):
    return pl.pallas_call(
        functools.partial(load_kernel, offsets),
        out_shape=pltpu.VMEM((len(offsets), deep, head.shape[1]), head.dtype),
        in_specs=[pl.BlockSpec(memory_space=pltpu.SMEM), pl.BlockSpec(memory_space=pl.ANY)],
        out_specs=pl.BlockSpec(memory_space=pltpu.VMEM),
        scratch_shapes=[pltpu.SemaphoreType.DMA((len(offsets),))],
        compiler_params=pltpu.CompilerParams(vmem_limit_bytes=SMALL_LIMIT),
    )(starts, far(head))


def join_kernel(*refs):
    tok = refs[0].shape[0]
    for j, ref in enumerate(refs[:-1]):
        refs[-1][j * tok : (j + 1) * tok, :] = ref[...]


def joined(blocks):
    tok, feat = blocks[0].shape
    vmem = pl.BlockSpec(memory_space=pltpu.VMEM)
    return pl.pallas_call(
        join_kernel,
        out_shape=jax.ShapeDtypeStruct((len(blocks) * tok, feat), blocks[0].dtype),
        in_specs=[vmem] * len(blocks),
        out_specs=vmem,
        compiler_params=pltpu.CompilerParams(vmem_limit_bytes=SMALL_LIMIT),
    )(*blocks)


def layer_kernel(n, n_t, place, layer, offset, own, first, last, *refs):
    refs = list(refs)
    start_ref, fine = refs.pop(0), refs.pop(0)
    blocks = [refs.pop(0) for _ in range(CORES * n)]
    weights = refs.pop(0)
    acc_ref = None if first else refs.pop(0)
    out_ref, rows = refs.pop(0), refs.pop(0)
    acc = refs.pop(0) if last else out_ref
    feat = blocks[0].shape[1]
    tok = rows.shape[0] // n
    if own:
        deep = rows.shape[1]
        source = weights.at[pl.ds(pl.multiple_of(start_ref[offset] * deep, deep), deep)]
        copy = pltpu.make_async_copy(source, refs[0].at[layer], refs[1])
        copy.start()
        weights = refs[0]
    c_me, base = start_ref[0], start_ref[1]
    owners = [start_ref[2 + k] for k in range(n)]
    scales = []
    for k in range(n):
        sums = jnp.sum(fine[pl.ds(owners[k] * n_t, n_t), :, feat : feat + tok], axis=0)
        scales.append(to_column(lax.rsqrt(sums / D + 1e-06)))
    for c in range(CORES):
        core = 1 - c_me if c else c_me
        gain = fine[start_ref[offset] * CORES + core, :, :feat]
        columns = pl.ds(pl.multiple_of(core * feat, feat), feat)
        for k in range(n):
            spot = place[k] if c else k
            part = blocks[c * n + k][layer * tok : (layer + 1) * tok, :].astype(jnp.float32)
            part = part * scales[spot] * gain
            rows[spot * tok : (spot + 1) * tok, columns] = part.astype(jnp.bfloat16)
    if own:
        copy.wait()
    product = jnp.dot(rows[...], weights[layer], preferred_element_type=jnp.float32)
    acc[...] = product if first else acc_ref[...] + product
    if not last:
        return
    for b in range(n):
        logits = acc[b * tok : (b + 1) * tok, :]
        top = jnp.max(logits, axis=1, keepdims=True)
        total = jnp.sum(jnp.exp(logits - top), axis=1, keepdims=True)
        entry = lax.broadcasted_iota(jnp.int32, logits.shape, 1) + base
        target = fine[owners[b] * n_t, :, feat + tok : feat + 2 * tok]
        target = to_column(target).astype(jnp.int32)
        pick = jnp.sum(jnp.where(entry == target, logits, 0.0), axis=1, keepdims=True)
        for peer in range(n_t):
            out_ref[owners[b], peer, 0:1, :] = to_row(top)
            out_ref[owners[b], peer, 1:2, :] = to_row(total)
            out_ref[owners[b], peer, 2:3, :] = to_row(pick)


def layer_product(tok, n_t, starts, layer, offset, fine, blocks, place, weights, acc, last):
    n = len(place)
    feat = blocks[0].shape[1]
    own = weights.ndim == 2
    deep, vocab = CORES * feat, weights.shape[-1]
    vmem = pl.BlockSpec(memory_space=pltpu.VMEM)
    first = acc is None
    logits = jax.ShapeDtypeStruct((n * tok, vocab), jnp.float32)
    operands = [starts, fine, *blocks, far(weights) if own else weights] + ([] if first else [acc])
    specs = [pl.BlockSpec(memory_space=pltpu.SMEM)] + [vmem] * (len(operands) - 1)
    scratch = [pltpu.VMEM((n * tok, deep), jnp.bfloat16)]
    if last:
        scratch.append(pltpu.VMEM(logits.shape, jnp.float32))
    if own:
        specs[2 + len(blocks)] = pl.BlockSpec(memory_space=pl.ANY)
        scratch += [pltpu.VMEM((1, deep, vocab), weights.dtype), pltpu.SemaphoreType.DMA]
    return pl.pallas_call(
        functools.partial(layer_kernel, n, n_t, place, layer, offset, own, first, last),
        out_shape=jax.ShapeDtypeStruct((n, n_t, 3, tok), jnp.float32) if last else logits,
        in_specs=specs,
        out_specs=vmem,
        scratch_shapes=scratch,
        compiler_params=pltpu.CompilerParams(vmem_limit_bytes=VMEM_LIMIT),
        cost_estimate=pl.CostEstimate(
            flops=2 * n * tok * deep * vocab, bytes_accessed=2 * deep * vocab, transcendentals=0
        ),
    )(*operands)


def squares_kernel(hidden_ref, gain_ref, target_ref, out_ref, raw, gain, target, sems):
    pairs = ((hidden_ref, raw), (gain_ref, gain), (target_ref, target))
    copies = [pltpu.make_async_copy(a, b, sems.at[i]) for i, (a, b) in enumerate(pairs)]
    for copy in copies:
        copy.start()
    for copy in copies:
        copy.wait()
    tok, feat = raw.shape
    values = raw[...].astype(jnp.float32)
    sums = to_row(jnp.sum(values * values, axis=1, keepdims=True))
    peers = out_ref.shape[0]
    for peer in range(peers):
        out_ref[peer, :, :feat] = gain[...]
        out_ref[peer, :, feat : feat + tok] = sums
        out_ref[peer, :, feat + tok :] = target[...].astype(jnp.float32)


def squares(hidden, gain, targets, peers):
    tok, feat = hidden.shape
    return pl.pallas_call(
        squares_kernel,
        out_shape=jax.ShapeDtypeStruct((peers, 1, feat + 2 * tok), jnp.float32),
        in_specs=[pl.BlockSpec(memory_space=pltpu.HBM)] * 3,
        out_specs=pl.BlockSpec(memory_space=pltpu.VMEM),
        scratch_shapes=[
            pltpu.VMEM(hidden.shape, hidden.dtype),
            pltpu.VMEM(gain.shape, gain.dtype),
            pltpu.VMEM(targets.shape, targets.dtype),
            pltpu.SemaphoreType.DMA((3,)),
        ],
        compiler_params=pltpu.CompilerParams(vmem_limit_bytes=SMALL_LIMIT),
    )(far(hidden), far(gain), far(targets))


def body(hidden, norm_gain, head, targets, old_logprob, lengths):
    n_dp, n_t = lax.axis_size("dp"), lax.axis_size("tensor")
    grid = Grid(n_dp, n_t)
    depth = grid.depth
    tok, feat = hidden.shape
    plane, tensor = lax.axis_index("dp"), lax.axis_index("tensor")
    z_me, c_me = tensor // CORES, tensor % CORES
    owners = grid.owners(plane // grid.cols, plane % grid.cols, c_me)
    groups = [[0]] + [[d, depth - d] for d in range(1, (depth + 1) // 2)] + [[depth // 2]]
    place = [grid.sibling_spot(k) for k in range(n_dp)]

    layers = {0: hidden}
    reached = [grid.reach(hidden)]
    before = []
    for group in groups[1:]:
        for dz in group:
            layers[dz] = grid.along(after(hidden, *before), dz)
        before = list(reached[0].values()) if len(before) == 0 else [layers[dz] for dz in group]
    for group in groups[1:]:
        sources = [layers[dz] for dz in group]
        sources[0] = after(sources[0], *reached[-1].values())
        reached.append(grid.reach(joined(sources) if len(sources) > 1 else sources[0]))

    vocab_cols = head.shape[1]
    vocab_start = lax.axis_index(("dp", "tensor")) * vocab_cols
    starts = jnp.stack([c_me, vocab_start] + owners + [(z_me - dz) % depth for dz in range(depth)])
    packed = squares(after(hidden, starts), norm_gain[None, :], targets[None, :], n_dp * n_t)
    fine = lax.all_to_all(packed, ("dp", "tensor"), 0, 0, tiled=True)

    acc, deep = None, CORES * feat
    for at, group in enumerate(groups):
        final = at == len(groups) - 1
        middle = at and not final
        offsets = [2 + n_dp + dz for dz in group]
        own = grid.sibling(reached[at][0, 0])
        held = [layers[dz] for dz in groups[at + 1]] + [own] if middle else []
        spread = grid.fill(dict(reached[at]), *([acc] if at == 1 else []), *held)
        if at == 0:
            weights = [head]
        elif at == 1:
            for later in groups[1:]:
                ready = after(head, acc, *(layers[dz] for dz in groups[2]))
                weights.append(loaded(starts, [2 + n_dp + dz for dz in later], ready, deep))
        following = [*reached[at + 1].values(), *weights[1:3]] if middle else []
        others = [own] + [grid.sibling(after(a, *following)) for a in spread[1:-1]]
        others.append(grid.sibling(after(spread[-1], *([acc] if final else following))))
        blocks = spread + others
        for layer, offset in enumerate(offsets):
            done = layer == len(offsets) - 1
            if middle and done:
                blocks[0] = after(blocks[0], *reached[at + 1].values())
            last = final and done
            acc = layer_product(tok, n_t, starts, layer, offset, fine, blocks, place, weights[at], acc, last)

    parts = lax.all_to_all(acc.reshape(n_dp * n_t, 3, tok), ("dp", "tensor"), 0, 0, tiled=True)
    top = jnp.max(parts[:, 0], axis=0)
    total = jnp.sum(parts[:, 1] * jnp.exp(parts[:, 0] - top[None, :]), axis=0)
    picked = jnp.sum(parts[:, 2], axis=0)

    seq_count = lengths.shape[0]
    position = jnp.arange(tok // seq_count, dtype=jnp.int32)
    live = (position[None, :] < lengths[:, None]).reshape(-1).astype(jnp.float32)
    logprob = picked - top - jnp.log(total)
    return (live * logprob, live * (logprob - old_logprob))


def solution(mesh):
    in_specs = (
        P("dp", "tensor"),
        P("tensor"),
        P(None, ("dp", "tensor")),
        P("dp"),
        P("dp"),
        P("dp"),
    )
    out_specs = (P("dp"), P("dp"))
    return jax.shard_map(body, mesh=mesh, in_specs=in_specs, out_specs=out_specs, check_vma=False)
```

```python
import functools

import jax
import jax.numpy as jnp
from jax import lax
from jax.experimental import pallas as pl
from jax.experimental.pallas import tpu as pltpu
from jax.sharding import PartitionSpec as P

D = 8192
CORES = 2
X_ONLY, Y_ONLY = (0, 1), (1, 0)
VMEM_LIMIT = 16 * 1024 * 1024
SMALL_LIMIT = 6 * 1024 * 1024


class Grid:
    def __init__(self, n_dp, n_t):
        self.n_t = n_t
        self.cols = 2
        self.rows = n_dp // self.cols
        self.depth = n_t // CORES
        self.square = self.rows == self.cols
        self.first = (X_ONLY, Y_ONLY) if self.square else (X_ONLY, X_ONLY)
        self.second = (Y_ONLY, X_ONLY) if self.square else (Y_ONLY, Y_ONLY)
        self.spots = [(j, i) for j in range(self.rows) for i in range(self.cols)]

    def permute(self, a, place):
        perm = []
        for y in range(self.rows):
            for x in range(self.cols):
                for z in range(self.depth):
                    for c in range(CORES):
                        src = (y * self.cols + x) * self.n_t + z * CORES + c
                        v, u, w, d = place(y, x, z, c)
                        dst = (v % self.rows * self.cols + u % self.cols) * self.n_t
                        perm.append((src, dst + w % self.depth * CORES + d % CORES))
        return lax.ppermute(a, ("dp", "tensor"), perm)

    def plane(self, a, ways, step):
        def place(y, x, z, c):
            return y + ways[c][0] * step, x + ways[c][1] * step, z, c

        return self.permute(a, place)

    def along(self, a, step):
        return self.permute(a, lambda y, x, z, c: (y, x, z + step, c))

    def sibling(self, a):
        return self.permute(a, lambda y, x, z, c: (y, x, z, c + 1))

    def reach(self, a):
        got = {(0, 0): a}
        for i in range(1, self.cols):
            got[0, i] = self.plane(a, self.first, i)
        for j in range(1, self.rows):
            got[j, 0] = self.plane(a, self.second, j)
        return got

    def fill(self, got, *late):
        late = (*late, *got.values())
        for j in range(1, self.rows):
            for i in range(1, self.cols):
                got[j, i] = self.plane(after(got[0, i], *late), self.second, j)
        return [got[s] for s in self.spots]

    def owners(self, y, x, c):
        ways = [(self.first[k], self.second[k]) for k in range(CORES)]
        out = []
        for j, i in self.spots:
            at = [
                (y - f[0] * i - s[0] * j) % self.rows * self.cols + (x - f[1] * i - s[1] * j) % self.cols
                for f, s in ways
            ]
            out.append(jnp.where(c == 0, at[0], at[1]))
        return out

    def sibling_spot(self, k):
        j, i = self.spots[k]
        return self.spots.index((i, j)) if self.square else k


def far(a):
    return pltpu.with_memory_space_constraint(a, pltpu.HBM)


def after(a, *others):
    return lax.optimization_barrier((a, *others))[0] if others else a


def diagonal(size):
    row = lax.broadcasted_iota(jnp.int32, (size, size), 0)
    return row == lax.broadcasted_iota(jnp.int32, (size, size), 1)


def to_column(row):
    return jnp.sum(jnp.where(diagonal(row.shape[1]), row, 0.0), axis=1, keepdims=True)


def to_row(column):
    return jnp.sum(jnp.where(diagonal(column.shape[0]), column, 0.0), axis=0, keepdims=True)


def load_kernel(offsets, start_ref, head_ref, out_ref, sems):
    size, deep = out_ref.shape[:2]
    copies = []
    for j in range(size):
        rows = pl.ds(pl.multiple_of(start_ref[offsets[j]] * deep, deep), deep)
        copies.append(pltpu.make_async_copy(head_ref.at[rows], out_ref.at[j], sems.at[j]))
        copies[-1].start()
    for copy in copies:
        copy.wait()


def loaded(starts, offsets, head, deep):
    return pl.pallas_call(
        functools.partial(load_kernel, offsets),
        out_shape=pltpu.VMEM((len(offsets), deep, head.shape[1]), head.dtype),
        in_specs=[pl.BlockSpec(memory_space=pltpu.SMEM), pl.BlockSpec(memory_space=pl.ANY)],
        out_specs=pl.BlockSpec(memory_space=pltpu.VMEM),
        scratch_shapes=[pltpu.SemaphoreType.DMA((len(offsets),))],
        compiler_params=pltpu.CompilerParams(vmem_limit_bytes=SMALL_LIMIT),
    )(starts, far(head))


def join_kernel(*refs):
    tok = refs[0].shape[0]
    for j, ref in enumerate(refs[:-1]):
        refs[-1][j * tok : (j + 1) * tok, :] = ref[...]


def joined(blocks):
    tok, feat = blocks[0].shape
    vmem = pl.BlockSpec(memory_space=pltpu.VMEM)
    return pl.pallas_call(
        join_kernel,
        out_shape=jax.ShapeDtypeStruct((len(blocks) * tok, feat), blocks[0].dtype),
        in_specs=[vmem] * len(blocks),
        out_specs=vmem,
        compiler_params=pltpu.CompilerParams(vmem_limit_bytes=SMALL_LIMIT),
    )(*blocks)


def layer_kernel(n, n_t, place, layer, offset, own, first, last, *refs):
    refs = list(refs)
    start_ref, fine = refs.pop(0), refs.pop(0)
    blocks = [refs.pop(0) for _ in range(CORES * n)]
    weights = refs.pop(0)
    acc_ref = None if first else refs.pop(0)
    out_ref, rows = refs.pop(0), refs.pop(0)
    acc = refs.pop(0) if last else out_ref
    feat = blocks[0].shape[1]
    tok = rows.shape[0] // n
    if own:
        deep = rows.shape[1]
        source = weights.at[pl.ds(pl.multiple_of(start_ref[offset] * deep, deep), deep)]
        copy = pltpu.make_async_copy(source, refs[0].at[layer], refs[1])
        copy.start()
        weights = refs[0]
    c_me, base = start_ref[0], start_ref[1]
    owners = [start_ref[2 + k] for k in range(n)]
    scales = []
    for k in range(n):
        sums = jnp.sum(fine[pl.ds(owners[k] * n_t, n_t), :, feat : feat + tok], axis=0)
        scales.append(to_column(lax.rsqrt(sums / D + 1e-06)))
    for c in range(CORES):
        core = 1 - c_me if c else c_me
        gain = fine[start_ref[offset] * CORES + core, :, :feat]
        columns = pl.ds(pl.multiple_of(core * feat, feat), feat)
        for k in range(n):
            spot = place[k] if c else k
            part = blocks[c * n + k][layer * tok : (layer + 1) * tok, :].astype(jnp.float32)
            part = part * scales[spot] * gain
            rows[spot * tok : (spot + 1) * tok, columns] = part.astype(jnp.bfloat16)
    if own:
        copy.wait()
    product = jnp.dot(rows[...], weights[layer], preferred_element_type=jnp.float32)
    acc[...] = product if first else acc_ref[...] + product
    if not last:
        return
    for b in range(n):
        logits = acc[b * tok : (b + 1) * tok, :]
        top = jnp.max(logits, axis=1, keepdims=True)
        total = jnp.sum(jnp.exp(logits - top), axis=1, keepdims=True)
        entry = lax.broadcasted_iota(jnp.int32, logits.shape, 1) + base
        target = fine[owners[b] * n_t, :, feat + tok : feat + 2 * tok]
        target = to_column(target).astype(jnp.int32)
        pick = jnp.sum(jnp.where(entry == target, logits, 0.0), axis=1, keepdims=True)
        for peer in range(n_t):
            out_ref[owners[b], peer, 0:1, :] = to_row(top)
            out_ref[owners[b], peer, 1:2, :] = to_row(total)
            out_ref[owners[b], peer, 2:3, :] = to_row(pick)


def layer_product(tok, n_t, starts, layer, offset, fine, blocks, place, weights, acc, last):
    n = len(place)
    feat = blocks[0].shape[1]
    own = weights.ndim == 2
    deep, vocab = CORES * feat, weights.shape[-1]
    vmem = pl.BlockSpec(memory_space=pltpu.VMEM)
    first = acc is None
    logits = jax.ShapeDtypeStruct((n * tok, vocab), jnp.float32)
    operands = [starts, fine, *blocks, far(weights) if own else weights] + ([] if first else [acc])
    specs = [pl.BlockSpec(memory_space=pltpu.SMEM)] + [vmem] * (len(operands) - 1)
    scratch = [pltpu.VMEM((n * tok, deep), jnp.bfloat16)]
    if last:
        scratch.append(pltpu.VMEM(logits.shape, jnp.float32))
    if own:
        specs[2 + len(blocks)] = pl.BlockSpec(memory_space=pl.ANY)
        scratch += [pltpu.VMEM((1, deep, vocab), weights.dtype), pltpu.SemaphoreType.DMA]
    return pl.pallas_call(
        functools.partial(layer_kernel, n, n_t, place, layer, offset, own, first, last),
        out_shape=jax.ShapeDtypeStruct((n, n_t, 3, tok), jnp.float32) if last else logits,
        in_specs=specs,
        out_specs=vmem,
        scratch_shapes=scratch,
        compiler_params=pltpu.CompilerParams(vmem_limit_bytes=VMEM_LIMIT),
        cost_estimate=pl.CostEstimate(
            flops=2 * n * tok * deep * vocab, bytes_accessed=2 * deep * vocab, transcendentals=0
        ),
    )(*operands)


def squares_kernel(hidden_ref, gain_ref, target_ref, out_ref, raw, gain, target, sems):
    pairs = ((hidden_ref, raw), (gain_ref, gain), (target_ref, target))
    copies = [pltpu.make_async_copy(a, b, sems.at[i]) for i, (a, b) in enumerate(pairs)]
    for copy in copies:
        copy.start()
    for copy in copies:
        copy.wait()
    tok, feat = raw.shape
    values = raw[...].astype(jnp.float32)
    sums = to_row(jnp.sum(values * values, axis=1, keepdims=True))
    peers = out_ref.shape[0]
    for peer in range(peers):
        out_ref[peer, :, :feat] = gain[...]
        out_ref[peer, :, feat : feat + tok] = sums
        out_ref[peer, :, feat + tok :] = target[...].astype(jnp.float32)


def squares(hidden, gain, targets, peers):
    tok, feat = hidden.shape
    return pl.pallas_call(
        squares_kernel,
        out_shape=jax.ShapeDtypeStruct((peers, 1, feat + 2 * tok), jnp.float32),
        in_specs=[pl.BlockSpec(memory_space=pltpu.HBM)] * 3,
        out_specs=pl.BlockSpec(memory_space=pltpu.VMEM),
        scratch_shapes=[
            pltpu.VMEM(hidden.shape, hidden.dtype),
            pltpu.VMEM(gain.shape, gain.dtype),
            pltpu.VMEM(targets.shape, targets.dtype),
            pltpu.SemaphoreType.DMA((3,)),
        ],
        compiler_params=pltpu.CompilerParams(vmem_limit_bytes=SMALL_LIMIT),
    )(far(hidden), far(gain), far(targets))


def body(hidden, norm_gain, head, targets, old_logprob, lengths):
    n_dp, n_t = lax.axis_size("dp"), lax.axis_size("tensor")
    grid = Grid(n_dp, n_t)
    depth = grid.depth
    tok, feat = hidden.shape
    plane, tensor = lax.axis_index("dp"), lax.axis_index("tensor")
    z_me, c_me = tensor // CORES, tensor % CORES
    owners = grid.owners(plane // grid.cols, plane % grid.cols, c_me)
    rest = [depth - 1, *range(2, depth - 1)]
    groups = [[0], [1]] + [rest[k : k + 2] for k in range(0, len(rest), 2)]
    place = [grid.sibling_spot(k) for k in range(n_dp)]

    layers = {0: hidden}
    reached = [grid.reach(hidden)]
    for at, group in enumerate(groups[1:], 1):
        for dz in group:
            before = [layers[d] for d in groups[at - 1]] if at > 1 else []
            layers[dz] = grid.along(after(hidden, *before), dz)
    for group in groups[1:]:
        sources = [layers[dz] for dz in group]
        sources[0] = after(sources[0], *reached[0].values())
        reached.append(grid.reach(joined(sources) if len(sources) > 1 else sources[0]))

    vocab_cols = head.shape[1]
    vocab_start = lax.axis_index(("dp", "tensor")) * vocab_cols
    starts = jnp.stack([c_me, vocab_start] + owners + [(z_me - dz) % depth for dz in range(depth)])
    packed = squares(after(hidden, starts), norm_gain[None, :], targets[None, :], n_dp * n_t)
    fine = lax.all_to_all(packed, ("dp", "tensor"), 0, 0, tiled=True)

    acc, deep, results = None, CORES * feat, []
    for at, group in enumerate(groups):
        final = at == len(groups) - 1
        offsets = [2 + n_dp + dz for dz in group]
        spread = grid.fill(dict(reached[at]), *(results[at - 2 : at - 1] if at >= 2 else []))
        weights, ready = head, []
        if len(group) > 1:
            weights = loaded(starts, offsets, after(head, *results[-1:]), deep)
            ready = [weights]
        others = [grid.sibling(a) for a in spread[:-1]] + [grid.sibling(after(spread[-1], *ready))]
        blocks = spread + others
        for layer, offset in enumerate(offsets):
            last = final and layer == len(offsets) - 1
            acc = layer_product(tok, n_t, starts, layer, offset, fine, blocks, place, weights, acc, last)
        results.append(acc)

    parts = lax.all_to_all(acc.reshape(n_dp * n_t, 3, tok), ("dp", "tensor"), 0, 0, tiled=True)
    top = jnp.max(parts[:, 0], axis=0)
    total = jnp.sum(parts[:, 1] * jnp.exp(parts[:, 0] - top[None, :]), axis=0)
    picked = jnp.sum(parts[:, 2], axis=0)

    seq_count = lengths.shape[0]
    position = jnp.arange(tok // seq_count, dtype=jnp.int32)
    live = (position[None, :] < lengths[:, None]).reshape(-1).astype(jnp.float32)
    logprob = picked - top - jnp.log(total)
    return (live * logprob, live * (logprob - old_logprob))


def solution(mesh):
    in_specs = (
        P("dp", "tensor"),
        P("tensor"),
        P(None, ("dp", "tensor")),
        P("dp"),
        P("dp"),
        P("dp"),
    )
    out_specs = (P("dp"), P("dp"))
    return jax.shard_map(body, mesh=mesh, in_specs=in_specs, out_specs=out_specs, check_vma=False)
```

```python
import functools

import jax
import jax.numpy as jnp
from jax import lax
from jax.experimental import pallas as pl
from jax.experimental.pallas import tpu as pltpu
from jax.sharding import PartitionSpec as P

D = 8192
CORES = 2
X_ONLY, Y_ONLY = (0, 1), (1, 0)
VMEM_LIMIT = 16 * 1024 * 1024
SMALL_LIMIT = 6 * 1024 * 1024


class Grid:
    def __init__(self, n_dp, n_t):
        self.n_t = n_t
        self.cols = 2
        self.rows = n_dp // self.cols
        self.depth = n_t // CORES
        self.square = self.rows == self.cols
        self.first = (X_ONLY, Y_ONLY) if self.square else (X_ONLY, X_ONLY)
        self.second = (Y_ONLY, X_ONLY) if self.square else (Y_ONLY, Y_ONLY)
        self.spots = [(j, i) for j in range(self.rows) for i in range(self.cols)]

    def permute(self, a, place):
        perm = []
        for y in range(self.rows):
            for x in range(self.cols):
                for z in range(self.depth):
                    for c in range(CORES):
                        src = (y * self.cols + x) * self.n_t + z * CORES + c
                        v, u, w, d = place(y, x, z, c)
                        dst = (v % self.rows * self.cols + u % self.cols) * self.n_t
                        perm.append((src, dst + w % self.depth * CORES + d % CORES))
        return lax.ppermute(a, ("dp", "tensor"), perm)

    def plane(self, a, ways, step):
        def place(y, x, z, c):
            return y + ways[c][0] * step, x + ways[c][1] * step, z, c

        return self.permute(a, place)

    def along(self, a, step):
        return self.permute(a, lambda y, x, z, c: (y, x, z + step, c))

    def sibling(self, a):
        return self.permute(a, lambda y, x, z, c: (y, x, z, c + 1))

    def reach(self, a):
        got = {(0, 0): a}
        for i in range(1, self.cols):
            got[0, i] = self.plane(a, self.first, i)
        for j in range(1, self.rows):
            got[j, 0] = self.plane(a, self.second, j)
        return got

    def fill(self, got, *late):
        late = (*late, *got.values())
        for j in range(1, self.rows):
            for i in range(1, self.cols):
                got[j, i] = self.plane(after(got[0, i], *late), self.second, j)
        return [got[s] for s in self.spots]

    def owners(self, y, x, c):
        ways = [(self.first[k], self.second[k]) for k in range(CORES)]
        out = []
        for j, i in self.spots:
            at = [
                (y - f[0] * i - s[0] * j) % self.rows * self.cols + (x - f[1] * i - s[1] * j) % self.cols
                for f, s in ways
            ]
            out.append(jnp.where(c == 0, at[0], at[1]))
        return out

    def sibling_spot(self, k):
        j, i = self.spots[k]
        return self.spots.index((i, j)) if self.square else k


def far(a):
    return pltpu.with_memory_space_constraint(a, pltpu.HBM)


def after(a, *others):
    return lax.optimization_barrier((a, *others))[0] if others else a


def diagonal(size):
    row = lax.broadcasted_iota(jnp.int32, (size, size), 0)
    return row == lax.broadcasted_iota(jnp.int32, (size, size), 1)


def to_column(row):
    return jnp.sum(jnp.where(diagonal(row.shape[1]), row, 0.0), axis=1, keepdims=True)


def to_row(column):
    return jnp.sum(jnp.where(diagonal(column.shape[0]), column, 0.0), axis=0, keepdims=True)


def load_kernel(offsets, start_ref, head_ref, out_ref, sems):
    size, deep = out_ref.shape[:2]
    copies = []
    for j in range(size):
        rows = pl.ds(pl.multiple_of(start_ref[offsets[j]] * deep, deep), deep)
        copies.append(pltpu.make_async_copy(head_ref.at[rows], out_ref.at[j], sems.at[j]))
        copies[-1].start()
    for copy in copies:
        copy.wait()


def loaded(starts, offsets, head, deep):
    return pl.pallas_call(
        functools.partial(load_kernel, offsets),
        out_shape=pltpu.VMEM((len(offsets), deep, head.shape[1]), head.dtype),
        in_specs=[pl.BlockSpec(memory_space=pltpu.SMEM), pl.BlockSpec(memory_space=pl.ANY)],
        out_specs=pl.BlockSpec(memory_space=pltpu.VMEM),
        scratch_shapes=[pltpu.SemaphoreType.DMA((len(offsets),))],
        compiler_params=pltpu.CompilerParams(vmem_limit_bytes=SMALL_LIMIT),
    )(starts, far(head))


def join_kernel(*refs):
    tok = refs[0].shape[0]
    for j, ref in enumerate(refs[:-1]):
        refs[-1][j * tok : (j + 1) * tok, :] = ref[...]


def joined(blocks):
    tok, feat = blocks[0].shape
    vmem = pl.BlockSpec(memory_space=pltpu.VMEM)
    return pl.pallas_call(
        join_kernel,
        out_shape=jax.ShapeDtypeStruct((len(blocks) * tok, feat), blocks[0].dtype),
        in_specs=[vmem] * len(blocks),
        out_specs=vmem,
        compiler_params=pltpu.CompilerParams(vmem_limit_bytes=SMALL_LIMIT),
    )(*blocks)


def layer_kernel(n, n_t, place, layer, offset, own, first, last, *refs):
    refs = list(refs)
    start_ref, fine = refs.pop(0), refs.pop(0)
    blocks = [refs.pop(0) for _ in range(CORES * n)]
    weights = refs.pop(0)
    acc_ref = None if first else refs.pop(0)
    out_ref, rows = refs.pop(0), refs.pop(0)
    acc = refs.pop(0) if last else out_ref
    feat = blocks[0].shape[1]
    tok = rows.shape[0] // n
    if own:
        deep = rows.shape[1]
        source = weights.at[pl.ds(pl.multiple_of(start_ref[offset] * deep, deep), deep)]
        copy = pltpu.make_async_copy(source, refs[0].at[layer], refs[1])
        copy.start()
        weights = refs[0]
    c_me, base = start_ref[0], start_ref[1]
    owners = [start_ref[2 + k] for k in range(n)]
    scales = []
    for k in range(n):
        sums = jnp.sum(fine[pl.ds(owners[k] * n_t, n_t), :, feat : feat + tok], axis=0)
        scales.append(to_column(lax.rsqrt(sums / D + 1e-06)))
    for c in range(CORES):
        core = 1 - c_me if c else c_me
        gain = fine[start_ref[offset] * CORES + core, :, :feat]
        columns = pl.ds(pl.multiple_of(core * feat, feat), feat)
        for k in range(n):
            spot = place[k] if c else k
            part = blocks[c * n + k][layer * tok : (layer + 1) * tok, :].astype(jnp.float32)
            part = part * scales[spot] * gain
            rows[spot * tok : (spot + 1) * tok, columns] = part.astype(jnp.bfloat16)
    if own:
        copy.wait()
    product = jnp.dot(rows[...], weights[layer], preferred_element_type=jnp.float32)
    acc[...] = product if first else acc_ref[...] + product
    if not last:
        return
    for b in range(n):
        logits = acc[b * tok : (b + 1) * tok, :]
        top = jnp.max(logits, axis=1, keepdims=True)
        total = jnp.sum(jnp.exp(logits - top), axis=1, keepdims=True)
        entry = lax.broadcasted_iota(jnp.int32, logits.shape, 1) + base
        target = fine[owners[b] * n_t, :, feat + tok : feat + 2 * tok]
        target = to_column(target).astype(jnp.int32)
        pick = jnp.sum(jnp.where(entry == target, logits, 0.0), axis=1, keepdims=True)
        for peer in range(n_t):
            out_ref[owners[b], peer, 0:1, :] = to_row(top)
            out_ref[owners[b], peer, 1:2, :] = to_row(total)
            out_ref[owners[b], peer, 2:3, :] = to_row(pick)


def layer_product(tok, n_t, starts, layer, offset, fine, blocks, place, weights, acc, last):
    n = len(place)
    feat = blocks[0].shape[1]
    own = weights.ndim == 2
    deep, vocab = CORES * feat, weights.shape[-1]
    vmem = pl.BlockSpec(memory_space=pltpu.VMEM)
    first = acc is None
    logits = jax.ShapeDtypeStruct((n * tok, vocab), jnp.float32)
    operands = [starts, fine, *blocks, far(weights) if own else weights] + ([] if first else [acc])
    specs = [pl.BlockSpec(memory_space=pltpu.SMEM)] + [vmem] * (len(operands) - 1)
    scratch = [pltpu.VMEM((n * tok, deep), jnp.bfloat16)]
    if last:
        scratch.append(pltpu.VMEM(logits.shape, jnp.float32))
    if own:
        specs[2 + len(blocks)] = pl.BlockSpec(memory_space=pl.ANY)
        scratch += [pltpu.VMEM((1, deep, vocab), weights.dtype), pltpu.SemaphoreType.DMA]
    return pl.pallas_call(
        functools.partial(layer_kernel, n, n_t, place, layer, offset, own, first, last),
        out_shape=jax.ShapeDtypeStruct((n, n_t, 3, tok), jnp.float32) if last else logits,
        in_specs=specs,
        out_specs=vmem,
        scratch_shapes=scratch,
        compiler_params=pltpu.CompilerParams(vmem_limit_bytes=VMEM_LIMIT),
        cost_estimate=pl.CostEstimate(
            flops=2 * n * tok * deep * vocab, bytes_accessed=2 * deep * vocab, transcendentals=0
        ),
    )(*operands)


def squares_kernel(hidden_ref, gain_ref, target_ref, out_ref, raw, gain, target, sems):
    pairs = ((hidden_ref, raw), (gain_ref, gain), (target_ref, target))
    copies = [pltpu.make_async_copy(a, b, sems.at[i]) for i, (a, b) in enumerate(pairs)]
    for copy in copies:
        copy.start()
    for copy in copies:
        copy.wait()
    tok, feat = raw.shape
    values = raw[...].astype(jnp.float32)
    sums = to_row(jnp.sum(values * values, axis=1, keepdims=True))
    peers = out_ref.shape[0]
    for peer in range(peers):
        out_ref[peer, :, :feat] = gain[...]
        out_ref[peer, :, feat : feat + tok] = sums
        out_ref[peer, :, feat + tok :] = target[...].astype(jnp.float32)


def squares(hidden, gain, targets, peers):
    tok, feat = hidden.shape
    return pl.pallas_call(
        squares_kernel,
        out_shape=jax.ShapeDtypeStruct((peers, 1, feat + 2 * tok), jnp.float32),
        in_specs=[pl.BlockSpec(memory_space=pltpu.HBM)] * 3,
        out_specs=pl.BlockSpec(memory_space=pltpu.VMEM),
        scratch_shapes=[
            pltpu.VMEM(hidden.shape, hidden.dtype),
            pltpu.VMEM(gain.shape, gain.dtype),
            pltpu.VMEM(targets.shape, targets.dtype),
            pltpu.SemaphoreType.DMA((3,)),
        ],
        compiler_params=pltpu.CompilerParams(vmem_limit_bytes=SMALL_LIMIT),
    )(far(hidden), far(gain), far(targets))


def body(hidden, norm_gain, head, targets, old_logprob, lengths):
    n_dp, n_t = lax.axis_size("dp"), lax.axis_size("tensor")
    grid = Grid(n_dp, n_t)
    depth = grid.depth
    tok, feat = hidden.shape
    plane, tensor = lax.axis_index("dp"), lax.axis_index("tensor")
    z_me, c_me = tensor // CORES, tensor % CORES
    owners = grid.owners(plane // grid.cols, plane % grid.cols, c_me)
    groups = [[0]] + [[d, depth - d] for d in range(1, (depth + 1) // 2)] + [[depth // 2]]
    place = [grid.sibling_spot(k) for k in range(n_dp)]

    layers = {0: hidden}
    reached = [grid.reach(hidden)]
    for at, group in enumerate(groups[1:], 1):
        for dz in group:
            step = 1 if dz <= depth // 2 else -1
            layers[dz] = grid.along(layers[dz - step], step) if at > 1 else grid.along(hidden, dz)

    def reach_next(at, *late):
        if at < len(groups):
            sources = [layers[dz] for dz in groups[at]]
            sources[0] = after(sources[0], *late)
            reached.append(grid.reach(joined(sources) if len(sources) > 1 else sources[0]))

    reach_next(1, *reached[0].values())
    vocab_cols = head.shape[1]
    vocab_start = lax.axis_index(("dp", "tensor")) * vocab_cols
    starts = jnp.stack([c_me, vocab_start] + owners + [(z_me - dz) % depth for dz in range(depth)])
    packed = squares(after(hidden, starts), norm_gain[None, :], targets[None, :], n_dp * n_t)
    fine = lax.all_to_all(packed, ("dp", "tensor"), 0, 0, tiled=True)

    acc, deep, half = None, CORES * feat, []
    for at, group in enumerate(groups):
        final = at == len(groups) - 1
        middle = at and not final
        offsets = [2 + n_dp + dz for dz in group]
        own = grid.sibling(reached[at][0, 0])
        held = [acc, own, *(layers[dz] for dz in groups[2])] if at == 1 else half
        spread = grid.fill(dict(reached[at]), *held)
        if at:
            reach_next(at + 1, spread[-1])
        if at == 0:
            weights = [head]
        elif at == 1:
            for later in groups[1:]:
                ready = after(head, acc, *(layers[dz] for dz in groups[2]))
                weights.append(loaded(starts, [2 + n_dp + dz for dz in later], ready, deep))
        others = [own] + [grid.sibling(a) for a in spread[1:-1]]
        others.append(grid.sibling(after(spread[-1], *([acc] if final else weights[1:3] if middle else []))))
        blocks = spread + others
        for layer, offset in enumerate(offsets):
            done = layer == len(offsets) - 1
            if middle and done:
                half = [acc]
                blocks[0] = after(blocks[0], *reached[at + 1].values())
            last = final and done
            acc = layer_product(tok, n_t, starts, layer, offset, fine, blocks, place, weights[at], acc, last)

    parts = lax.all_to_all(acc.reshape(n_dp * n_t, 3, tok), ("dp", "tensor"), 0, 0, tiled=True)
    top = jnp.max(parts[:, 0], axis=0)
    total = jnp.sum(parts[:, 1] * jnp.exp(parts[:, 0] - top[None, :]), axis=0)
    picked = jnp.sum(parts[:, 2], axis=0)

    seq_count = lengths.shape[0]
    position = jnp.arange(tok // seq_count, dtype=jnp.int32)
    live = (position[None, :] < lengths[:, None]).reshape(-1).astype(jnp.float32)
    logprob = picked - top - jnp.log(total)
    return (live * logprob, live * (logprob - old_logprob))


def solution(mesh):
    in_specs = (
        P("dp", "tensor"),
        P("tensor"),
        P(None, ("dp", "tensor")),
        P("dp"),
        P("dp"),
        P("dp"),
    )
    out_specs = (P("dp"), P("dp"))
    return jax.shard_map(body, mesh=mesh, in_specs=in_specs, out_specs=out_specs, check_vma=False)
```

```python
import functools

import jax
import jax.numpy as jnp
from jax import lax
from jax.experimental import pallas as pl
from jax.experimental.pallas import tpu as pltpu
from jax.sharding import PartitionSpec as P

D = 8192
CORES = 2
X_ONLY, Y_ONLY = (0, 1), (1, 0)
VMEM_LIMIT = 16 * 1024 * 1024
SMALL_LIMIT = 6 * 1024 * 1024


class Grid:
    def __init__(self, n_dp, n_t):
        self.n_t = n_t
        self.cols = 2
        self.rows = n_dp // self.cols
        self.depth = n_t // CORES
        self.square = self.rows == self.cols
        self.first = (X_ONLY, Y_ONLY) if self.square else (X_ONLY, X_ONLY)
        self.second = (Y_ONLY, X_ONLY) if self.square else (Y_ONLY, Y_ONLY)
        self.spots = [(j, i) for j in range(self.rows) for i in range(self.cols)]

    def permute(self, a, place):
        perm = []
        for y in range(self.rows):
            for x in range(self.cols):
                for z in range(self.depth):
                    for c in range(CORES):
                        src = (y * self.cols + x) * self.n_t + z * CORES + c
                        v, u, w, d = place(y, x, z, c)
                        dst = (v % self.rows * self.cols + u % self.cols) * self.n_t
                        perm.append((src, dst + w % self.depth * CORES + d % CORES))
        return lax.ppermute(a, ("dp", "tensor"), perm)

    def plane(self, a, ways, step):
        def place(y, x, z, c):
            return y + ways[c][0] * step, x + ways[c][1] * step, z, c

        return self.permute(a, place)

    def along(self, a, step):
        return self.permute(a, lambda y, x, z, c: (y, x, z + step, c))

    def sibling(self, a):
        return self.permute(a, lambda y, x, z, c: (y, x, z, c + 1))

    def reach(self, a):
        got = {(0, 0): a}
        for i in range(1, self.cols):
            got[0, i] = self.plane(a, self.first, i)
        for j in range(1, self.rows):
            got[j, 0] = self.plane(a, self.second, j)
        return got

    def fill(self, got, *late):
        late = (*late, *got.values())
        for j in range(1, self.rows):
            for i in range(1, self.cols):
                got[j, i] = self.plane(after(got[0, i], *late), self.second, j)
        return [got[s] for s in self.spots]

    def owners(self, y, x, c):
        ways = [(self.first[k], self.second[k]) for k in range(CORES)]
        out = []
        for j, i in self.spots:
            at = [
                (y - f[0] * i - s[0] * j) % self.rows * self.cols + (x - f[1] * i - s[1] * j) % self.cols
                for f, s in ways
            ]
            out.append(jnp.where(c == 0, at[0], at[1]))
        return out

    def sibling_spot(self, k):
        j, i = self.spots[k]
        return self.spots.index((i, j)) if self.square else k


def far(a):
    return pltpu.with_memory_space_constraint(a, pltpu.HBM)


def after(a, *others):
    return lax.optimization_barrier((a, *others))[0] if others else a


def diagonal(size):
    row = lax.broadcasted_iota(jnp.int32, (size, size), 0)
    return row == lax.broadcasted_iota(jnp.int32, (size, size), 1)


def to_column(row):
    return jnp.sum(jnp.where(diagonal(row.shape[1]), row, 0.0), axis=1, keepdims=True)


def to_row(column):
    return jnp.sum(jnp.where(diagonal(column.shape[0]), column, 0.0), axis=0, keepdims=True)


def load_kernel(offsets, start_ref, head_ref, out_ref, sems):
    size, deep = out_ref.shape[:2]
    copies = []
    for j in range(size):
        rows = pl.ds(pl.multiple_of(start_ref[offsets[j]] * deep, deep), deep)
        copies.append(pltpu.make_async_copy(head_ref.at[rows], out_ref.at[j], sems.at[j]))
        copies[-1].start()
    for copy in copies:
        copy.wait()


def loaded(starts, offsets, head, deep):
    return pl.pallas_call(
        functools.partial(load_kernel, offsets),
        out_shape=pltpu.VMEM((len(offsets), deep, head.shape[1]), head.dtype),
        in_specs=[pl.BlockSpec(memory_space=pltpu.SMEM), pl.BlockSpec(memory_space=pl.ANY)],
        out_specs=pl.BlockSpec(memory_space=pltpu.VMEM),
        scratch_shapes=[pltpu.SemaphoreType.DMA((len(offsets),))],
        compiler_params=pltpu.CompilerParams(vmem_limit_bytes=SMALL_LIMIT),
    )(starts, far(head))


def join_kernel(*refs):
    tok = refs[0].shape[0]
    for j, ref in enumerate(refs[:-1]):
        refs[-1][j * tok : (j + 1) * tok, :] = ref[...]


def joined(blocks):
    tok, feat = blocks[0].shape
    vmem = pl.BlockSpec(memory_space=pltpu.VMEM)
    return pl.pallas_call(
        join_kernel,
        out_shape=jax.ShapeDtypeStruct((len(blocks) * tok, feat), blocks[0].dtype),
        in_specs=[vmem] * len(blocks),
        out_specs=vmem,
        compiler_params=pltpu.CompilerParams(vmem_limit_bytes=SMALL_LIMIT),
    )(*blocks)


def layer_kernel(n, n_t, place, layer, offset, own, first, last, *refs):
    refs = list(refs)
    start_ref, fine = refs.pop(0), refs.pop(0)
    blocks = [refs.pop(0) for _ in range(CORES * n)]
    weights = refs.pop(0)
    acc_ref = None if first else refs.pop(0)
    out_ref, rows = refs.pop(0), refs.pop(0)
    acc = refs.pop(0) if last else out_ref
    feat = blocks[0].shape[1]
    tok = rows.shape[0] // n
    if own:
        deep = rows.shape[1]
        source = weights.at[pl.ds(pl.multiple_of(start_ref[offset] * deep, deep), deep)]
        copy = pltpu.make_async_copy(source, refs[0].at[layer], refs[1])
        copy.start()
        weights = refs[0]
    c_me, base = start_ref[0], start_ref[1]
    owners = [start_ref[2 + k] for k in range(n)]
    scales = []
    for k in range(n):
        sums = jnp.sum(fine[pl.ds(owners[k] * n_t, n_t), :, feat : feat + tok], axis=0)
        scales.append(to_column(lax.rsqrt(sums / D + 1e-06)))
    for c in range(CORES):
        core = 1 - c_me if c else c_me
        gain = fine[start_ref[offset] * CORES + core, :, :feat]
        columns = pl.ds(pl.multiple_of(core * feat, feat), feat)
        for k in range(n):
            spot = place[k] if c else k
            part = blocks[c * n + k][layer * tok : (layer + 1) * tok, :].astype(jnp.float32)
            part = part * scales[spot] * gain
            rows[spot * tok : (spot + 1) * tok, columns] = part.astype(jnp.bfloat16)
    if own:
        copy.wait()
    product = jnp.dot(rows[...], weights[layer], preferred_element_type=jnp.float32)
    acc[...] = product if first else acc_ref[...] + product
    if not last:
        return
    for b in range(n):
        logits = acc[b * tok : (b + 1) * tok, :]
        top = jnp.max(logits, axis=1, keepdims=True)
        total = jnp.sum(jnp.exp(logits - top), axis=1, keepdims=True)
        entry = lax.broadcasted_iota(jnp.int32, logits.shape, 1) + base
        target = fine[owners[b] * n_t, :, feat + tok : feat + 2 * tok]
        target = to_column(target).astype(jnp.int32)
        pick = jnp.sum(jnp.where(entry == target, logits, 0.0), axis=1, keepdims=True)
        for peer in range(n_t):
            out_ref[owners[b], peer, 0:1, :] = to_row(top)
            out_ref[owners[b], peer, 1:2, :] = to_row(total)
            out_ref[owners[b], peer, 2:3, :] = to_row(pick)


def layer_product(tok, n_t, starts, layer, offset, fine, blocks, place, weights, acc, last):
    n = len(place)
    feat = blocks[0].shape[1]
    own = weights.ndim == 2
    deep, vocab = CORES * feat, weights.shape[-1]
    vmem = pl.BlockSpec(memory_space=pltpu.VMEM)
    first = acc is None
    logits = jax.ShapeDtypeStruct((n * tok, vocab), jnp.float32)
    operands = [starts, fine, *blocks, far(weights) if own else weights] + ([] if first else [acc])
    specs = [pl.BlockSpec(memory_space=pltpu.SMEM)] + [vmem] * (len(operands) - 1)
    scratch = [pltpu.VMEM((n * tok, deep), jnp.bfloat16)]
    if last:
        scratch.append(pltpu.VMEM(logits.shape, jnp.float32))
    if own:
        specs[2 + len(blocks)] = pl.BlockSpec(memory_space=pl.ANY)
        scratch += [pltpu.VMEM((1, deep, vocab), weights.dtype), pltpu.SemaphoreType.DMA]
    return pl.pallas_call(
        functools.partial(layer_kernel, n, n_t, place, layer, offset, own, first, last),
        out_shape=jax.ShapeDtypeStruct((n, n_t, 3, tok), jnp.float32) if last else logits,
        in_specs=specs,
        out_specs=vmem,
        scratch_shapes=scratch,
        compiler_params=pltpu.CompilerParams(vmem_limit_bytes=VMEM_LIMIT),
        cost_estimate=pl.CostEstimate(
            flops=2 * n * tok * deep * vocab, bytes_accessed=2 * deep * vocab, transcendentals=0
        ),
    )(*operands)


def squares_kernel(hidden_ref, gain_ref, target_ref, out_ref, raw, gain, target, sems):
    pairs = ((hidden_ref, raw), (gain_ref, gain), (target_ref, target))
    copies = [pltpu.make_async_copy(a, b, sems.at[i]) for i, (a, b) in enumerate(pairs)]
    for copy in copies:
        copy.start()
    for copy in copies:
        copy.wait()
    tok, feat = raw.shape
    values = raw[...].astype(jnp.float32)
    sums = to_row(jnp.sum(values * values, axis=1, keepdims=True))
    peers = out_ref.shape[0]
    for peer in range(peers):
        out_ref[peer, :, :feat] = gain[...]
        out_ref[peer, :, feat : feat + tok] = sums
        out_ref[peer, :, feat + tok :] = target[...].astype(jnp.float32)


def squares(hidden, gain, targets, peers):
    tok, feat = hidden.shape
    return pl.pallas_call(
        squares_kernel,
        out_shape=jax.ShapeDtypeStruct((peers, 1, feat + 2 * tok), jnp.float32),
        in_specs=[pl.BlockSpec(memory_space=pltpu.HBM)] * 3,
        out_specs=pl.BlockSpec(memory_space=pltpu.VMEM),
        scratch_shapes=[
            pltpu.VMEM(hidden.shape, hidden.dtype),
            pltpu.VMEM(gain.shape, gain.dtype),
            pltpu.VMEM(targets.shape, targets.dtype),
            pltpu.SemaphoreType.DMA((3,)),
        ],
        compiler_params=pltpu.CompilerParams(vmem_limit_bytes=SMALL_LIMIT),
    )(far(hidden), far(gain), far(targets))


def body(hidden, norm_gain, head, targets, old_logprob, lengths):
    n_dp, n_t = lax.axis_size("dp"), lax.axis_size("tensor")
    grid = Grid(n_dp, n_t)
    depth = grid.depth
    tok, feat = hidden.shape
    plane, tensor = lax.axis_index("dp"), lax.axis_index("tensor")
    z_me, c_me = tensor // CORES, tensor % CORES
    owners = grid.owners(plane // grid.cols, plane % grid.cols, c_me)
    groups = [[0]] + [[d, depth - d] for d in range(1, (depth + 1) // 2)] + [[depth // 2]]
    place = [grid.sibling_spot(k) for k in range(n_dp)]

    layers = {0: hidden}
    reached = [grid.reach(hidden)]
    for at, group in enumerate(groups[1:], 1):
        for dz in group:
            step = 1 if dz <= depth // 2 else -1
            layers[dz] = grid.along(layers[dz - step], step) if at > 1 else grid.along(hidden, dz)

    def reach_next(at, *late):
        if at < len(groups):
            sources = [layers[dz] for dz in groups[at]]
            sources[0] = after(sources[0], *late)
            reached.append(grid.reach(joined(sources) if len(sources) > 1 else sources[0]))

    reach_next(1, *reached[0].values())
    vocab_cols = head.shape[1]
    vocab_start = lax.axis_index(("dp", "tensor")) * vocab_cols
    starts = jnp.stack([c_me, vocab_start] + owners + [(z_me - dz) % depth for dz in range(depth)])
    packed = squares(after(hidden, starts), norm_gain[None, :], targets[None, :], n_dp * n_t)
    fine = lax.all_to_all(packed, ("dp", "tensor"), 0, 0, tiled=True)

    acc, deep, half = None, CORES * feat, []
    for at, group in enumerate(groups):
        final = at == len(groups) - 1
        middle = at and not final
        offsets = [2 + n_dp + dz for dz in group]
        own = grid.sibling(reached[at][0, 0])
        held = [acc, own, *(layers[dz] for dz in groups[2])] if at == 1 else half if at else [packed]
        spread = grid.fill(dict(reached[at]), *held)
        if at == 0:
            weights = [head]
        elif at == 1:
            for later in groups[1:]:
                ready = after(head, acc, *(layers[dz] for dz in groups[2]))
                weights.append(loaded(starts, [2 + n_dp + dz for dz in later], ready, deep))
        if at:
            reach_next(at + 1, weights[1] if at == 1 else spread[-1])
        others = [own] + [grid.sibling(a) for a in spread[1:-1]]
        others.append(grid.sibling(after(spread[-1], *([acc] if final else weights[1:3] if middle else []))))
        blocks = spread + others
        for layer, offset in enumerate(offsets):
            done = layer == len(offsets) - 1
            if middle and done:
                half = [acc]
                blocks[0] = after(blocks[0], *reached[at + 1].values())
            last = final and done
            acc = layer_product(tok, n_t, starts, layer, offset, fine, blocks, place, weights[at], acc, last)

    parts = lax.all_to_all(acc.reshape(n_dp * n_t, 3, tok), ("dp", "tensor"), 0, 0, tiled=True)
    top = jnp.max(parts[:, 0], axis=0)
    total = jnp.sum(parts[:, 1] * jnp.exp(parts[:, 0] - top[None, :]), axis=0)
    picked = jnp.sum(parts[:, 2], axis=0)

    seq_count = lengths.shape[0]
    position = jnp.arange(tok // seq_count, dtype=jnp.int32)
    live = (position[None, :] < lengths[:, None]).reshape(-1).astype(jnp.float32)
    logprob = picked - top - jnp.log(total)
    return (live * logprob, live * (logprob - old_logprob))


def solution(mesh):
    in_specs = (
        P("dp", "tensor"),
        P("tensor"),
        P(None, ("dp", "tensor")),
        P("dp"),
        P("dp"),
        P("dp"),
    )
    out_specs = (P("dp"), P("dp"))
    return jax.shard_map(body, mesh=mesh, in_specs=in_specs, out_specs=out_specs, check_vma=False)
```

```python
import functools

import jax
import jax.numpy as jnp
from jax import lax
from jax.experimental import pallas as pl
from jax.experimental.pallas import tpu as pltpu
from jax.sharding import PartitionSpec as P

D = 8192
CORES = 2
X_ONLY, Y_ONLY = (0, 1), (1, 0)
VMEM_LIMIT = 16 * 1024 * 1024
SMALL_LIMIT = 6 * 1024 * 1024


class Grid:
    def __init__(self, n_dp, n_t):
        self.n_t = n_t
        self.cols = 2
        self.rows = n_dp // self.cols
        self.depth = n_t // CORES
        self.square = self.rows == self.cols
        self.first = (X_ONLY, Y_ONLY) if self.square else (X_ONLY, X_ONLY)
        self.second = (Y_ONLY, X_ONLY) if self.square else (Y_ONLY, Y_ONLY)
        self.spots = [(j, i) for j in range(self.rows) for i in range(self.cols)]

    def permute(self, a, place):
        perm = []
        for y in range(self.rows):
            for x in range(self.cols):
                for z in range(self.depth):
                    for c in range(CORES):
                        src = (y * self.cols + x) * self.n_t + z * CORES + c
                        v, u, w, d = place(y, x, z, c)
                        dst = (v % self.rows * self.cols + u % self.cols) * self.n_t
                        perm.append((src, dst + w % self.depth * CORES + d % CORES))
        return lax.ppermute(a, ("dp", "tensor"), perm)

    def plane(self, a, ways, step):
        def place(y, x, z, c):
            return y + ways[c][0] * step, x + ways[c][1] * step, z, c

        return self.permute(a, place)

    def along(self, a, step):
        return self.permute(a, lambda y, x, z, c: (y, x, z + step, c))

    def sibling(self, a):
        return self.permute(a, lambda y, x, z, c: (y, x, z, c + 1))

    def reach(self, a):
        got = {(0, 0): a}
        for i in range(1, self.cols):
            got[0, i] = self.plane(a, self.first, i)
        for j in range(1, self.rows):
            got[j, 0] = self.plane(a, self.second, j)
        return got

    def fill(self, got, *late):
        late = (*late, *got.values())
        for j in range(1, self.rows):
            for i in range(1, self.cols):
                got[j, i] = self.plane(after(got[0, i], *late), self.second, j)
        return [got[s] for s in self.spots]

    def leap(self, got):
        def place_of(j, i):
            def place(y, x, z, c):
                (fy, fx), (sy, sx) = self.first[c], self.second[c]
                return y + fy * i + sy * j, x + fx * i + sx * j, z, c

            return place

        return [got[s] if s in got else self.permute(got[0, 0], place_of(*s)) for s in self.spots]

    def owners(self, y, x, c):
        ways = [(self.first[k], self.second[k]) for k in range(CORES)]
        out = []
        for j, i in self.spots:
            at = [
                (y - f[0] * i - s[0] * j) % self.rows * self.cols + (x - f[1] * i - s[1] * j) % self.cols
                for f, s in ways
            ]
            out.append(jnp.where(c == 0, at[0], at[1]))
        return out

    def sibling_spot(self, k):
        j, i = self.spots[k]
        return self.spots.index((i, j)) if self.square else k


def far(a):
    return pltpu.with_memory_space_constraint(a, pltpu.HBM)


def after(a, *others):
    return lax.optimization_barrier((a, *others))[0] if others else a


def diagonal(size):
    row = lax.broadcasted_iota(jnp.int32, (size, size), 0)
    return row == lax.broadcasted_iota(jnp.int32, (size, size), 1)


def to_column(row):
    return jnp.sum(jnp.where(diagonal(row.shape[1]), row, 0.0), axis=1, keepdims=True)


def to_row(column):
    return jnp.sum(jnp.where(diagonal(column.shape[0]), column, 0.0), axis=0, keepdims=True)


def load_kernel(offsets, start_ref, head_ref, out_ref, sems):
    size, deep = out_ref.shape[:2]
    copies = []
    for j in range(size):
        rows = pl.ds(pl.multiple_of(start_ref[offsets[j]] * deep, deep), deep)
        copies.append(pltpu.make_async_copy(head_ref.at[rows], out_ref.at[j], sems.at[j]))
        copies[-1].start()
    for copy in copies:
        copy.wait()


def loaded(starts, offsets, head, deep):
    return pl.pallas_call(
        functools.partial(load_kernel, offsets),
        out_shape=pltpu.VMEM((len(offsets), deep, head.shape[1]), head.dtype),
        in_specs=[pl.BlockSpec(memory_space=pltpu.SMEM), pl.BlockSpec(memory_space=pl.ANY)],
        out_specs=pl.BlockSpec(memory_space=pltpu.VMEM),
        scratch_shapes=[pltpu.SemaphoreType.DMA((len(offsets),))],
        compiler_params=pltpu.CompilerParams(vmem_limit_bytes=SMALL_LIMIT),
    )(starts, far(head))


def join_kernel(*refs):
    tok = refs[0].shape[0]
    for j, ref in enumerate(refs[:-1]):
        refs[-1][j * tok : (j + 1) * tok, :] = ref[...]


def joined(blocks):
    tok, feat = blocks[0].shape
    vmem = pl.BlockSpec(memory_space=pltpu.VMEM)
    return pl.pallas_call(
        join_kernel,
        out_shape=jax.ShapeDtypeStruct((len(blocks) * tok, feat), blocks[0].dtype),
        in_specs=[vmem] * len(blocks),
        out_specs=vmem,
        compiler_params=pltpu.CompilerParams(vmem_limit_bytes=SMALL_LIMIT),
    )(*blocks)


def layer_kernel(n, n_t, place, layer, offset, own, first, last, *refs):
    refs = list(refs)
    start_ref, fine = refs.pop(0), refs.pop(0)
    blocks = [refs.pop(0) for _ in range(CORES * n)]
    weights = refs.pop(0)
    acc_ref = None if first else refs.pop(0)
    out_ref, rows = refs.pop(0), refs.pop(0)
    acc = refs.pop(0) if last else out_ref
    feat = blocks[0].shape[1]
    tok = rows.shape[0] // n
    if own:
        deep = rows.shape[1]
        source = weights.at[pl.ds(pl.multiple_of(start_ref[offset] * deep, deep), deep)]
        copy = pltpu.make_async_copy(source, refs[0].at[layer], refs[1])
        copy.start()
        weights = refs[0]
    c_me, base = start_ref[0], start_ref[1]
    owners = [start_ref[2 + k] for k in range(n)]
    scales = []
    for k in range(n):
        sums = jnp.sum(fine[pl.ds(owners[k] * n_t, n_t), :, feat : feat + tok], axis=0)
        scales.append(to_column(lax.rsqrt(sums / D + 1e-06)))
    for c in range(CORES):
        core = 1 - c_me if c else c_me
        gain = fine[start_ref[offset] * CORES + core, :, :feat]
        columns = pl.ds(pl.multiple_of(core * feat, feat), feat)
        for k in range(n):
            spot = place[k] if c else k
            part = blocks[c * n + k][layer * tok : (layer + 1) * tok, :].astype(jnp.float32)
            part = part * scales[spot] * gain
            rows[spot * tok : (spot + 1) * tok, columns] = part.astype(jnp.bfloat16)
    if own:
        copy.wait()
    product = jnp.dot(rows[...], weights[layer], preferred_element_type=jnp.float32)
    acc[...] = product if first else acc_ref[...] + product
    if not last:
        return
    for b in range(n):
        logits = acc[b * tok : (b + 1) * tok, :]
        top = jnp.max(logits, axis=1, keepdims=True)
        total = jnp.sum(jnp.exp(logits - top), axis=1, keepdims=True)
        entry = lax.broadcasted_iota(jnp.int32, logits.shape, 1) + base
        target = fine[owners[b] * n_t, :, feat + tok : feat + 2 * tok]
        target = to_column(target).astype(jnp.int32)
        pick = jnp.sum(jnp.where(entry == target, logits, 0.0), axis=1, keepdims=True)
        stats = [to_row(top), to_row(total), to_row(pick)]
        for peer in range(n_t):
            for i, row in enumerate(stats):
                out_ref[owners[b], peer, i : i + 1, :] = row


def layer_product(tok, n_t, starts, layer, offset, fine, blocks, place, weights, acc, last):
    n = len(place)
    feat = blocks[0].shape[1]
    own = weights.ndim == 2
    deep, vocab = CORES * feat, weights.shape[-1]
    vmem = pl.BlockSpec(memory_space=pltpu.VMEM)
    first = acc is None
    logits = jax.ShapeDtypeStruct((n * tok, vocab), jnp.float32)
    operands = [starts, fine, *blocks, far(weights) if own else weights] + ([] if first else [acc])
    specs = [pl.BlockSpec(memory_space=pltpu.SMEM)] + [vmem] * (len(operands) - 1)
    scratch = [pltpu.VMEM((n * tok, deep), jnp.bfloat16)]
    if last:
        scratch.append(pltpu.VMEM(logits.shape, jnp.float32))
    if own:
        specs[2 + len(blocks)] = pl.BlockSpec(memory_space=pl.ANY)
        scratch += [pltpu.VMEM((1, deep, vocab), weights.dtype), pltpu.SemaphoreType.DMA]
    return pl.pallas_call(
        functools.partial(layer_kernel, n, n_t, place, layer, offset, own, first, last),
        out_shape=jax.ShapeDtypeStruct((n, n_t, 3, tok), jnp.float32) if last else logits,
        in_specs=specs,
        out_specs=vmem,
        scratch_shapes=scratch,
        compiler_params=pltpu.CompilerParams(vmem_limit_bytes=VMEM_LIMIT),
        cost_estimate=pl.CostEstimate(
            flops=2 * n * tok * deep * vocab, bytes_accessed=2 * deep * vocab, transcendentals=0
        ),
    )(*operands)


def squares_kernel(hidden_ref, gain_ref, target_ref, out_ref, raw, gain, target, sems):
    pairs = ((hidden_ref, raw), (gain_ref, gain), (target_ref, target))
    copies = [pltpu.make_async_copy(a, b, sems.at[i]) for i, (a, b) in enumerate(pairs)]
    for copy in copies:
        copy.start()
    for copy in copies:
        copy.wait()
    tok, feat = raw.shape
    values = raw[...].astype(jnp.float32)
    sums = to_row(jnp.sum(values * values, axis=1, keepdims=True))
    peers = out_ref.shape[0]
    for peer in range(peers):
        out_ref[peer, :, :feat] = gain[...]
        out_ref[peer, :, feat : feat + tok] = sums
        out_ref[peer, :, feat + tok :] = target[...].astype(jnp.float32)


def squares(hidden, gain, targets, peers):
    tok, feat = hidden.shape
    return pl.pallas_call(
        squares_kernel,
        out_shape=jax.ShapeDtypeStruct((peers, 1, feat + 2 * tok), jnp.float32),
        in_specs=[pl.BlockSpec(memory_space=pltpu.HBM)] * 3,
        out_specs=pl.BlockSpec(memory_space=pltpu.VMEM),
        scratch_shapes=[
            pltpu.VMEM(hidden.shape, hidden.dtype),
            pltpu.VMEM(gain.shape, gain.dtype),
            pltpu.VMEM(targets.shape, targets.dtype),
            pltpu.SemaphoreType.DMA((3,)),
        ],
        compiler_params=pltpu.CompilerParams(vmem_limit_bytes=SMALL_LIMIT),
    )(far(hidden), far(gain), far(targets))


def body(hidden, norm_gain, head, targets, old_logprob, lengths):
    n_dp, n_t = lax.axis_size("dp"), lax.axis_size("tensor")
    grid = Grid(n_dp, n_t)
    depth = grid.depth
    tok, feat = hidden.shape
    plane, tensor = lax.axis_index("dp"), lax.axis_index("tensor")
    z_me, c_me = tensor // CORES, tensor % CORES
    owners = grid.owners(plane // grid.cols, plane % grid.cols, c_me)
    groups = [[0]] + [[d, depth - d] for d in range(1, (depth + 1) // 2)] + [[depth // 2]]
    place = [grid.sibling_spot(k) for k in range(n_dp)]

    layers = {0: hidden}
    reached = [grid.reach(hidden)]
    for at, group in enumerate(groups[1:], 1):
        for dz in group:
            step = 1 if dz <= depth // 2 else -1
            layers[dz] = grid.along(layers[dz - step], step) if at > 1 else grid.along(hidden, dz)

    def reach_next(at, *late):
        if at < len(groups):
            sources = [layers[dz] for dz in groups[at]]
            sources[0] = after(sources[0], *late)
            reached.append(grid.reach(joined(sources) if len(sources) > 1 else sources[0]))

    reach_next(1, *reached[0].values())
    vocab_cols = head.shape[1]
    vocab_start = lax.axis_index(("dp", "tensor")) * vocab_cols
    starts = jnp.stack([c_me, vocab_start] + owners + [(z_me - dz) % depth for dz in range(depth)])
    packed = squares(after(hidden, starts), norm_gain[None, :], targets[None, :], n_dp * n_t)
    fine = lax.all_to_all(packed, ("dp", "tensor"), 0, 0, tiled=True)

    acc, deep = None, CORES * feat
    for at, group in enumerate(groups):
        final = at == len(groups) - 1
        middle = at and not final
        offsets = [2 + n_dp + dz for dz in group]
        own = grid.sibling(reached[at][0, 0])
        held = [acc, own, *(layers[dz] for dz in groups[2])] if at == 1 else [] if at else [packed]
        spread = grid.leap(reached[at]) if final else grid.fill(dict(reached[at]), *held)
        early = [grid.sibling(after(a, acc)) for a in spread[1:-1]] if middle else []
        if at == 0:
            weights = [head]
        elif at == 1:
            for later in groups[1:]:
                ready = after(head, acc, *early, *(layers[dz] for dz in groups[2]))
                weights.append(loaded(starts, [2 + n_dp + dz for dz in later], ready, deep))
        if at:
            reach_next(at + 1, weights[1] if at == 1 else spread[-1])
        others = [own] + (early or [grid.sibling(after(a, acc) if final else a) for a in spread[1:-1]])
        others.append(grid.sibling(after(spread[-1], *([acc] if final else weights[1:3] if middle else []))))
        blocks = spread + others
        for layer, offset in enumerate(offsets):
            done = layer == len(offsets) - 1
            last = final and done
            acc = layer_product(tok, n_t, starts, layer, offset, fine, blocks, place, weights[at], acc, last)

    parts = lax.all_to_all(acc.reshape(n_dp * n_t, 3, tok), ("dp", "tensor"), 0, 0, tiled=True)
    top = jnp.max(parts[:, 0], axis=0)
    total = jnp.sum(parts[:, 1] * jnp.exp(parts[:, 0] - top[None, :]), axis=0)
    picked = jnp.sum(parts[:, 2], axis=0)

    seq_count = lengths.shape[0]
    position = jnp.arange(tok // seq_count, dtype=jnp.int32)
    live = (position[None, :] < lengths[:, None]).reshape(-1).astype(jnp.float32)
    logprob = picked - top - jnp.log(total)
    return (live * logprob, live * (logprob - old_logprob))


def solution(mesh):
    in_specs = (
        P("dp", "tensor"),
        P("tensor"),
        P(None, ("dp", "tensor")),
        P("dp"),
        P("dp"),
        P("dp"),
    )
    out_specs = (P("dp"), P("dp"))
    return jax.shard_map(body, mesh=mesh, in_specs=in_specs, out_specs=out_specs, check_vma=False)
```

```python
import functools

import jax
import jax.numpy as jnp
from jax import lax
from jax.experimental import pallas as pl
from jax.experimental.pallas import tpu as pltpu
from jax.sharding import PartitionSpec as P

D = 8192
CORES = 2
X_ONLY, Y_ONLY = (0, 1), (1, 0)
VMEM_LIMIT = 16 * 1024 * 1024
SMALL_LIMIT = 6 * 1024 * 1024


class Grid:
    def __init__(self, n_dp, n_t):
        self.n_t = n_t
        self.cols = 2
        self.rows = n_dp // self.cols
        self.depth = n_t // CORES
        self.square = self.rows == self.cols
        self.first = (X_ONLY, Y_ONLY) if self.square else (X_ONLY, X_ONLY)
        self.second = (Y_ONLY, X_ONLY) if self.square else (Y_ONLY, Y_ONLY)
        self.spots = [(j, i) for j in range(self.rows) for i in range(self.cols)]

    def permute(self, a, place):
        perm = []
        for y in range(self.rows):
            for x in range(self.cols):
                for z in range(self.depth):
                    for c in range(CORES):
                        src = (y * self.cols + x) * self.n_t + z * CORES + c
                        v, u, w, d = place(y, x, z, c)
                        dst = (v % self.rows * self.cols + u % self.cols) * self.n_t
                        perm.append((src, dst + w % self.depth * CORES + d % CORES))
        return lax.ppermute(a, ("dp", "tensor"), perm)

    def plane(self, a, ways, step):
        def place(y, x, z, c):
            return y + ways[c][0] * step, x + ways[c][1] * step, z, c

        return self.permute(a, place)

    def along(self, a, step):
        return self.permute(a, lambda y, x, z, c: (y, x, z + step, c))

    def sibling(self, a):
        return self.permute(a, lambda y, x, z, c: (y, x, z, c + 1))

    def reach(self, a):
        got = {(0, 0): a}
        for i in range(1, self.cols):
            got[0, i] = self.plane(a, self.first, i)
        for j in range(1, self.rows):
            got[j, 0] = self.plane(a, self.second, j)
        return got

    def fill(self, got, *late):
        late = (*late, *got.values())
        for j in range(1, self.rows):
            for i in range(1, self.cols):
                got[j, i] = self.plane(after(got[0, i], *late), self.second, j)
        return [got[s] for s in self.spots]

    def owners(self, y, x, c):
        ways = [(self.first[k], self.second[k]) for k in range(CORES)]
        out = []
        for j, i in self.spots:
            at = [
                (y - f[0] * i - s[0] * j) % self.rows * self.cols + (x - f[1] * i - s[1] * j) % self.cols
                for f, s in ways
            ]
            out.append(jnp.where(c == 0, at[0], at[1]))
        return out

    def sibling_spot(self, k):
        j, i = self.spots[k]
        return self.spots.index((i, j)) if self.square else k


def far(a):
    return pltpu.with_memory_space_constraint(a, pltpu.HBM)


def after(a, *others):
    return lax.optimization_barrier((a, *others))[0] if others else a


def diagonal(size):
    row = lax.broadcasted_iota(jnp.int32, (size, size), 0)
    return row == lax.broadcasted_iota(jnp.int32, (size, size), 1)


def to_column(row):
    return jnp.sum(jnp.where(diagonal(row.shape[1]), row, 0.0), axis=1, keepdims=True)


def to_row(column):
    return jnp.sum(jnp.where(diagonal(column.shape[0]), column, 0.0), axis=0, keepdims=True)


def load_kernel(offsets, start_ref, head_ref, out_ref, sems):
    size, deep = out_ref.shape[:2]
    copies = []
    for j in range(size):
        rows = pl.ds(pl.multiple_of(start_ref[offsets[j]] * deep, deep), deep)
        copies.append(pltpu.make_async_copy(head_ref.at[rows], out_ref.at[j], sems.at[j]))
        copies[-1].start()
    for copy in copies:
        copy.wait()


def loaded(starts, offsets, head, deep):
    return pl.pallas_call(
        functools.partial(load_kernel, offsets),
        out_shape=pltpu.VMEM((len(offsets), deep, head.shape[1]), head.dtype),
        in_specs=[pl.BlockSpec(memory_space=pltpu.SMEM), pl.BlockSpec(memory_space=pl.ANY)],
        out_specs=pl.BlockSpec(memory_space=pltpu.VMEM),
        scratch_shapes=[pltpu.SemaphoreType.DMA((len(offsets),))],
        compiler_params=pltpu.CompilerParams(vmem_limit_bytes=SMALL_LIMIT),
    )(starts, far(head))


def layer_kernel(n, n_t, place, layer, offset, own, first, last, *refs):
    refs = list(refs)
    start_ref, fine = refs.pop(0), refs.pop(0)
    blocks = [refs.pop(0) for _ in range(CORES * n)]
    weights = refs.pop(0)
    acc_ref = None if first else refs.pop(0)
    out_ref, rows = refs.pop(0), refs.pop(0)
    acc = refs.pop(0) if last else out_ref
    feat = blocks[0].shape[1]
    tok = rows.shape[0] // n
    if own:
        deep = rows.shape[1]
        source = weights.at[pl.ds(pl.multiple_of(start_ref[offset] * deep, deep), deep)]
        copy = pltpu.make_async_copy(source, refs[0].at[layer], refs[1])
        copy.start()
        weights = refs[0]
    c_me, base = start_ref[0], start_ref[1]
    owners = [start_ref[2 + k] for k in range(n)]
    scales = []
    for k in range(n):
        sums = jnp.sum(fine[pl.ds(owners[k] * n_t, n_t), :, feat : feat + tok], axis=0)
        scales.append(to_column(lax.rsqrt(sums / D + 1e-06)))
    for c in range(CORES):
        core = 1 - c_me if c else c_me
        gain = fine[start_ref[offset] * CORES + core, :, :feat]
        columns = pl.ds(pl.multiple_of(core * feat, feat), feat)
        for k in range(n):
            spot = place[k] if c else k
            part = blocks[c * n + k][layer * tok : (layer + 1) * tok, :].astype(jnp.float32)
            part = part * scales[spot] * gain
            rows[spot * tok : (spot + 1) * tok, columns] = part.astype(jnp.bfloat16)
    if own:
        copy.wait()
    product = jnp.dot(rows[...], weights[layer], preferred_element_type=jnp.float32)
    acc[...] = product if first else acc_ref[...] + product
    if not last:
        return
    for b in range(n):
        logits = acc[b * tok : (b + 1) * tok, :]
        top = jnp.max(logits, axis=1, keepdims=True)
        total = jnp.sum(jnp.exp(logits - top), axis=1, keepdims=True)
        entry = lax.broadcasted_iota(jnp.int32, logits.shape, 1) + base
        target = fine[owners[b] * n_t, :, feat + tok : feat + 2 * tok]
        target = to_column(target).astype(jnp.int32)
        pick = jnp.sum(jnp.where(entry == target, logits, 0.0), axis=1, keepdims=True)
        for peer in range(n_t):
            out_ref[owners[b], peer, 0:1, :] = to_row(top)
            out_ref[owners[b], peer, 1:2, :] = to_row(total)
            out_ref[owners[b], peer, 2:3, :] = to_row(pick)


def layer_product(tok, n_t, starts, layer, offset, fine, blocks, place, weights, acc, last):
    n = len(place)
    feat = blocks[0].shape[1]
    own = weights.ndim == 2
    deep, vocab = CORES * feat, weights.shape[-1]
    vmem = pl.BlockSpec(memory_space=pltpu.VMEM)
    first = acc is None
    logits = jax.ShapeDtypeStruct((n * tok, vocab), jnp.float32)
    operands = [starts, fine, *blocks, far(weights) if own else weights] + ([] if first else [acc])
    specs = [pl.BlockSpec(memory_space=pltpu.SMEM)] + [vmem] * (len(operands) - 1)
    scratch = [pltpu.VMEM((n * tok, deep), jnp.bfloat16)]
    if last:
        scratch.append(pltpu.VMEM(logits.shape, jnp.float32))
    if own:
        specs[2 + len(blocks)] = pl.BlockSpec(memory_space=pl.ANY)
        scratch += [pltpu.VMEM((1, deep, vocab), weights.dtype), pltpu.SemaphoreType.DMA]
    return pl.pallas_call(
        functools.partial(layer_kernel, n, n_t, place, layer, offset, own, first, last),
        out_shape=jax.ShapeDtypeStruct((n, n_t, 3, tok), jnp.float32) if last else logits,
        in_specs=specs,
        out_specs=vmem,
        scratch_shapes=scratch,
        compiler_params=pltpu.CompilerParams(vmem_limit_bytes=VMEM_LIMIT),
        cost_estimate=pl.CostEstimate(
            flops=2 * n * tok * deep * vocab, bytes_accessed=2 * deep * vocab, transcendentals=0
        ),
    )(*operands)


def squares_kernel(hidden_ref, gain_ref, target_ref, out_ref, raw, gain, target, sems):
    pairs = ((hidden_ref, raw), (gain_ref, gain), (target_ref, target))
    copies = [pltpu.make_async_copy(a, b, sems.at[i]) for i, (a, b) in enumerate(pairs)]
    for copy in copies:
        copy.start()
    for copy in copies:
        copy.wait()
    tok, feat = raw.shape
    values = raw[...].astype(jnp.float32)
    sums = to_row(jnp.sum(values * values, axis=1, keepdims=True))
    peers = out_ref.shape[0]
    for peer in range(peers):
        out_ref[peer, :, :feat] = gain[...]
        out_ref[peer, :, feat : feat + tok] = sums
        out_ref[peer, :, feat + tok :] = target[...].astype(jnp.float32)


def squares(hidden, gain, targets, peers):
    tok, feat = hidden.shape
    return pl.pallas_call(
        squares_kernel,
        out_shape=jax.ShapeDtypeStruct((peers, 1, feat + 2 * tok), jnp.float32),
        in_specs=[pl.BlockSpec(memory_space=pltpu.HBM)] * 3,
        out_specs=pl.BlockSpec(memory_space=pltpu.VMEM),
        scratch_shapes=[
            pltpu.VMEM(hidden.shape, hidden.dtype),
            pltpu.VMEM(gain.shape, gain.dtype),
            pltpu.VMEM(targets.shape, targets.dtype),
            pltpu.SemaphoreType.DMA((3,)),
        ],
        compiler_params=pltpu.CompilerParams(vmem_limit_bytes=SMALL_LIMIT),
    )(far(hidden), far(gain), far(targets))


def body(hidden, norm_gain, head, targets, old_logprob, lengths):
    n_dp, n_t = lax.axis_size("dp"), lax.axis_size("tensor")
    grid = Grid(n_dp, n_t)
    depth = grid.depth
    tok, feat = hidden.shape
    plane, tensor = lax.axis_index("dp"), lax.axis_index("tensor")
    z_me, c_me = tensor // CORES, tensor % CORES
    owners = grid.owners(plane // grid.cols, plane % grid.cols, c_me)
    order = [0] + [d for k in range(1, depth // 2) for d in (k, depth - k)] + [depth // 2]
    place = [grid.sibling_spot(k) for k in range(n_dp)]

    layers = {0: hidden}
    reached = [grid.reach(hidden)]
    for dz in order[1:]:
        step = 1 if dz <= depth // 2 else -1
        layers[dz] = grid.along(layers[(dz - step) % depth], step)

    def reach_next(at, *late):
        if at < depth:
            reached.append(grid.reach(after(layers[order[at]], *late)))

    reach_next(1, *reached[0].values())
    reach_next(2, layers[1])

    vocab_cols = head.shape[1]
    vocab_start = lax.axis_index(("dp", "tensor")) * vocab_cols
    starts = jnp.stack([c_me, vocab_start] + owners + [(z_me - dz) % depth for dz in range(depth)])
    packed = squares(after(hidden, starts), norm_gain[None, :], targets[None, :], n_dp * n_t)
    fine = lax.all_to_all(packed, ("dp", "tensor"), 0, 0, tiled=True)

    acc, deep, results, weights = None, CORES * feat, [], [head]
    for at, dz in enumerate(order):
        final = at == depth - 1
        own = grid.sibling(reached[at][0, 0])
        if at == 1:
            for later in order[1:]:
                ready = after(head, acc, layers[order[3]])
                weights.append(loaded(starts, [2 + n_dp + later], ready, deep))
        held = [packed] if at == 0 else [] if at == 1 else [acc if at == 2 else results[at - 2]]
        if at == 2:
            held = [results[0], own, layers[order[3]]]
        spread = grid.fill(dict(reached[at]), *held)
        if at >= 2:
            reach_next(at + 1, spread[-1])
        others = [own] + [grid.sibling(a) for a in spread[1:-1]]
        others.append(grid.sibling(after(spread[-1], *([acc] if final else weights[1:4] if at == 2 else []))))
        blocks = spread + others
        if at >= 2 and not final:
            blocks[0] = after(blocks[0], *reached[at + 1].values())
        acc = layer_product(tok, n_t, starts, 0, 2 + n_dp + dz, fine, blocks, place, weights[at], acc, final)
        results.append(acc)

    parts = lax.all_to_all(acc.reshape(n_dp * n_t, 3, tok), ("dp", "tensor"), 0, 0, tiled=True)
    top = jnp.max(parts[:, 0], axis=0)
    total = jnp.sum(parts[:, 1] * jnp.exp(parts[:, 0] - top[None, :]), axis=0)
    picked = jnp.sum(parts[:, 2], axis=0)

    seq_count = lengths.shape[0]
    position = jnp.arange(tok // seq_count, dtype=jnp.int32)
    live = (position[None, :] < lengths[:, None]).reshape(-1).astype(jnp.float32)
    logprob = picked - top - jnp.log(total)
    return (live * logprob, live * (logprob - old_logprob))


def solution(mesh):
    in_specs = (
        P("dp", "tensor"),
        P("tensor"),
        P(None, ("dp", "tensor")),
        P("dp"),
        P("dp"),
        P("dp"),
    )
    out_specs = (P("dp"), P("dp"))
    return jax.shard_map(body, mesh=mesh, in_specs=in_specs, out_specs=out_specs, check_vma=False)
```

```python
import functools

import jax
import jax.numpy as jnp
from jax import lax
from jax.experimental import pallas as pl
from jax.experimental.pallas import tpu as pltpu
from jax.sharding import PartitionSpec as P

D = 8192
CORES = 2
X_ONLY, Y_ONLY = (0, 1), (1, 0)
VMEM_LIMIT = 16 * 1024 * 1024
SMALL_LIMIT = 6 * 1024 * 1024


class Grid:
    def __init__(self, n_dp, n_t):
        self.n_t = n_t
        self.cols = 2
        self.rows = n_dp // self.cols
        self.depth = n_t // CORES
        self.square = self.rows == self.cols
        self.first = (X_ONLY, Y_ONLY) if self.square else (X_ONLY, X_ONLY)
        self.second = (Y_ONLY, X_ONLY) if self.square else (Y_ONLY, Y_ONLY)
        self.spots = [(j, i) for j in range(self.rows) for i in range(self.cols)]

    def permute(self, a, place):
        perm = []
        for y in range(self.rows):
            for x in range(self.cols):
                for z in range(self.depth):
                    for c in range(CORES):
                        src = (y * self.cols + x) * self.n_t + z * CORES + c
                        v, u, w, d = place(y, x, z, c)
                        dst = (v % self.rows * self.cols + u % self.cols) * self.n_t
                        perm.append((src, dst + w % self.depth * CORES + d % CORES))
        return lax.ppermute(a, ("dp", "tensor"), perm)

    def plane(self, a, ways, step):
        def place(y, x, z, c):
            return y + ways[c][0] * step, x + ways[c][1] * step, z, c

        return self.permute(a, place)

    def along(self, a, step):
        return self.permute(a, lambda y, x, z, c: (y, x, z + step, c))

    def sibling(self, a):
        return self.permute(a, lambda y, x, z, c: (y, x, z, c + 1))

    def reach(self, a):
        got = {(0, 0): a}
        for i in range(1, self.cols):
            got[0, i] = self.plane(a, self.first, i)
        for j in range(1, self.rows):
            got[j, 0] = self.plane(a, self.second, j)
        return got

    def fill(self, got, *late):
        late = (*late, *got.values())
        for j in range(1, self.rows):
            for i in range(1, self.cols):
                got[j, i] = self.plane(after(got[0, i], *late), self.second, j)
        return [got[s] for s in self.spots]

    def owners(self, y, x, c):
        ways = [(self.first[k], self.second[k]) for k in range(CORES)]
        out = []
        for j, i in self.spots:
            at = [
                (y - f[0] * i - s[0] * j) % self.rows * self.cols + (x - f[1] * i - s[1] * j) % self.cols
                for f, s in ways
            ]
            out.append(jnp.where(c == 0, at[0], at[1]))
        return out

    def sibling_spot(self, k):
        j, i = self.spots[k]
        return self.spots.index((i, j)) if self.square else k


def far(a):
    return pltpu.with_memory_space_constraint(a, pltpu.HBM)


def after(a, *others):
    return lax.optimization_barrier((a, *others))[0] if others else a


def diagonal(size):
    row = lax.broadcasted_iota(jnp.int32, (size, size), 0)
    return row == lax.broadcasted_iota(jnp.int32, (size, size), 1)


def to_column(row):
    return jnp.sum(jnp.where(diagonal(row.shape[1]), row, 0.0), axis=1, keepdims=True)


def to_row(column):
    return jnp.sum(jnp.where(diagonal(column.shape[0]), column, 0.0), axis=0, keepdims=True)


def load_kernel(offsets, start_ref, head_ref, out_ref, sems):
    size, deep = out_ref.shape[:2]
    copies = []
    for j in range(size):
        rows = pl.ds(pl.multiple_of(start_ref[offsets[j]] * deep, deep), deep)
        copies.append(pltpu.make_async_copy(head_ref.at[rows], out_ref.at[j], sems.at[j]))
        copies[-1].start()
    for copy in copies:
        copy.wait()


def loaded(starts, offsets, head, deep):
    return pl.pallas_call(
        functools.partial(load_kernel, offsets),
        out_shape=pltpu.VMEM((len(offsets), deep, head.shape[1]), head.dtype),
        in_specs=[pl.BlockSpec(memory_space=pltpu.SMEM), pl.BlockSpec(memory_space=pl.ANY)],
        out_specs=pl.BlockSpec(memory_space=pltpu.VMEM),
        scratch_shapes=[pltpu.SemaphoreType.DMA((len(offsets),))],
        compiler_params=pltpu.CompilerParams(vmem_limit_bytes=SMALL_LIMIT),
    )(starts, far(head))


def join_kernel(*refs):
    tok = refs[0].shape[0]
    for j, ref in enumerate(refs[:-1]):
        refs[-1][j * tok : (j + 1) * tok, :] = ref[...]


def joined(blocks):
    tok, feat = blocks[0].shape
    vmem = pl.BlockSpec(memory_space=pltpu.VMEM)
    return pl.pallas_call(
        join_kernel,
        out_shape=jax.ShapeDtypeStruct((len(blocks) * tok, feat), blocks[0].dtype),
        in_specs=[vmem] * len(blocks),
        out_specs=vmem,
        compiler_params=pltpu.CompilerParams(vmem_limit_bytes=SMALL_LIMIT),
    )(*blocks)


def layer_kernel(n, n_t, place, layer, offset, own, first, last, *refs):
    refs = list(refs)
    start_ref, fine = refs.pop(0), refs.pop(0)
    blocks = [refs.pop(0) for _ in range(CORES * n)]
    weights = refs.pop(0)
    acc_ref = None if first else refs.pop(0)
    out_ref, rows = refs.pop(0), refs.pop(0)
    acc = refs.pop(0) if last else out_ref
    feat = blocks[0].shape[1]
    tok = rows.shape[0] // n
    if own:
        deep = rows.shape[1]
        source = weights.at[pl.ds(pl.multiple_of(start_ref[offset] * deep, deep), deep)]
        copy = pltpu.make_async_copy(source, refs[0].at[layer], refs[1])
        copy.start()
        weights = refs[0]
    c_me, base = start_ref[0], start_ref[1]
    owners = [start_ref[2 + k] for k in range(n)]
    scales = []
    for k in range(n):
        sums = jnp.sum(fine[pl.ds(owners[k] * n_t, n_t), :, feat : feat + tok], axis=0)
        scales.append(to_column(lax.rsqrt(sums / D + 1e-06)))
    for c in range(CORES):
        core = 1 - c_me if c else c_me
        gain = fine[start_ref[offset] * CORES + core, :, :feat]
        columns = pl.ds(pl.multiple_of(core * feat, feat), feat)
        for k in range(n):
            spot = place[k] if c else k
            part = blocks[c * n + k][layer * tok : (layer + 1) * tok, :].astype(jnp.float32)
            part = part * scales[spot] * gain
            rows[spot * tok : (spot + 1) * tok, columns] = part.astype(jnp.bfloat16)
    if own:
        copy.wait()
    product = jnp.dot(rows[...], weights[layer], preferred_element_type=jnp.float32)
    acc[...] = product if first else acc_ref[...] + product
    if not last:
        return
    for b in range(n):
        logits = acc[b * tok : (b + 1) * tok, :]
        top = jnp.max(logits, axis=1, keepdims=True)
        total = jnp.sum(jnp.exp(logits - top), axis=1, keepdims=True)
        entry = lax.broadcasted_iota(jnp.int32, logits.shape, 1) + base
        target = fine[owners[b] * n_t, :, feat + tok : feat + 2 * tok]
        target = to_column(target).astype(jnp.int32)
        pick = jnp.sum(jnp.where(entry == target, logits, 0.0), axis=1, keepdims=True)
        for peer in range(n_t):
            out_ref[owners[b], peer, 0:1, :] = to_row(top)
            out_ref[owners[b], peer, 1:2, :] = to_row(total)
            out_ref[owners[b], peer, 2:3, :] = to_row(pick)


def layer_product(tok, n_t, starts, layer, offset, fine, blocks, place, weights, acc, last):
    n = len(place)
    feat = blocks[0].shape[1]
    own = weights.ndim == 2
    deep, vocab = CORES * feat, weights.shape[-1]
    vmem = pl.BlockSpec(memory_space=pltpu.VMEM)
    first = acc is None
    logits = jax.ShapeDtypeStruct((n * tok, vocab), jnp.float32)
    operands = [starts, fine, *blocks, far(weights) if own else weights] + ([] if first else [acc])
    specs = [pl.BlockSpec(memory_space=pltpu.SMEM)] + [vmem] * (len(operands) - 1)
    scratch = [pltpu.VMEM((n * tok, deep), jnp.bfloat16)]
    if last:
        scratch.append(pltpu.VMEM(logits.shape, jnp.float32))
    if own:
        specs[2 + len(blocks)] = pl.BlockSpec(memory_space=pl.ANY)
        scratch += [pltpu.VMEM((1, deep, vocab), weights.dtype), pltpu.SemaphoreType.DMA]
    return pl.pallas_call(
        functools.partial(layer_kernel, n, n_t, place, layer, offset, own, first, last),
        out_shape=jax.ShapeDtypeStruct((n, n_t, 3, tok), jnp.float32) if last else logits,
        in_specs=specs,
        out_specs=vmem,
        scratch_shapes=scratch,
        compiler_params=pltpu.CompilerParams(vmem_limit_bytes=VMEM_LIMIT),
        cost_estimate=pl.CostEstimate(
            flops=2 * n * tok * deep * vocab, bytes_accessed=2 * deep * vocab, transcendentals=0
        ),
    )(*operands)


def squares_kernel(hidden_ref, gain_ref, target_ref, out_ref, raw, gain, target, sems):
    pairs = ((hidden_ref, raw), (gain_ref, gain), (target_ref, target))
    copies = [pltpu.make_async_copy(a, b, sems.at[i]) for i, (a, b) in enumerate(pairs)]
    for copy in copies:
        copy.start()
    for copy in copies:
        copy.wait()
    tok, feat = raw.shape
    values = raw[...].astype(jnp.float32)
    sums = to_row(jnp.sum(values * values, axis=1, keepdims=True))
    peers = out_ref.shape[0]
    for peer in range(peers):
        out_ref[peer, :, :feat] = gain[...]
        out_ref[peer, :, feat : feat + tok] = sums
        out_ref[peer, :, feat + tok :] = target[...].astype(jnp.float32)


def squares(hidden, gain, targets, peers):
    tok, feat = hidden.shape
    return pl.pallas_call(
        squares_kernel,
        out_shape=jax.ShapeDtypeStruct((peers, 1, feat + 2 * tok), jnp.float32),
        in_specs=[pl.BlockSpec(memory_space=pltpu.HBM)] * 3,
        out_specs=pl.BlockSpec(memory_space=pltpu.VMEM),
        scratch_shapes=[
            pltpu.VMEM(hidden.shape, hidden.dtype),
            pltpu.VMEM(gain.shape, gain.dtype),
            pltpu.VMEM(targets.shape, targets.dtype),
            pltpu.SemaphoreType.DMA((3,)),
        ],
        compiler_params=pltpu.CompilerParams(vmem_limit_bytes=SMALL_LIMIT),
    )(far(hidden), far(gain), far(targets))


def body(hidden, norm_gain, head, targets, old_logprob, lengths):
    n_dp, n_t = lax.axis_size("dp"), lax.axis_size("tensor")
    grid = Grid(n_dp, n_t)
    depth = grid.depth
    tok, feat = hidden.shape
    plane, tensor = lax.axis_index("dp"), lax.axis_index("tensor")
    z_me, c_me = tensor // CORES, tensor % CORES
    owners = grid.owners(plane // grid.cols, plane % grid.cols, c_me)
    groups = [[0]] + [[d, depth - d] for d in range(1, (depth + 1) // 2)] + [[depth // 2]]
    place = [grid.sibling_spot(k) for k in range(n_dp)]

    layers = {0: hidden}
    reached = [grid.reach(hidden)]
    for at, group in enumerate(groups[1:], 1):
        for dz in group:
            step = 1 if dz <= depth // 2 else -1
            layers[dz] = grid.along(layers[dz - step], step) if at > 1 else grid.along(hidden, dz)

    def reach_next(at, *late):
        if at < len(groups):
            sources = [layers[dz] for dz in groups[at]]
            sources[0] = after(sources[0], *late)
            reached.append(grid.reach(joined(sources) if len(sources) > 1 else sources[0]))

    reach_next(1, *reached[0].values())
    vocab_cols = head.shape[1]
    vocab_start = lax.axis_index(("dp", "tensor")) * vocab_cols
    starts = jnp.stack([c_me, vocab_start] + owners + [(z_me - dz) % depth for dz in range(depth)])
    packed = squares(after(hidden, starts), norm_gain[None, :], targets[None, :], n_dp * n_t)
    fine = lax.all_to_all(packed, ("dp", "tensor"), 0, 0, tiled=True)

    acc, deep, spreads, half = None, CORES * feat, {}, []
    for at, group in enumerate(groups):
        final = at == len(groups) - 1
        middle = at and not final
        offsets = [2 + n_dp + dz for dz in group]
        own = grid.sibling(after(reached[at][0, 0], *(half if final else [])))
        if at == 1:
            held = [acc, own, *(layers[dz] for dz in groups[2])]
        else:
            held = [] if at else [packed]
        spread = spreads.get(at) or grid.fill(dict(reached[at]), *held)
        if at == 0:
            weights = [head]
        elif at == 1:
            for later in groups[1:]:
                ready = after(head, acc, *(layers[dz] for dz in groups[2]))
                weights.append(loaded(starts, [2 + n_dp + dz for dz in later], ready, deep))
        following = half if final else []
        if middle:
            reach_next(at + 1, *reached[at].values())
            following = [*reached[at + 1].values(), *weights[1:3]]
            spreads[at + 1] = grid.fill(dict(reached[at + 1]))
        others = [own] + [grid.sibling(after(a, *following)) for a in spread[1:]]
        blocks = spread + others
        for layer, offset in enumerate(offsets):
            done = layer == len(offsets) - 1
            if middle and done:
                half = [acc]
                blocks[0] = after(blocks[0], spreads[at + 1][-1])
            last = final and done
            acc = layer_product(tok, n_t, starts, layer, offset, fine, blocks, place, weights[at], acc, last)

    parts = lax.all_to_all(acc.reshape(n_dp * n_t, 3, tok), ("dp", "tensor"), 0, 0, tiled=True)
    top = jnp.max(parts[:, 0], axis=0)
    total = jnp.sum(parts[:, 1] * jnp.exp(parts[:, 0] - top[None, :]), axis=0)
    picked = jnp.sum(parts[:, 2], axis=0)

    seq_count = lengths.shape[0]
    position = jnp.arange(tok // seq_count, dtype=jnp.int32)
    live = (position[None, :] < lengths[:, None]).reshape(-1).astype(jnp.float32)
    logprob = picked - top - jnp.log(total)
    return (live * logprob, live * (logprob - old_logprob))


def solution(mesh):
    in_specs = (
        P("dp", "tensor"),
        P("tensor"),
        P(None, ("dp", "tensor")),
        P("dp"),
        P("dp"),
        P("dp"),
    )
    out_specs = (P("dp"), P("dp"))
    return jax.shard_map(body, mesh=mesh, in_specs=in_specs, out_specs=out_specs, check_vma=False)
```

```python
import functools

import jax
import jax.numpy as jnp
from jax import lax
from jax.experimental import pallas as pl
from jax.experimental.pallas import tpu as pltpu
from jax.sharding import PartitionSpec as P

D = 8192
CORES = 2
X_ONLY, Y_ONLY = (0, 1), (1, 0)
VMEM_LIMIT = 16 * 1024 * 1024
SMALL_LIMIT = 6 * 1024 * 1024


class Grid:
    def __init__(self, n_dp, n_t):
        self.n_t = n_t
        self.cols = 2
        self.rows = n_dp // self.cols
        self.depth = n_t // CORES
        self.square = self.rows == self.cols
        self.first = (X_ONLY, Y_ONLY) if self.square else (X_ONLY, X_ONLY)
        self.second = (Y_ONLY, X_ONLY) if self.square else (Y_ONLY, Y_ONLY)
        self.spots = [(j, i) for j in range(self.rows) for i in range(self.cols)]

    def permute(self, a, place):
        perm = []
        for y in range(self.rows):
            for x in range(self.cols):
                for z in range(self.depth):
                    for c in range(CORES):
                        src = (y * self.cols + x) * self.n_t + z * CORES + c
                        v, u, w, d = place(y, x, z, c)
                        dst = (v % self.rows * self.cols + u % self.cols) * self.n_t
                        perm.append((src, dst + w % self.depth * CORES + d % CORES))
        return lax.ppermute(a, ("dp", "tensor"), perm)

    def plane(self, a, ways, step):
        def place(y, x, z, c):
            return y + ways[c][0] * step, x + ways[c][1] * step, z, c

        return self.permute(a, place)

    def along(self, a, step):
        return self.permute(a, lambda y, x, z, c: (y, x, z + step, c))

    def sibling(self, a):
        return self.permute(a, lambda y, x, z, c: (y, x, z, c + 1))

    def reach(self, a):
        got = {(0, 0): a}
        for i in range(1, self.cols):
            got[0, i] = self.plane(a, self.first, i)
        for j in range(1, self.rows):
            got[j, 0] = self.plane(a, self.second, j)
        return got

    def fill(self, got, *late):
        late = (*late, *got.values())
        for j in range(1, self.rows):
            for i in range(1, self.cols):
                got[j, i] = self.plane(after(got[0, i], *late), self.second, j)
        return [got[s] for s in self.spots]

    def owners(self, y, x, c):
        ways = [(self.first[k], self.second[k]) for k in range(CORES)]
        out = []
        for j, i in self.spots:
            at = [
                (y - f[0] * i - s[0] * j) % self.rows * self.cols + (x - f[1] * i - s[1] * j) % self.cols
                for f, s in ways
            ]
            out.append(jnp.where(c == 0, at[0], at[1]))
        return out

    def sibling_spot(self, k):
        j, i = self.spots[k]
        return self.spots.index((i, j)) if self.square else k


def far(a):
    return pltpu.with_memory_space_constraint(a, pltpu.HBM)


def after(a, *others):
    return lax.optimization_barrier((a, *others))[0] if others else a


def diagonal(size):
    row = lax.broadcasted_iota(jnp.int32, (size, size), 0)
    return row == lax.broadcasted_iota(jnp.int32, (size, size), 1)


def to_column(row):
    return jnp.sum(jnp.where(diagonal(row.shape[1]), row, 0.0), axis=1, keepdims=True)


def to_row(column):
    return jnp.sum(jnp.where(diagonal(column.shape[0]), column, 0.0), axis=0, keepdims=True)


def load_kernel(offsets, start_ref, head_ref, out_ref, sems):
    size, deep = out_ref.shape[:2]
    copies = []
    for j in range(size):
        rows = pl.ds(pl.multiple_of(start_ref[offsets[j]] * deep, deep), deep)
        copies.append(pltpu.make_async_copy(head_ref.at[rows], out_ref.at[j], sems.at[j]))
        copies[-1].start()
    for copy in copies:
        copy.wait()


def loaded(starts, offsets, head, deep):
    return pl.pallas_call(
        functools.partial(load_kernel, offsets),
        out_shape=pltpu.VMEM((len(offsets), deep, head.shape[1]), head.dtype),
        in_specs=[pl.BlockSpec(memory_space=pltpu.SMEM), pl.BlockSpec(memory_space=pl.ANY)],
        out_specs=pl.BlockSpec(memory_space=pltpu.VMEM),
        scratch_shapes=[pltpu.SemaphoreType.DMA((len(offsets),))],
        compiler_params=pltpu.CompilerParams(vmem_limit_bytes=SMALL_LIMIT),
    )(starts, far(head))


def join_kernel(*refs):
    tok = refs[0].shape[0]
    for j, ref in enumerate(refs[:-1]):
        refs[-1][j * tok : (j + 1) * tok, :] = ref[...]


def joined(blocks):
    tok, feat = blocks[0].shape
    vmem = pl.BlockSpec(memory_space=pltpu.VMEM)
    return pl.pallas_call(
        join_kernel,
        out_shape=jax.ShapeDtypeStruct((len(blocks) * tok, feat), blocks[0].dtype),
        in_specs=[vmem] * len(blocks),
        out_specs=vmem,
        compiler_params=pltpu.CompilerParams(vmem_limit_bytes=SMALL_LIMIT),
    )(*blocks)


def layer_kernel(n, n_t, place, layer, offset, own, first, last, *refs):
    refs = list(refs)
    start_ref, fine = refs.pop(0), refs.pop(0)
    blocks = [refs.pop(0) for _ in range(CORES * n)]
    weights = refs.pop(0)
    acc_ref = None if first else refs.pop(0)
    out_ref, rows = refs.pop(0), refs.pop(0)
    acc = refs.pop(0) if last else out_ref
    feat = blocks[0].shape[1]
    tok = rows.shape[0] // n
    if own:
        deep = rows.shape[1]
        source = weights.at[pl.ds(pl.multiple_of(start_ref[offset] * deep, deep), deep)]
        copy = pltpu.make_async_copy(source, refs[0].at[layer], refs[1])
        copy.start()
        weights = refs[0]
    c_me, base = start_ref[0], start_ref[1]
    owners = [start_ref[2 + k] for k in range(n)]
    scales = []
    for k in range(n):
        sums = jnp.sum(fine[pl.ds(owners[k] * n_t, n_t), :, feat : feat + tok], axis=0)
        scales.append(to_column(lax.rsqrt(sums / D + 1e-06)))
    for c in range(CORES):
        core = 1 - c_me if c else c_me
        gain = fine[start_ref[offset] * CORES + core, :, :feat]
        columns = pl.ds(pl.multiple_of(core * feat, feat), feat)
        for k in range(n):
            spot = place[k] if c else k
            part = blocks[c * n + k][layer * tok : (layer + 1) * tok, :].astype(jnp.float32)
            part = part * scales[spot] * gain
            rows[spot * tok : (spot + 1) * tok, columns] = part.astype(jnp.bfloat16)
    if own:
        copy.wait()
    product = jnp.dot(rows[...], weights[layer], preferred_element_type=jnp.float32)
    acc[...] = product if first else acc_ref[...] + product
    if not last:
        return
    for b in range(n):
        logits = acc[b * tok : (b + 1) * tok, :]
        top = jnp.max(logits, axis=1, keepdims=True)
        total = jnp.sum(jnp.exp(logits - top), axis=1, keepdims=True)
        entry = lax.broadcasted_iota(jnp.int32, logits.shape, 1) + base
        target = fine[owners[b] * n_t, :, feat + tok : feat + 2 * tok]
        target = to_column(target).astype(jnp.int32)
        pick = jnp.sum(jnp.where(entry == target, logits, 0.0), axis=1, keepdims=True)
        for peer in range(n_t):
            out_ref[owners[b], peer, 0:1, :] = to_row(top)
            out_ref[owners[b], peer, 1:2, :] = to_row(total)
            out_ref[owners[b], peer, 2:3, :] = to_row(pick)


def layer_product(tok, n_t, starts, layer, offset, fine, blocks, place, weights, acc, last):
    n = len(place)
    feat = blocks[0].shape[1]
    own = weights.ndim == 2
    deep, vocab = CORES * feat, weights.shape[-1]
    vmem = pl.BlockSpec(memory_space=pltpu.VMEM)
    first = acc is None
    logits = jax.ShapeDtypeStruct((n * tok, vocab), jnp.float32)
    operands = [starts, fine, *blocks, far(weights) if own else weights] + ([] if first else [acc])
    specs = [pl.BlockSpec(memory_space=pltpu.SMEM)] + [vmem] * (len(operands) - 1)
    scratch = [pltpu.VMEM((n * tok, deep), jnp.bfloat16)]
    if last:
        scratch.append(pltpu.VMEM(logits.shape, jnp.float32))
    if own:
        specs[2 + len(blocks)] = pl.BlockSpec(memory_space=pl.ANY)
        scratch += [pltpu.VMEM((1, deep, vocab), weights.dtype), pltpu.SemaphoreType.DMA]
    return pl.pallas_call(
        functools.partial(layer_kernel, n, n_t, place, layer, offset, own, first, last),
        out_shape=jax.ShapeDtypeStruct((n, n_t, 3, tok), jnp.float32) if last else logits,
        in_specs=specs,
        out_specs=vmem,
        scratch_shapes=scratch,
        compiler_params=pltpu.CompilerParams(vmem_limit_bytes=VMEM_LIMIT),
        cost_estimate=pl.CostEstimate(
            flops=2 * n * tok * deep * vocab, bytes_accessed=2 * deep * vocab, transcendentals=0
        ),
    )(*operands)


def squares_kernel(hidden_ref, gain_ref, target_ref, out_ref, raw, gain, target, sems):
    pairs = ((hidden_ref, raw), (gain_ref, gain), (target_ref, target))
    copies = [pltpu.make_async_copy(a, b, sems.at[i]) for i, (a, b) in enumerate(pairs)]
    for copy in copies:
        copy.start()
    for copy in copies:
        copy.wait()
    tok, feat = raw.shape
    values = raw[...].astype(jnp.float32)
    sums = to_row(jnp.sum(values * values, axis=1, keepdims=True))
    peers = out_ref.shape[0]
    for peer in range(peers):
        out_ref[peer, :, :feat] = gain[...]
        out_ref[peer, :, feat : feat + tok] = sums
        out_ref[peer, :, feat + tok :] = target[...].astype(jnp.float32)


def squares(hidden, gain, targets, peers):
    tok, feat = hidden.shape
    return pl.pallas_call(
        squares_kernel,
        out_shape=jax.ShapeDtypeStruct((peers, 1, feat + 2 * tok), jnp.float32),
        in_specs=[pl.BlockSpec(memory_space=pltpu.HBM)] * 3,
        out_specs=pl.BlockSpec(memory_space=pltpu.VMEM),
        scratch_shapes=[
            pltpu.VMEM(hidden.shape, hidden.dtype),
            pltpu.VMEM(gain.shape, gain.dtype),
            pltpu.VMEM(targets.shape, targets.dtype),
            pltpu.SemaphoreType.DMA((3,)),
        ],
        compiler_params=pltpu.CompilerParams(vmem_limit_bytes=SMALL_LIMIT),
    )(far(hidden), far(gain), far(targets))


def body(hidden, norm_gain, head, targets, old_logprob, lengths):
    n_dp, n_t = lax.axis_size("dp"), lax.axis_size("tensor")
    grid = Grid(n_dp, n_t)
    depth = grid.depth
    tok, feat = hidden.shape
    plane, tensor = lax.axis_index("dp"), lax.axis_index("tensor")
    z_me, c_me = tensor // CORES, tensor % CORES
    owners = grid.owners(plane // grid.cols, plane % grid.cols, c_me)
    groups = [[0]] + [[d, depth - d] for d in range(1, (depth + 1) // 2)] + [[depth // 2]]
    place = [grid.sibling_spot(k) for k in range(n_dp)]

    layers = {0: hidden}
    reached = [grid.reach(hidden)]
    for at, group in enumerate(groups[1:], 1):
        for dz in group:
            step = 1 if dz <= depth // 2 else -1
            layers[dz] = grid.along(layers[dz - step], step) if at > 1 else grid.along(hidden, dz)

    def reach_next(at, *late):
        if at < len(groups):
            sources = [layers[dz] for dz in groups[at]]
            sources[0] = after(sources[0], *late)
            reached.append(grid.reach(joined(sources) if len(sources) > 1 else sources[0]))

    reach_next(1, *reached[0].values())
    vocab_cols = head.shape[1]
    vocab_start = lax.axis_index(("dp", "tensor")) * vocab_cols
    starts = jnp.stack([c_me, vocab_start] + owners + [(z_me - dz) % depth for dz in range(depth)])
    packed = squares(after(hidden, starts), norm_gain[None, :], targets[None, :], n_dp * n_t)
    fine = lax.all_to_all(packed, ("dp", "tensor"), 0, 0, tiled=True)

    acc, deep, spreads, half = None, CORES * feat, {}, []
    for at, group in enumerate(groups):
        final = at == len(groups) - 1
        middle = at and not final
        offsets = [2 + n_dp + dz for dz in group]
        own = grid.sibling(after(reached[at][0, 0], *(half if final else [])))
        if at == 1:
            held = [acc, own, *(layers[dz] for dz in groups[2])]
        else:
            held = [] if at else [packed]
        spread = spreads.get(at) or grid.fill(dict(reached[at]), *held)
        early = [grid.sibling(after(a, acc)) for a in spread[1:-1]] if middle else []
        if at == 0:
            weights = [head]
        elif at == 1:
            for later in groups[1:]:
                ready = after(head, acc, *early, *(layers[dz] for dz in groups[2]))
                weights.append(loaded(starts, [2 + n_dp + dz for dz in later], ready, deep))
        following = half if final else []
        if middle:
            reach_next(at + 1, *reached[at].values())
            following = [*reached[at + 1].values(), *weights[1:3]]
            spreads[at + 1] = grid.fill(dict(reached[at + 1]))
        others = [own, *early]
        others += [grid.sibling(after(a, *following)) for a in spread[len(others) :]]
        blocks = spread + others
        for layer, offset in enumerate(offsets):
            done = layer == len(offsets) - 1
            if middle and done:
                half = [acc]
                blocks[0] = after(blocks[0], spreads[at + 1][-1])
            last = final and done
            acc = layer_product(tok, n_t, starts, layer, offset, fine, blocks, place, weights[at], acc, last)

    parts = lax.all_to_all(acc.reshape(n_dp * n_t, 3, tok), ("dp", "tensor"), 0, 0, tiled=True)
    top = jnp.max(parts[:, 0], axis=0)
    total = jnp.sum(parts[:, 1] * jnp.exp(parts[:, 0] - top[None, :]), axis=0)
    picked = jnp.sum(parts[:, 2], axis=0)

    seq_count = lengths.shape[0]
    position = jnp.arange(tok // seq_count, dtype=jnp.int32)
    live = (position[None, :] < lengths[:, None]).reshape(-1).astype(jnp.float32)
    logprob = picked - top - jnp.log(total)
    return (live * logprob, live * (logprob - old_logprob))


def solution(mesh):
    in_specs = (
        P("dp", "tensor"),
        P("tensor"),
        P(None, ("dp", "tensor")),
        P("dp"),
        P("dp"),
        P("dp"),
    )
    out_specs = (P("dp"), P("dp"))
    return jax.shard_map(body, mesh=mesh, in_specs=in_specs, out_specs=out_specs, check_vma=False)
```
